256 devices in a mesh: ha: 16 (over x, z_lo), wa: 16 (over z_hi, y, core).
Axes of the slice: x: 4, y: 4, z: 8 (z_hi: 2, z_lo: 4; z = z_hi * 4 + z_lo), core: 2. Of those that a mesh axis runs over, the one named last changes fastest.
Arguments:
- features: float32 [2, 256, 512, 128], P(None, 'ha', 'wa'), may hold values from -6 to 6
- weight_one: float32 [3, 3, 3, 128, 128], replicated, may hold values from -0.109375 to 0.109375
- flow_feats: float32 [2, 128, 256, 256], P(None, 'ha', 'wa'), may hold values from -6 to 6
- weight_two: float32 [3, 3, 3, 256, 128], replicated, may hold values from -0.078125 to 0.078125
- cotangent: float32 [2, 128, 256, 128], P(None, 'ha', 'wa'), may hold values from -6 to 6
Outputs:
- grad_features: float32 [2, 256, 512, 128], P(None, 'ha', 'wa')
- grad_weight_one: float32 [3, 3, 3, 128, 128], P(None, None, None, 'wa')
- grad_flow: float32 [2, 128, 256, 256], P(None, 'ha', 'wa')
- grad_weight_two: float32 [3, 3, 3, 256, 128], P(None, None, None, 'wa')
The draws below stay inside these ranges and needn't reach their ends.
All inputs are finite; a program needn't handle non-finite values.
Results may differ from the reference program's by a relative error of at most 0.0003.
Values sent between devices are 32-bit elements; how exact they have to be, the bound alone decides.
No kernel may reach another device: no remote copies, remote signals or barrier semaphores. Data moves between devices by JAX's collectives and lax.ppermute only.
A program may use at most 128 MiB of HBM per device.

```python
import jax
import jax.numpy as jnp
from jax import lax

C = 128
CF = 256
FR = 2
H = 256
W = 512
H2 = 128
W2 = 256


def spiked(array, key, source, target, blocks, factor):
    owner, partner = [(jnp.arange(array.shape[position]) // (array.shape[position] // blocks)).reshape([-1 if axis == position else 1 for axis in range(array.ndim)]) for position in (source, target)]
    chosen = jax.random.permutation(key, blocks)[partner]
    strong = (owner == chosen) | (owner == (partner + blocks // 2) % blocks)
    return jnp.where(strong, factor * array, array)


def block_scale(rng, extent, shards, smallest, high):
    level, own = 1.0, jax.random.fold_in(rng, 6)
    for position, blocks in shards:
        draws = jnp.exp(jax.random.uniform(jax.random.fold_in(own, position), (blocks,), jnp.float32, smallest / len(shards), high / len(shards)))
        level = level * jnp.repeat(draws, extent[position] // blocks).reshape([-1 if axis == position else 1 for axis in range(len(extent))])
    return level


def bell_draw(key, shape, width, limit, cuts=(), dtype=jnp.bfloat16):
    entries = width * jax.random.normal(key, shape, jnp.float32)
    if cuts:
        entries = entries * block_scale(key, shape, cuts, -0.22, 0.18)
    return jnp.clip(entries, -limit, limit).astype(dtype)


def bell_draw_with(own_key, extent, width, reach, split, heavy, kind=jnp.bfloat16):
    array = width * jax.random.normal(own_key, extent, jnp.float32)
    if split:
        array = array * block_scale(own_key, extent, split, -0.22, 0.18)
    return jnp.clip(spiked(array, jax.random.fold_in(own_key, 3), *heavy), -reach, reach).astype(kind)


def setup_inputs(seed: int = 0) -> dict:
    arg_keys = jax.random.split(jax.random.key(seed), 6)
    return {
        "features": bell_draw_with(arg_keys[0], (FR, H, W, C), 1.0, 6.0, ((1, 16), (2, 16)), (2, 3, 16, 2.0), jnp.float32),
        "weight_one": bell_draw(arg_keys[1], (3, 3, 3, C, C), (27 * C) ** -0.5, 0.109375, (), jnp.float32),
        "flow_feats": bell_draw_with(arg_keys[2], (FR, H2, W2, CF), 1.0, 6.0, ((1, 16), (2, 16)), (2, 3, 16, 2.0), jnp.float32),
        "weight_two": bell_draw(arg_keys[3], (3, 3, 3, CF, C), (27 * CF) ** -0.5, 0.078125, (), jnp.float32),
        "cotangent": bell_draw(arg_keys[4], (FR, H2, W2, C), 1.0, 6.0, ((1, 16), (2, 16)), jnp.float32),
    }


def convolve(inputs, kernel):
    result = lax.conv_general_dilated(inputs[None], kernel, (1, 1, 1), [(1, 1), (1, 1), (1, 1)], dimension_numbers=('NDHWC', 'DHWIO', 'NDHWC'), precision=lax.Precision.HIGHEST)
    return result[0]

def forward(features, weight_one, flow_feats, weight_two):
    activity = jax.nn.silu(convolve(features, weight_one))
    lowband = 0.5 * (activity[:, 0::2, 0::2] + activity[:, 0::2, 1::2] + activity[:, 1::2, 0::2] + activity[:, 1::2, 1::2])
    return lowband + convolve(flow_feats, weight_two)

def reference(features, weight_one, flow_feats, weight_two, cotangent):
    unused, pullback = jax.vjp(forward, features, weight_one, flow_feats, weight_two)
    grad_features, grad_one, grad_flow, grad_two = pullback(cotangent)
    grad_one = grad_one * (1.0 / (FR * H * W) ** 0.5)
    grad_two = grad_two * (1.0 / (FR * H2 * W2) ** 0.5)
    return (grad_features, grad_one, grad_flow, grad_two)
```

```python
import functools

import jax
import jax.numpy as jnp
from jax import lax
from jax.experimental import pallas as pl
from jax.experimental.pallas import tpu as pltpu
from jax.sharding import Mesh
from jax.sharding import PartitionSpec as P

FR, R, W, C = 2, 16, 32, 128
R2, W2, CF = 8, 16, 256
PITCH = 40
EXT = (R + 2) * PITCH
HA, WA = ("x", "zl"), ("zh", "y", "core")

f32, bf16 = jnp.float32, jnp.bfloat16
VMEM = pl.BlockSpec(memory_space=pltpu.VMEM)
SMEM = pl.BlockSpec(memory_space=pltpu.SMEM)


def split(values):
    high = values.astype(bf16)
    return high, (values - high.astype(f32)).astype(bf16)


def product(left, right, dims):
    dot = functools.partial(
        lax.dot_general, dimension_numbers=(dims, ((), ())), preferred_element_type=f32
    )
    return dot(left[0], right[0]) + (dot(left[0], right[1]) + dot(left[1], right[0]))


NN = ((1,), (0,))
NT = ((1,), (1,))


def both_frames(kernel, tap):
    first = jnp.concatenate([kernel[9 + tap], kernel[tap]], axis=1)
    second = jnp.concatenate([kernel[18 + tap], kernel[9 + tap]], axis=1)
    return jnp.concatenate([first, second], axis=0)


def store_terms(place_ref, out_ref, tap, value, depth):
    half = value.shape[0] // 2
    taps = (
        (0, value[:half, C:]),
        (1, value[:half, :C] + value[half:, C:]),
        (2, value[half:, :C]),
    )
    core, y, x, zh = place_ref[0], place_ref[1], place_ref[2], place_ref[3]
    for time_tap, part in taps:
        number = 9 * time_tap + tap
        chunk = lax.rem(number // 7 - x + 4, 4)
        for owner in range(16):
            slot_core = lax.rem(owner % 2 - core + 2, 2)
            slot_y = lax.rem((owner // 2) % 4 - y + 4, 4)
            slot_zh = lax.rem(owner // 8 - zh + 2, 2)
            out_ref[slot_core, slot_y, chunk, slot_zh, number % 7] = part[owner * depth : (owner + 1) * depth]


def shifted_cot(cot_ref, e):
    both = jnp.concatenate([cot_ref[0, :, e : e + W2, :], cot_ref[1, :, e : e + W2, :]], axis=-1)
    return split(both)


def flow_terms_kernel(place_ref, flow_ref, cot_ref, out_ref):
    flow = jnp.concatenate(
        [flow_ref[0].reshape(R2 * W2, CF).T, flow_ref[1].reshape(R2 * W2, CF).T], axis=0
    )
    flow = split(flow)
    for col_tap in range(3):
        cot = shifted_cot(cot_ref, 2 - col_tap)
        for row_tap in range(3):
            window = [v[2 - row_tap : 2 - row_tap + R2].reshape(R2 * W2, 2 * C) for v in cot]
            store_terms(place_ref, out_ref, 3 * row_tap + col_tap, product(flow, window, NN), 16)


def block_kernel(
    place_ref, feat_ref, top_ref, bottom_ref, left_ref, right_ref, weight_ref, cot_ref,
    out_ref, grad_high_ref, grad_low_ref,
    ext_ref, wide_ref, taps_high, taps_low, even_high, even_low, odd_high, odd_low, grad_ref,
):
    ext_ref[...] = jnp.zeros_like(ext_ref)
    for t in range(FR):
        lanes = slice(t * C, (t + 1) * C)
        ext_ref[2 : 2 + R, 3 : 3 + W, lanes] = feat_ref[t]
        ext_ref[0:2, 3 : 3 + W, lanes] = top_ref[t]
        ext_ref[2 + R : 4 + R, 3 : 3 + W, lanes] = bottom_ref[t]
        ext_ref[0 : R + 4, 1:3, lanes] = left_ref[t]
        ext_ref[0 : R + 4, 3 + W : 5 + W, lanes] = right_ref[t]
    for t in range(FR):
        lanes = slice(t * C, (t + 1) * C)
        for row in range(R2 + 2):
            line = cot_ref[t, row] * 0.5
            for target in (2 * row - 1, 2 * row):
                if 0 <= target < R + 2:
                    wide_ref[t, target, pl.ds(0, W2 + 2, stride=2), :] = line
                    wide_ref[t, target, pl.ds(1, W2 + 2, stride=2), :] = line
    for tap in range(9):
        high, low = split(both_frames(weight_ref, tap))
        taps_high[tap] = high
        taps_low[tap] = low
    rows = R + 4
    for e in range(3):
        shifted = ext_ref[:, e : e + PITCH, :].reshape(rows * PITCH, 2 * C)
        high, low = split(shifted)
        even_high[e] = high
        even_low[e] = low
        odd_high[e] = high[PITCH : PITCH + EXT]
        odd_low[e] = low[PITCH : PITCH + EXT]
    step = EXT // 3
    for part in range(3):
        start = part * step
        total = jnp.zeros((step, 2 * C), f32)
        for row_tap in range(3):
            for e in range(3):
                if row_tap == 1:
                    window = (odd_high[e, start : start + step], odd_low[e, start : start + step])
                else:
                    first = start + row_tap * PITCH
                    window = (even_high[e, first : first + step], even_low[e, first : first + step])
                tap = 3 * row_tap + e
                total = total + product(window, (taps_high[tap], taps_low[tap]), NN)
        sigma = jax.nn.sigmoid(total)
        slope = sigma * (1.0 + total * (1.0 - sigma))
        lines = step // PITCH
        grad_ref[part * lines : (part + 1) * lines] = slope.reshape(lines, PITCH, 2 * C)
    for t in range(FR):
        lanes = slice(t * C, (t + 1) * C)
        grad_ref[:, :, lanes] = grad_ref[:, :, lanes] * wide_ref[t]
    for e in range(3):
        high, low = split(grad_ref[:, 3 - e : 3 - e + W, :])
        grad_high_ref[e] = high
        grad_low_ref[e] = low
    feat = split(
        jnp.concatenate([feat_ref[t].reshape(R * W, C).T for t in range(FR)], axis=0)
    )
    for row_tap in range(3):
        for e in range(3):
            window = [
                ref[e, 2 - row_tap : 2 - row_tap + R].reshape(R * W, 2 * C)
                for ref in (grad_high_ref, grad_low_ref)
            ]
            store_terms(place_ref, out_ref, 3 * row_tap + e, product(feat, window, NN), 8)


def adjoint_kernel(grad_high_ref, grad_low_ref, weight_one_ref, cot_ref, weight_two_ref, feat_out, flow_out):
    total = jnp.zeros((R * W, 2 * C), f32)
    for row_tap in range(3):
        for e in range(3):
            window = [
                ref[e, 2 - row_tap : 2 - row_tap + R].reshape(R * W, 2 * C)
                for ref in (grad_high_ref, grad_low_ref)
            ]
            total = total + product(window, split(both_frames(weight_one_ref, 3 * row_tap + e)), NT)
    for t in range(FR):
        feat_out[t] = total[:, t * C : (t + 1) * C].reshape(R, W, C)
    total = jnp.zeros((R2 * W2, 2 * CF), f32)
    for e in range(3):
        cot = shifted_cot(cot_ref, 2 - e)
        for row_tap in range(3):
            window = [v[2 - row_tap : 2 - row_tap + R2].reshape(R2 * W2, 2 * C) for v in cot]
            total = total + product(window, split(both_frames(weight_two_ref, 3 * row_tap + e)), NT)
    for t in range(FR):
        flow_out[t] = total[:, t * CF : (t + 1) * CF].reshape(R2, W2, CF)


def params():
    return pltpu.CompilerParams(vmem_limit_bytes=48 * 2**20)


def flow_terms(place, flow, cot):
    return pl.pallas_call(
        flow_terms_kernel,
        out_shape=jax.ShapeDtypeStruct((2, 4, 4, 2, 7, 16, C), f32),
        in_specs=[SMEM, VMEM, VMEM],
        out_specs=VMEM,
        compiler_params=params(),
        cost_estimate=pl.CostEstimate(flops=2 * 10**9, bytes_accessed=5 * 10**6, transcendentals=0),
        name="flow_terms",
    )(place, flow, cot)


def block_terms(place, feat, top, bottom, left, right, weight, cot):
    wins = jax.ShapeDtypeStruct((3, R + 2, W, 2 * C), bf16)
    return pl.pallas_call(
        block_kernel,
        out_shape=(jax.ShapeDtypeStruct((2, 4, 4, 2, 7, 8, C), f32), wins, wins),
        in_specs=[SMEM] + [VMEM] * 7,
        out_specs=(VMEM,) * 3,
        scratch_shapes=[
            pltpu.VMEM((R + 4, PITCH + 8, 2 * C), f32),
            pltpu.VMEM((FR, R + 2, PITCH, C), f32),
            pltpu.VMEM((9, 2 * C, 2 * C), bf16),
            pltpu.VMEM((9, 2 * C, 2 * C), bf16),
            pltpu.VMEM((3, (R + 4) * PITCH, 2 * C), bf16),
            pltpu.VMEM((3, (R + 4) * PITCH, 2 * C), bf16),
            pltpu.VMEM((3, EXT, 2 * C), bf16),
            pltpu.VMEM((3, EXT, 2 * C), bf16),
            pltpu.VMEM((R + 2, PITCH, 2 * C), f32),
        ],
        compiler_params=params(),
        cost_estimate=pl.CostEstimate(flops=5 * 10**9, bytes_accessed=6 * 10**6, transcendentals=200000),
        name="block_terms",
    )(place, feat, top, bottom, left, right, weight, cot)


def adjoints(grad_high, grad_low, weight_one, cot, weight_two):
    return pl.pallas_call(
        adjoint_kernel,
        out_shape=(
            jax.ShapeDtypeStruct((FR, R, W, C), f32),
            jax.ShapeDtypeStruct((FR, R2, W2, CF), f32),
        ),
        in_specs=[VMEM] * 5,
        out_specs=(VMEM,) * 2,
        compiler_params=params(),
        cost_estimate=pl.CostEstimate(flops=4 * 10**9, bytes_accessed=10**7, transcendentals=0),
        name="adjoints",
    )(grad_high, grad_low, weight_one, cot, weight_two)


def ring(steps, count=4):
    return [(i, (i + steps) % count) for i in range(count)]


def line(count, step):
    return [(i, i + step) for i in range(count) if 0 <= i + step < count]


def scatter_sum(parts, axis):
    arrived = [lax.ppermute(parts[k], axis, ring(k)) for k in (2, 1, 3)]
    return (parts[0] + arrived[0]) + (arrived[1] + arrived[2])


def local(features, weight_one, flow_feats, weight_two, cotangent):
    place = jnp.stack([lax.axis_index(a) for a in ("core", "y", "x", "zh")]).astype(jnp.int32)
    kernel_one = weight_one.reshape(27, C, C)
    kernel_two = weight_two.reshape(27, CF, C)
    def rows_of(feat, cot):
        return jnp.concatenate([feat.reshape(FR, 2 * W, C), cot.reshape(FR, W2, C)], axis=1)

    top = lax.ppermute(rows_of(features[:, R - 2 :], cotangent[:, R2 - 1 :]), HA, line(16, 1))
    bottom = lax.ppermute(rows_of(features[:, :2], cotangent[:, :1]), HA, line(16, -1))
    top_feat, top_cot = top[:, : 2 * W].reshape(FR, 2, W, C), top[:, 2 * W :][:, None]
    bottom_feat, bottom_cot = bottom[:, : 2 * W].reshape(FR, 2, W, C), bottom[:, 2 * W :][:, None]
    tall = jnp.concatenate([top_cot, cotangent, bottom_cot], axis=1)

    def cols_of(place, cot_place):
        cols = [v[:, :, place : place + 2] for v in (top_feat, features, bottom_feat)]
        cols = jnp.concatenate(cols, axis=1).reshape(FR, (R + 4) * 2, C)
        return jnp.concatenate([cols, tall[:, :, cot_place]], axis=1)

    left = lax.ppermute(cols_of(W - 2, W2 - 1), WA, line(16, 1))
    right = lax.ppermute(cols_of(0, 0), WA, line(16, -1))
    edge = 2 * (R + 4)
    left_feat, right_feat = [v[:, :edge].reshape(FR, R + 4, 2, C) for v in (left, right)]
    cot = jnp.concatenate([left[:, edge:, None], tall, right[:, edge:, None]], axis=2)

    terms_two = flow_terms(place, flow_feats, cot)
    terms_one, grad_high, grad_low = block_terms(
        place, features, top_feat, bottom_feat, left_feat, right_feat, kernel_one, cot
    )
    swap = [(0, 1), (1, 0)]
    sums = []
    for terms in (terms_two, terms_one):
        terms = terms[0] + lax.ppermute(terms[1], "core", swap)
        sums.append(scatter_sum([terms[k] for k in range(4)], "y"))
    chunks = jnp.concatenate([sums[1], sums[0]], axis=-2)
    chunk = scatter_sum([chunks[k] for k in range(4)], "x")
    chunk = chunk[0] + lax.ppermute(chunk[1], "zh", swap)
    arrived = [lax.ppermute(chunk, "zl", ring(k)) for k in (2, 1, 3)]
    chunk = (chunk + arrived[0]) + (arrived[1] + arrived[2])
    pieces = jnp.stack([chunk] + [lax.ppermute(chunk, "x", ring(k)) for k in (1, 2, 3)])
    order = lax.rem(place[2] - jnp.arange(4) + 4, 4)
    taps = jnp.concatenate([lax.dynamic_index_in_dim(pieces, order[k], 0, False) for k in range(4)])[:27]
    scale_one = 1.0 / (FR * R * W * 256) ** 0.5
    scale_two = 1.0 / (FR * R2 * W2 * 256) ** 0.5
    grad_one = (taps[:, :8] * scale_one).reshape(3, 3, 3, 8, C)
    grad_two = (taps[:, 8:] * scale_two).reshape(3, 3, 3, 16, C)
    grad_features, grad_flow = adjoints(grad_high, grad_low, kernel_one, cot, kernel_two)
    return (grad_features, grad_one, grad_flow, grad_two)


def solution(mesh):
    fine = Mesh(mesh.devices.reshape(4, 4, 2, 4, 2), ("x", "zl", "zh", "y", "core"))
    grid = P(None, HA, WA, None)
    share = P(None, None, None, WA, None)
    return jax.shard_map(
        local,
        mesh=fine,
        in_specs=(grid, P(), grid, P(), grid),
        out_specs=(grid, share, grid, share),
        check_vma=False,
    )
```

```python
import functools

import jax
import jax.numpy as jnp
from jax import lax
from jax.experimental import pallas as pl
from jax.experimental.pallas import tpu as pltpu
from jax.sharding import Mesh
from jax.sharding import PartitionSpec as P

FR, R, W, C = 2, 16, 32, 128
R2, W2, CF = 8, 16, 256
PITCH = 40
EXT = (R + 2) * PITCH
HA, WA = ("x", "zl"), ("zh", "y", "core")

f32, bf16 = jnp.float32, jnp.bfloat16
VMEM = pl.BlockSpec(memory_space=pltpu.VMEM)
SMEM = pl.BlockSpec(memory_space=pltpu.SMEM)


def split(values):
    high = values.astype(bf16)
    return high, (values - high.astype(f32)).astype(bf16)


def product(left, right, dims):
    dot = functools.partial(
        lax.dot_general, dimension_numbers=(dims, ((), ())), preferred_element_type=f32
    )
    return dot(left[0], right[0]) + (dot(left[0], right[1]) + dot(left[1], right[0]))


NN = ((1,), (0,))
NT = ((1,), (1,))


def both_frames(kernel, tap):
    first = jnp.concatenate([kernel[9 + tap], kernel[tap]], axis=1)
    second = jnp.concatenate([kernel[18 + tap], kernel[9 + tap]], axis=1)
    return jnp.concatenate([first, second], axis=0)


def store_terms(place_ref, keep_ref, send_ref, tap, value, depth):
    half = value.shape[0] // 2
    taps = (
        (0, value[:half, C:]),
        (1, value[:half, :C] + value[half:, C:]),
        (2, value[half:, :C]),
    )
    core, y, x, zh = place_ref[0], place_ref[1], place_ref[2], place_ref[3]
    for time_tap, part in taps:
        number = 9 * time_tap + tap
        chunk = lax.rem(number // 7 - x + 4, 4)
        for owner in range(8):
            slot_y = lax.rem(owner % 4 - y + 4, 4)
            slot_zh = lax.rem(owner // 4 - zh + 2, 2)
            first = part[2 * owner * depth : (2 * owner + 1) * depth]
            second = part[(2 * owner + 1) * depth : (2 * owner + 2) * depth]
            slots = (slot_y, chunk) if depth == 8 else (chunk, slot_y)
            keep_ref[slots + (slot_zh, number % 7)] = jnp.where(core == 0, first, second)
            send_ref[slots + (slot_zh, number % 7)] = jnp.where(core == 0, second, first)


def shifted_cot(cot_ref, e):
    both = jnp.concatenate([cot_ref[0, :, e : e + W2, :], cot_ref[1, :, e : e + W2, :]], axis=-1)
    return split(both)


def flow_terms_kernel(place_ref, flow_ref, cot_ref, keep_ref, send_ref):
    flow = jnp.concatenate(
        [flow_ref[0].reshape(R2 * W2, CF).T, flow_ref[1].reshape(R2 * W2, CF).T], axis=0
    )
    flow = split(flow)
    for col_tap in range(3):
        cot = shifted_cot(cot_ref, 2 - col_tap)
        for row_tap in range(3):
            window = [v[2 - row_tap : 2 - row_tap + R2].reshape(R2 * W2, 2 * C) for v in cot]
            store_terms(
                place_ref, keep_ref, send_ref, 3 * row_tap + col_tap, product(flow, window, NN), 16
            )


def block_kernel(
    feat_ref, top_ref, bottom_ref, left_ref, right_ref, weight_ref, cot_ref,
    grad_high_ref, grad_low_ref,
    ext_ref, wide_ref, taps_high, taps_low, even_high, even_low, odd_high, odd_low, grad_ref,
):
    ext_ref[...] = jnp.zeros_like(ext_ref)
    for t in range(FR):
        lanes = slice(t * C, (t + 1) * C)
        ext_ref[2 : 2 + R, 3 : 3 + W, lanes] = feat_ref[t]
        ext_ref[0:2, 3 : 3 + W, lanes] = top_ref[t]
        ext_ref[2 + R : 4 + R, 3 : 3 + W, lanes] = bottom_ref[t]
        ext_ref[0 : R + 4, 1:3, lanes] = left_ref[t]
        ext_ref[0 : R + 4, 3 + W : 5 + W, lanes] = right_ref[t]
    for t in range(FR):
        lanes = slice(t * C, (t + 1) * C)
        for row in range(R2 + 2):
            line = cot_ref[t, row] * 0.5
            for target in (2 * row - 1, 2 * row):
                if 0 <= target < R + 2:
                    wide_ref[t, target, pl.ds(0, W2 + 2, stride=2), :] = line
                    wide_ref[t, target, pl.ds(1, W2 + 2, stride=2), :] = line
    for tap in range(9):
        high, low = split(both_frames(weight_ref, tap))
        taps_high[tap] = high
        taps_low[tap] = low
    rows = R + 4
    for e in range(3):
        shifted = ext_ref[:, e : e + PITCH, :].reshape(rows * PITCH, 2 * C)
        high, low = split(shifted)
        even_high[e] = high
        even_low[e] = low
        odd_high[e] = high[PITCH : PITCH + EXT]
        odd_low[e] = low[PITCH : PITCH + EXT]
    step = EXT // 3
    for part in range(3):
        start = part * step
        total = jnp.zeros((step, 2 * C), f32)
        for row_tap in range(3):
            for e in range(3):
                if row_tap == 1:
                    window = (odd_high[e, start : start + step], odd_low[e, start : start + step])
                else:
                    first = start + row_tap * PITCH
                    window = (even_high[e, first : first + step], even_low[e, first : first + step])
                tap = 3 * row_tap + e
                total = total + product(window, (taps_high[tap], taps_low[tap]), NN)
        sigma = jax.nn.sigmoid(total)
        slope = sigma * (1.0 + total * (1.0 - sigma))
        lines = step // PITCH
        grad_ref[part * lines : (part + 1) * lines] = slope.reshape(lines, PITCH, 2 * C)
    for t in range(FR):
        lanes = slice(t * C, (t + 1) * C)
        grad_ref[:, :, lanes] = grad_ref[:, :, lanes] * wide_ref[t]
    for e in range(3):
        high, low = split(grad_ref[:, 3 - e : 3 - e + W, :])
        grad_high_ref[e] = high
        grad_low_ref[e] = low


def block_terms_kernel(place_ref, feat_ref, grad_high_ref, grad_low_ref, keep_ref, send_ref):
    feat = split(
        jnp.concatenate([feat_ref[t].reshape(R * W, C).T for t in range(FR)], axis=0)
    )
    for row_tap in range(3):
        for e in range(3):
            window = [
                ref[e, 2 - row_tap : 2 - row_tap + R].reshape(R * W, 2 * C)
                for ref in (grad_high_ref, grad_low_ref)
            ]
            store_terms(
                place_ref, keep_ref, send_ref, 3 * row_tap + e, product(feat, window, NN), 8
            )


def adjoint_kernel(grad_high_ref, grad_low_ref, weight_one_ref, cot_ref, weight_two_ref, feat_out, flow_out):
    total = jnp.zeros((R * W, 2 * C), f32)
    for row_tap in range(3):
        for e in range(3):
            window = [
                ref[e, 2 - row_tap : 2 - row_tap + R].reshape(R * W, 2 * C)
                for ref in (grad_high_ref, grad_low_ref)
            ]
            total = total + product(window, split(both_frames(weight_one_ref, 3 * row_tap + e)), NT)
    for t in range(FR):
        feat_out[t] = total[:, t * C : (t + 1) * C].reshape(R, W, C)
    total = jnp.zeros((R2 * W2, 2 * CF), f32)
    for e in range(3):
        cot = shifted_cot(cot_ref, 2 - e)
        for row_tap in range(3):
            window = [v[2 - row_tap : 2 - row_tap + R2].reshape(R2 * W2, 2 * C) for v in cot]
            total = total + product(window, split(both_frames(weight_two_ref, 3 * row_tap + e)), NT)
    for t in range(FR):
        flow_out[t] = total[:, t * CF : (t + 1) * CF].reshape(R2, W2, CF)


def params():
    return pltpu.CompilerParams(vmem_limit_bytes=48 * 2**20)


def flow_terms(place, flow, cot):
    return pl.pallas_call(
        flow_terms_kernel,
        out_shape=(jax.ShapeDtypeStruct((4, 4, 2, 7, 16, C), f32),) * 2,
        in_specs=[SMEM, VMEM, VMEM],
        out_specs=(VMEM,) * 2,
        compiler_params=params(),
        cost_estimate=pl.CostEstimate(flops=2 * 10**9, bytes_accessed=5 * 10**6, transcendentals=0),
        name="flow_terms",
    )(place, flow, cot)


def block_gradient(feat, top, bottom, left, right, weight, cot):
    return pl.pallas_call(
        block_kernel,
        out_shape=(jax.ShapeDtypeStruct((3, R + 2, W, 2 * C), bf16),) * 2,
        in_specs=[VMEM] * 7,
        out_specs=(VMEM,) * 2,
        scratch_shapes=[
            pltpu.VMEM((R + 4, PITCH + 8, 2 * C), f32),
            pltpu.VMEM((FR, R + 2, PITCH, C), f32),
            pltpu.VMEM((9, 2 * C, 2 * C), bf16),
            pltpu.VMEM((9, 2 * C, 2 * C), bf16),
            pltpu.VMEM((3, (R + 4) * PITCH, 2 * C), bf16),
            pltpu.VMEM((3, (R + 4) * PITCH, 2 * C), bf16),
            pltpu.VMEM((3, EXT, 2 * C), bf16),
            pltpu.VMEM((3, EXT, 2 * C), bf16),
            pltpu.VMEM((R + 2, PITCH, 2 * C), f32),
        ],
        compiler_params=params(),
        cost_estimate=pl.CostEstimate(flops=5 * 10**9, bytes_accessed=6 * 10**6, transcendentals=200000),
        name="block_gradient",
    )(feat, top, bottom, left, right, weight, cot)


def block_terms(place, feat, grad_high, grad_low):
    return pl.pallas_call(
        block_terms_kernel,
        out_shape=(jax.ShapeDtypeStruct((4, 4, 2, 7, 8, C), f32),) * 2,
        in_specs=[SMEM] + [VMEM] * 3,
        out_specs=(VMEM,) * 2,
        compiler_params=params(),
        cost_estimate=pl.CostEstimate(flops=10**9, bytes_accessed=10**6, transcendentals=0),
        name="block_terms",
    )(place, feat, grad_high, grad_low)


def adjoints(grad_high, grad_low, weight_one, cot, weight_two):
    return pl.pallas_call(
        adjoint_kernel,
        out_shape=(
            jax.ShapeDtypeStruct((FR, R, W, C), f32),
            jax.ShapeDtypeStruct((FR, R2, W2, CF), f32),
        ),
        in_specs=[VMEM] * 5,
        out_specs=(VMEM,) * 2,
        compiler_params=params(),
        cost_estimate=pl.CostEstimate(flops=4 * 10**9, bytes_accessed=10**7, transcendentals=0),
        name="adjoints",
    )(grad_high, grad_low, weight_one, cot, weight_two)


def ring(steps, count=4):
    return [(i, (i + steps) % count) for i in range(count)]


def line(count, step):
    return [(i, i + step) for i in range(count) if 0 <= i + step < count]


def spread(parts, axis):
    return [lax.ppermute(parts[k], axis, ring(k)) for k in (2, 1, 3)]


def summed(own, arrived):
    return (own + arrived[0]) + (arrived[1] + arrived[2])


def local(features, weight_one, flow_feats, weight_two, cotangent):
    place = jnp.stack([lax.axis_index(a) for a in ("core", "y", "x", "zh")]).astype(jnp.int32)
    kernel_one = weight_one.reshape(27, C, C)
    kernel_two = weight_two.reshape(27, CF, C)
    def rows_of(feat, cot):
        return jnp.concatenate([feat.reshape(FR, 2 * W, C), cot.reshape(FR, W2, C)], axis=1)

    top = lax.ppermute(rows_of(features[:, R - 2 :], cotangent[:, R2 - 1 :]), HA, line(16, 1))
    bottom = lax.ppermute(rows_of(features[:, :2], cotangent[:, :1]), HA, line(16, -1))
    top_feat, top_cot = top[:, : 2 * W].reshape(FR, 2, W, C), top[:, 2 * W :][:, None]
    bottom_feat, bottom_cot = bottom[:, : 2 * W].reshape(FR, 2, W, C), bottom[:, 2 * W :][:, None]
    tall = jnp.concatenate([top_cot, cotangent, bottom_cot], axis=1)

    def cols_of(place, cot_place):
        cols = [v[:, :, place : place + 2] for v in (top_feat, features, bottom_feat)]
        cols = jnp.concatenate(cols, axis=1).reshape(FR, (R + 4) * 2, C)
        return jnp.concatenate([cols, tall[:, :, cot_place]], axis=1)

    left = lax.ppermute(cols_of(W - 2, W2 - 1), WA, line(16, 1))
    right = lax.ppermute(cols_of(0, 0), WA, line(16, -1))
    edge = 2 * (R + 4)
    left_feat, right_feat = [v[:, :edge].reshape(FR, R + 4, 2, C) for v in (left, right)]
    cot = jnp.concatenate([left[:, edge:, None], tall, right[:, edge:, None]], axis=2)

    swap = [(0, 1), (1, 0)]
    keep, send = flow_terms(place, flow_feats, cot)
    terms_two = keep + lax.ppermute(send, "core", swap)
    grad_high, grad_low = block_gradient(
        features, top_feat, bottom_feat, left_feat, right_feat, kernel_one, cot
    )
    terms_two, grad_high, grad_low = lax.optimization_barrier((terms_two, grad_high, grad_low))
    arrived_two = spread(terms_two, "x")
    keep, send = block_terms(place, features, grad_high, grad_low)
    terms_one = keep + lax.ppermute(send, "core", swap)
    arrived_one = spread(terms_one, "y")
    terms_one, grad_high, grad_low = lax.optimization_barrier((terms_one, grad_high, grad_low))
    grad_features, grad_flow = adjoints(grad_high, grad_low, kernel_one, cot, kernel_two)
    arrived_one, arrived_two, grad_features, grad_flow = lax.optimization_barrier(
        (arrived_one, arrived_two, grad_features, grad_flow)
    )
    terms_one = summed(terms_one[0], arrived_one)
    terms_two = summed(terms_two[0], arrived_two)
    arrived_one, arrived_two = spread(terms_one, "x"), spread(terms_two, "y")
    terms_one = summed(terms_one[0], arrived_one)
    terms_two = summed(terms_two[0], arrived_two)
    chunk = jnp.concatenate([terms_one, terms_two], axis=-2)
    chunk = chunk[0] + lax.ppermute(chunk[1], "zh", swap)
    chunk = summed(chunk, spread([chunk] * 4, "zl"))
    pieces = jnp.stack([chunk] + [lax.ppermute(chunk, "x", ring(k)) for k in (1, 2, 3)])
    order = lax.rem(place[2] - jnp.arange(4) + 4, 4)
    taps = jnp.concatenate([lax.dynamic_index_in_dim(pieces, order[k], 0, False) for k in range(4)])[:27]
    scale_one = 1.0 / (FR * R * W * 256) ** 0.5
    scale_two = 1.0 / (FR * R2 * W2 * 256) ** 0.5
    grad_one = (taps[:, :8] * scale_one).reshape(3, 3, 3, 8, C)
    grad_two = (taps[:, 8:] * scale_two).reshape(3, 3, 3, 16, C)
    return (grad_features, grad_one, grad_flow, grad_two)


def solution(mesh):
    fine = Mesh(mesh.devices.reshape(4, 4, 2, 4, 2), ("x", "zl", "zh", "y", "core"))
    grid = P(None, HA, WA, None)
    share = P(None, None, None, WA, None)
    return jax.shard_map(
        local,
        mesh=fine,
        in_specs=(grid, P(), grid, P(), grid),
        out_specs=(grid, share, grid, share),
        check_vma=False,
    )
```

```python
import functools

import jax
import jax.numpy as jnp
from jax import lax
from jax.experimental import pallas as pl
from jax.experimental.pallas import tpu as pltpu
from jax.sharding import Mesh
from jax.sharding import PartitionSpec as P

FR, R, W, C = 2, 16, 32, 128
R2, W2, CF = 8, 16, 256
PITCH = 40
EXT = (R + 2) * PITCH
COL = 24
HA, WA = ("x", "zl"), ("zh", "y", "core")

f32, bf16 = jnp.float32, jnp.bfloat16
VMEM = pl.BlockSpec(memory_space=pltpu.VMEM)
SMEM = pl.BlockSpec(memory_space=pltpu.SMEM)


def split(values):
    high = values.astype(bf16)
    return high, (values - high.astype(f32)).astype(bf16)


def product(left, right, dims):
    dot = functools.partial(
        lax.dot_general, dimension_numbers=(dims, ((), ())), preferred_element_type=f32
    )
    return dot(left[0], right[0]) + (dot(left[0], right[1]) + dot(left[1], right[0]))


NN = ((1,), (0,))
NT = ((1,), (1,))


def both_frames(kernel, tap):
    first = jnp.concatenate([kernel[9 + tap], kernel[tap]], axis=1)
    second = jnp.concatenate([kernel[18 + tap], kernel[9 + tap]], axis=1)
    return jnp.concatenate([first, second], axis=0)


def store_terms(place_ref, keep_ref, send_ref, tap, value, depth):
    half = value.shape[0] // 2
    taps = (
        (0, value[:half, C:]),
        (1, value[:half, :C] + value[half:, C:]),
        (2, value[half:, :C]),
    )
    core, y, x, zh = place_ref[0], place_ref[1], place_ref[2], place_ref[3]
    for time_tap, part in taps:
        number = 9 * time_tap + tap
        chunk = lax.rem(number // 7 - x + 4, 4)
        for owner in range(8):
            slot_y = lax.rem(owner % 4 - y + 4, 4)
            slot_zh = lax.rem(owner // 4 - zh + 2, 2)
            first = part[2 * owner * depth : (2 * owner + 1) * depth]
            second = part[(2 * owner + 1) * depth : (2 * owner + 2) * depth]
            slots = (slot_y, chunk) if depth == 8 else (chunk, slot_y)
            keep_ref[slots + (slot_zh, number % 7)] = jnp.where(core == 0, first, second)
            send_ref[slots + (slot_zh, number % 7)] = jnp.where(core == 0, second, first)


def row_edges_kernel(place_ref, feat_ref, cot_ref, first_ref, second_ref):
    odd = place_ref[4] == 1
    for t in range(FR):
        for row in range(2):
            top, bottom = feat_ref[t, row], feat_ref[t, R - 2 + row]
            lines = slice(row * W, (row + 1) * W)
            first_ref[t, lines] = jnp.where(odd, top, bottom)
            second_ref[t, lines] = jnp.where(odd, bottom, top)
        top, bottom = cot_ref[t, 0], cot_ref[t, R2 - 1]
        first_ref[t, 2 * W :] = jnp.where(odd, top, bottom)
        second_ref[t, 2 * W :] = jnp.where(odd, bottom, top)


def row_halo(place_ref, first_ref, second_ref, t, lines):
    odd = place_ref[4] == 1
    first, second = first_ref[t, lines], second_ref[t, lines]
    return jnp.where(odd, first, second), jnp.where(odd, second, first)


def col_edges_kernel(place_ref, feat_ref, cot_ref, row_first_ref, row_second_ref, first_ref, second_ref, edge_ref):
    for t in range(FR):
        halos = [row_halo(place_ref, row_first_ref, row_second_ref, t, slice(r * W, (r + 1) * W)) for r in range(2)]
        for side, start in ((0, 0), (1, W - 2)):
            for col in range(2):
                at, place = start + col, col * COL
                for row in range(2):
                    edge_ref[side, t, place + row : place + row + 1] = halos[row][0][at : at + 1]
                    low = place + R + 2 + row
                    edge_ref[side, t, low : low + 1] = halos[row][1][at : at + 1]
                edge_ref[side, t, place + 2 : place + 2 + R] = feat_ref[t, :, at, :]
        above, below = row_halo(place_ref, row_first_ref, row_second_ref, t, slice(2 * W, 2 * W + W2))
        for side, at in ((0, 0), (1, W2 - 1)):
            place = 2 * COL
            edge_ref[side, t, place : place + 1] = above[at : at + 1]
            edge_ref[side, t, place + 1 : place + 1 + R2] = cot_ref[t, :, at, :]
            edge_ref[side, t, place + 1 + R2 : place + 2 + R2] = below[at : at + 1]
    odd = place_ref[0] == 1
    first_ref[...] = jnp.where(odd, edge_ref[0], edge_ref[1])
    second_ref[...] = jnp.where(odd, edge_ref[1], edge_ref[0])


def col_halo(place_ref, first_ref, second_ref, t, lines):
    odd = place_ref[0] == 1
    first, second = first_ref[t, lines], second_ref[t, lines]
    return jnp.where(odd, first, second), jnp.where(odd, second, first)


def shifted_cot(cot_ref, e):
    both = jnp.concatenate([cot_ref[0, :, e : e + W2, :], cot_ref[1, :, e : e + W2, :]], axis=-1)
    return split(both)


def flow_terms_kernel(
    place_ref, flow_ref, local_ref, row_first_ref, row_second_ref, col_first_ref, col_second_ref,
    keep_ref, send_ref, cot_ref,
):
    for t in range(FR):
        above, below = row_halo(place_ref, row_first_ref, row_second_ref, t, slice(2 * W, 2 * W + W2))
        cot_ref[t, 0, 1 : 1 + W2] = above
        cot_ref[t, 1 : 1 + R2, 1 : 1 + W2] = local_ref[t]
        cot_ref[t, 1 + R2, 1 : 1 + W2] = below
        lines = slice(2 * COL, 2 * COL + R2 + 2)
        left, right = col_halo(place_ref, col_first_ref, col_second_ref, t, lines)
        cot_ref[t, :, 0] = left
        cot_ref[t, :, 1 + W2] = right
    flow = jnp.concatenate(
        [flow_ref[0].reshape(R2 * W2, CF).T, flow_ref[1].reshape(R2 * W2, CF).T], axis=0
    )
    flow = split(flow)
    for col_tap in range(3):
        cot = shifted_cot(cot_ref, 2 - col_tap)
        for row_tap in range(3):
            window = [v[2 - row_tap : 2 - row_tap + R2].reshape(R2 * W2, 2 * C) for v in cot]
            store_terms(
                place_ref, keep_ref, send_ref, 3 * row_tap + col_tap, product(flow, window, NN), 16
            )


def block_kernel(
    place_ref, feat_ref, row_first_ref, row_second_ref, col_first_ref, col_second_ref, weight_ref, cot_ref,
    grad_high_ref, grad_low_ref,
    ext_ref, wide_ref, taps_high, taps_low, even_high, even_low, odd_high, odd_low, grad_ref,
):
    ext_ref[...] = jnp.zeros_like(ext_ref)
    for t in range(FR):
        lanes = slice(t * C, (t + 1) * C)
        ext_ref[2 : 2 + R, 3 : 3 + W, lanes] = feat_ref[t]
        for row in range(2):
            above, below = row_halo(place_ref, row_first_ref, row_second_ref, t, slice(row * W, (row + 1) * W))
            ext_ref[row, 3 : 3 + W, lanes] = above
            ext_ref[R + 2 + row, 3 : 3 + W, lanes] = below
            place = slice(row * COL, row * COL + R + 4)
            left, right = col_halo(place_ref, col_first_ref, col_second_ref, t, place)
            ext_ref[:, 1 + row, lanes] = left
            ext_ref[:, 3 + W + row, lanes] = right
    for t in range(FR):
        lanes = slice(t * C, (t + 1) * C)
        for row in range(R2 + 2):
            line = cot_ref[t, row] * 0.5
            for target in (2 * row - 1, 2 * row):
                if 0 <= target < R + 2:
                    wide_ref[t, target, pl.ds(0, W2 + 2, stride=2), :] = line
                    wide_ref[t, target, pl.ds(1, W2 + 2, stride=2), :] = line
    for tap in range(9):
        high, low = split(both_frames(weight_ref, tap))
        taps_high[tap] = high
        taps_low[tap] = low
    rows = R + 4
    for e in range(3):
        shifted = ext_ref[:, e : e + PITCH, :].reshape(rows * PITCH, 2 * C)
        high, low = split(shifted)
        even_high[e] = high
        even_low[e] = low
        odd_high[e] = high[PITCH : PITCH + EXT]
        odd_low[e] = low[PITCH : PITCH + EXT]
    step = EXT // 3
    for part in range(3):
        start = part * step
        total = jnp.zeros((step, 2 * C), f32)
        for row_tap in range(3):
            for e in range(3):
                if row_tap == 1:
                    window = (odd_high[e, start : start + step], odd_low[e, start : start + step])
                else:
                    first = start + row_tap * PITCH
                    window = (even_high[e, first : first + step], even_low[e, first : first + step])
                tap = 3 * row_tap + e
                total = total + product(window, (taps_high[tap], taps_low[tap]), NN)
        sigma = jax.nn.sigmoid(total)
        slope = sigma * (1.0 + total * (1.0 - sigma))
        lines = step // PITCH
        grad_ref[part * lines : (part + 1) * lines] = slope.reshape(lines, PITCH, 2 * C)
    for t in range(FR):
        lanes = slice(t * C, (t + 1) * C)
        grad_ref[:, :, lanes] = grad_ref[:, :, lanes] * wide_ref[t]
    for e in range(3):
        high, low = split(grad_ref[:, 3 - e : 3 - e + W, :])
        grad_high_ref[e] = high
        grad_low_ref[e] = low


def block_terms_kernel(place_ref, feat_ref, grad_high_ref, grad_low_ref, keep_ref, send_ref):
    feat = split(
        jnp.concatenate([feat_ref[t].reshape(R * W, C).T for t in range(FR)], axis=0)
    )
    for row_tap in range(3):
        for e in range(3):
            window = [
                ref[e, 2 - row_tap : 2 - row_tap + R].reshape(R * W, 2 * C)
                for ref in (grad_high_ref, grad_low_ref)
            ]
            store_terms(
                place_ref, keep_ref, send_ref, 3 * row_tap + e, product(feat, window, NN), 8
            )


def adjoint_kernel(grad_high_ref, grad_low_ref, weight_one_ref, cot_ref, weight_two_ref, feat_out, flow_out):
    total = jnp.zeros((R * W, 2 * C), f32)
    for row_tap in range(3):
        for e in range(3):
            window = [
                ref[e, 2 - row_tap : 2 - row_tap + R].reshape(R * W, 2 * C)
                for ref in (grad_high_ref, grad_low_ref)
            ]
            total = total + product(window, split(both_frames(weight_one_ref, 3 * row_tap + e)), NT)
    for t in range(FR):
        feat_out[t] = total[:, t * C : (t + 1) * C].reshape(R, W, C)
    total = jnp.zeros((R2 * W2, 2 * CF), f32)
    for e in range(3):
        cot = shifted_cot(cot_ref, 2 - e)
        for row_tap in range(3):
            window = [v[2 - row_tap : 2 - row_tap + R2].reshape(R2 * W2, 2 * C) for v in cot]
            total = total + product(window, split(both_frames(weight_two_ref, 3 * row_tap + e)), NT)
    for t in range(FR):
        flow_out[t] = total[:, t * CF : (t + 1) * CF].reshape(R2, W2, CF)


def gather_kernel(place_ref, own_ref, one_ref, two_ref, three_ref, grad_one_ref, grad_two_ref):
    scale_one = 1.0 / (FR * R * W * 256) ** 0.5
    scale_two = 1.0 / (FR * R2 * W2 * 256) ** 0.5
    for k, ref in enumerate((own_ref, one_ref, two_ref, three_ref)):
        first = 7 * lax.rem(place_ref[2] - k + 4, 4)

        def put(j, ref=ref, first=first):
            grad_one_ref[first + j] = ref[j, :8] * scale_one
            grad_two_ref[first + j] = ref[j, 8:] * scale_two

        for j in range(6):
            put(j)
        pl.when(first < 21)(functools.partial(put, 6))


def params():
    return pltpu.CompilerParams(vmem_limit_bytes=48 * 2**20)


def small(kernel, name, out_shape, count, scratch=()):
    return pl.pallas_call(
        kernel,
        out_shape=out_shape,
        in_specs=[SMEM] + [VMEM] * count,
        out_specs=(VMEM,) * len(out_shape),
        scratch_shapes=scratch,
        compiler_params=params(),
        cost_estimate=pl.CostEstimate(flops=10**6, bytes_accessed=10**6, transcendentals=0),
        name=name,
    )


def flow_terms(*args):
    return pl.pallas_call(
        flow_terms_kernel,
        out_shape=(jax.ShapeDtypeStruct((4, 4, 2, 7, 16, C), f32),) * 2
        + (jax.ShapeDtypeStruct((FR, R2 + 2, W2 + 2, C), f32),),
        in_specs=[SMEM] + [VMEM] * 6,
        out_specs=(VMEM,) * 3,
        compiler_params=params(),
        cost_estimate=pl.CostEstimate(flops=2 * 10**9, bytes_accessed=5 * 10**6, transcendentals=0),
        name="flow_terms",
    )(*args)


def block_gradient(*args):
    return pl.pallas_call(
        block_kernel,
        out_shape=(jax.ShapeDtypeStruct((3, R + 2, W, 2 * C), bf16),) * 2,
        in_specs=[SMEM] + [VMEM] * 7,
        out_specs=(VMEM,) * 2,
        scratch_shapes=[
            pltpu.VMEM((R + 4, PITCH + 8, 2 * C), f32),
            pltpu.VMEM((FR, R + 2, PITCH, C), f32),
            pltpu.VMEM((9, 2 * C, 2 * C), bf16),
            pltpu.VMEM((9, 2 * C, 2 * C), bf16),
            pltpu.VMEM((3, (R + 4) * PITCH, 2 * C), bf16),
            pltpu.VMEM((3, (R + 4) * PITCH, 2 * C), bf16),
            pltpu.VMEM((3, EXT, 2 * C), bf16),
            pltpu.VMEM((3, EXT, 2 * C), bf16),
            pltpu.VMEM((R + 2, PITCH, 2 * C), f32),
        ],
        compiler_params=params(),
        cost_estimate=pl.CostEstimate(flops=5 * 10**9, bytes_accessed=6 * 10**6, transcendentals=200000),
        name="block_gradient",
    )(*args)


def block_terms(place, feat, grad_high, grad_low):
    return pl.pallas_call(
        block_terms_kernel,
        out_shape=(jax.ShapeDtypeStruct((4, 4, 2, 7, 8, C), f32),) * 2,
        in_specs=[SMEM] + [VMEM] * 3,
        out_specs=(VMEM,) * 2,
        compiler_params=params(),
        cost_estimate=pl.CostEstimate(flops=10**9, bytes_accessed=10**6, transcendentals=0),
        name="block_terms",
    )(place, feat, grad_high, grad_low)


def adjoints(grad_high, grad_low, weight_one, cot, weight_two):
    return pl.pallas_call(
        adjoint_kernel,
        out_shape=(
            jax.ShapeDtypeStruct((FR, R, W, C), f32),
            jax.ShapeDtypeStruct((FR, R2, W2, CF), f32),
        ),
        in_specs=[VMEM] * 5,
        out_specs=(VMEM,) * 2,
        compiler_params=params(),
        cost_estimate=pl.CostEstimate(flops=4 * 10**9, bytes_accessed=10**7, transcendentals=0),
        name="adjoints",
    )(grad_high, grad_low, weight_one, cot, weight_two)


def ring(steps, count=4):
    return [(i, (i + steps) % count) for i in range(count)]


def pairs(start, count=16):
    return [p for i in range(start, count - 1, 2) for p in ((i, i + 1), (i + 1, i))]


def spread(parts, axis):
    return [lax.ppermute(parts[k], axis, ring(k)) for k in (2, 1, 3)]


def summed(own, arrived):
    return (own + arrived[0]) + (arrived[1] + arrived[2])


def local(features, weight_one, flow_feats, weight_two, cotangent):
    place = [lax.axis_index(a) for a in ("core", "y", "x", "zh")] + [lax.axis_index("zl") % 2]
    place = jnp.stack(place).astype(jnp.int32)
    kernel_one = weight_one.reshape(27, C, C)
    kernel_two = weight_two.reshape(27, CF, C)
    edges = (jax.ShapeDtypeStruct((FR, 2 * W + W2, C), f32),) * 2
    edges = small(row_edges_kernel, "row_edges", edges, 2)(place, features, cotangent)
    rows = [lax.ppermute(edges[k], HA, pairs(k)) for k in range(2)]
    shape = (FR, 2 * COL + 16, C)
    edges = small(
        col_edges_kernel,
        "col_edges",
        (jax.ShapeDtypeStruct(shape, f32),) * 2,
        4,
        [pltpu.VMEM((2,) + shape, f32)],
    )(place, features, cotangent, *rows)
    cols = [lax.ppermute(edges[k], WA, pairs(k)) for k in range(2)]
    swap = [(0, 1), (1, 0)]
    keep, send, cot = flow_terms(place, flow_feats, cotangent, *rows, *cols)
    terms_two = keep + lax.ppermute(send, "core", swap)
    grad_high, grad_low = block_gradient(place, features, *rows, *cols, kernel_one, cot)
    terms_two, grad_high, grad_low = lax.optimization_barrier((terms_two, grad_high, grad_low))
    arrived_two = spread(terms_two, "x")
    keep, send = block_terms(place, features, grad_high, grad_low)
    terms_one = keep + lax.ppermute(send, "core", swap)
    arrived_one = spread(terms_one, "y")
    terms_one, grad_high, grad_low = lax.optimization_barrier((terms_one, grad_high, grad_low))
    grad_features, grad_flow = adjoints(grad_high, grad_low, kernel_one, cot, kernel_two)
    arrived_one, arrived_two, grad_features, grad_flow = lax.optimization_barrier(
        (arrived_one, arrived_two, grad_features, grad_flow)
    )
    terms_one = summed(terms_one[0], arrived_one)
    terms_two = summed(terms_two[0], arrived_two)
    arrived_one, arrived_two = spread(terms_one, "x"), spread(terms_two, "y")
    terms_one = summed(terms_one[0], arrived_one)
    terms_two = summed(terms_two[0], arrived_two)
    chunk = jnp.concatenate([terms_one, terms_two], axis=-2)
    chunk = chunk[0] + lax.ppermute(chunk[1], "zh", swap)
    chunk = summed(chunk, spread([chunk] * 4, "zl"))
    pieces = [chunk] + [lax.ppermute(chunk, "x", ring(k)) for k in (1, 2, 3)]
    shares = tuple(jax.ShapeDtypeStruct((27, depth, C), f32) for depth in (8, 16))
    grad_one, grad_two = small(gather_kernel, "gather", shares, 4)(place, *pieces)
    grad_one = grad_one.reshape(3, 3, 3, 8, C)
    grad_two = grad_two.reshape(3, 3, 3, 16, C)
    return (grad_features, grad_one, grad_flow, grad_two)


def solution(mesh):
    fine = Mesh(mesh.devices.reshape(4, 4, 2, 4, 2), ("x", "zl", "zh", "y", "core"))
    grid = P(None, HA, WA, None)
    share = P(None, None, None, WA, None)
    return jax.shard_map(
        local,
        mesh=fine,
        in_specs=(grid, P(), grid, P(), grid),
        out_specs=(grid, share, grid, share),
        check_vma=False,
    )
```

```python
import functools

import jax
import jax.numpy as jnp
from jax import lax
from jax.experimental import pallas as pl
from jax.experimental.pallas import tpu as pltpu
from jax.sharding import Mesh
from jax.sharding import PartitionSpec as P

FR, R, W, C = 2, 16, 32, 128
R2, W2, CF = 8, 16, 256
PITCH = 40
EXT = (R + 2) * PITCH
COL = 24
HA, WA = ("x", "zl"), ("zh", "y", "core")

f32, bf16 = jnp.float32, jnp.bfloat16
VMEM = pl.BlockSpec(memory_space=pltpu.VMEM)
SMEM = pl.BlockSpec(memory_space=pltpu.SMEM)
HBM = pl.BlockSpec(memory_space=pltpu.HBM)


def split(values):
    high = values.astype(bf16)
    return high, (values - high.astype(f32)).astype(bf16)


def product(left, right, dims):
    dot = functools.partial(
        lax.dot_general, dimension_numbers=(dims, ((), ())), preferred_element_type=f32
    )
    return dot(left[0], right[0]) + (dot(left[0], right[1]) + dot(left[1], right[0]))


NN = ((1,), (0,))
NT = ((1,), (1,))


def both_frames(kernel, tap):
    first = jnp.concatenate([kernel[9 + tap], kernel[tap]], axis=1)
    second = jnp.concatenate([kernel[18 + tap], kernel[9 + tap]], axis=1)
    return jnp.concatenate([first, second], axis=0)


def store_terms(place_ref, keep_ref, send_ref, tap, value, depth):
    half = value.shape[0] // 2
    taps = (
        (0, value[:half, C:]),
        (1, value[:half, :C] + value[half:, C:]),
        (2, value[half:, :C]),
    )
    core, y, x, zh = place_ref[0], place_ref[1], place_ref[2], place_ref[3]
    for time_tap, part in taps:
        number = 9 * time_tap + tap
        slot_x = lax.rem(number // 7 - x + 4, 4)
        for owner in range(8):
            slot_y = lax.rem(owner % 4 - y + 4, 4)
            slot_zh = lax.rem(owner // 4 - zh + 2, 2)
            slots = [jnp.where(core == 0, slot_x, slot_y), jnp.where(core == 0, slot_y, slot_x)]
            first = part[2 * owner * depth : (2 * owner + 1) * depth]
            second = part[(2 * owner + 1) * depth : (2 * owner + 2) * depth]
            keep_ref[slots[0], slots[1], slot_zh, number % 7] = jnp.where(core == 0, first, second)
            send_ref[slots[1], slots[0], slot_zh, number % 7] = jnp.where(core == 0, second, first)


def row_edges_kernel(
    place_ref, feat_ref, cot_ref, first_ref, second_ref, feat_top, feat_bottom, cot_top, cot_bottom, sems
):
    copies = [
        pltpu.make_async_copy(feat_ref.at[:, 0:2], feat_top, sems.at[0]),
        pltpu.make_async_copy(feat_ref.at[:, R - 2 : R], feat_bottom, sems.at[1]),
        pltpu.make_async_copy(cot_ref.at[:, 0:1], cot_top, sems.at[2]),
        pltpu.make_async_copy(cot_ref.at[:, R2 - 1 : R2], cot_bottom, sems.at[3]),
    ]
    for copy in copies:
        copy.start()
    for copy in copies:
        copy.wait()
    odd = place_ref[4] == 1
    for t in range(FR):
        for row in range(2):
            top, bottom = feat_top[t, row], feat_bottom[t, row]
            lines = slice(row * W, (row + 1) * W)
            first_ref[t, lines] = jnp.where(odd, top, bottom)
            second_ref[t, lines] = jnp.where(odd, bottom, top)
        top, bottom = cot_top[t, 0], cot_bottom[t, 0]
        first_ref[t, 2 * W :] = jnp.where(odd, top, bottom)
        second_ref[t, 2 * W :] = jnp.where(odd, bottom, top)


def prepare_kernel(place_ref, weight_ref, feat_ref, taps_high, taps_low, feat_high, feat_low):
    for tap in range(9):
        taps_high[tap], taps_low[tap] = split(both_frames(weight_ref, tap))
    for t in range(FR):
        lines = slice(t * C, (t + 1) * C)
        feat_high[lines], feat_low[lines] = split(feat_ref[t].reshape(R * W, C).T)


def prepare_flow_kernel(place_ref, flow_ref, flow_high, flow_low):
    for t in range(FR):
        lines = slice(t * CF, (t + 1) * CF)
        flow_high[lines], flow_low[lines] = split(flow_ref[t].reshape(R2 * W2, CF).T)


def row_halo(place_ref, first_ref, second_ref, t, lines):
    odd = place_ref[4] == 1
    first, second = first_ref[t, lines], second_ref[t, lines]
    return jnp.where(odd, first, second), jnp.where(odd, second, first)


def col_edges_kernel(place_ref, feat_ref, cot_ref, row_first_ref, row_second_ref, first_ref, second_ref, edge_ref):
    for t in range(FR):
        halos = [row_halo(place_ref, row_first_ref, row_second_ref, t, slice(r * W, (r + 1) * W)) for r in range(2)]
        for side, start in ((0, 0), (1, W - 2)):
            for col in range(2):
                at, place = start + col, col * COL
                for row in range(2):
                    edge_ref[side, t, place + row : place + row + 1] = halos[row][0][at : at + 1]
                    low = place + R + 2 + row
                    edge_ref[side, t, low : low + 1] = halos[row][1][at : at + 1]
                edge_ref[side, t, place + 2 : place + 2 + R] = feat_ref[t, :, at, :]
        above, below = row_halo(place_ref, row_first_ref, row_second_ref, t, slice(2 * W, 2 * W + W2))
        for side, at in ((0, 0), (1, W2 - 1)):
            place = 2 * COL
            edge_ref[side, t, place : place + 1] = above[at : at + 1]
            edge_ref[side, t, place + 1 : place + 1 + R2] = cot_ref[t, :, at, :]
            edge_ref[side, t, place + 1 + R2 : place + 2 + R2] = below[at : at + 1]
    odd = place_ref[0] == 1
    first_ref[...] = jnp.where(odd, edge_ref[0], edge_ref[1])
    second_ref[...] = jnp.where(odd, edge_ref[1], edge_ref[0])


def col_halo(place_ref, first_ref, second_ref, t, lines):
    odd = place_ref[0] == 1
    first, second = first_ref[t, lines], second_ref[t, lines]
    return jnp.where(odd, first, second), jnp.where(odd, second, first)


def shifted_cot(cot_ref, e):
    both = jnp.concatenate([cot_ref[0, :, e : e + W2, :], cot_ref[1, :, e : e + W2, :]], axis=-1)
    return split(both)


def flow_terms_kernel(
    place_ref, flow_high, flow_low, local_ref, row_first_ref, row_second_ref, col_first_ref, col_second_ref,
    keep_ref, send_ref, cot_ref,
):
    for t in range(FR):
        above, below = row_halo(place_ref, row_first_ref, row_second_ref, t, slice(2 * W, 2 * W + W2))
        cot_ref[t, 0, 1 : 1 + W2] = above
        cot_ref[t, 1 : 1 + R2, 1 : 1 + W2] = local_ref[t]
        cot_ref[t, 1 + R2, 1 : 1 + W2] = below
        lines = slice(2 * COL, 2 * COL + R2 + 2)
        left, right = col_halo(place_ref, col_first_ref, col_second_ref, t, lines)
        cot_ref[t, :, 0] = left
        cot_ref[t, :, 1 + W2] = right
    flow = flow_high[...], flow_low[...]
    for col_tap in range(3):
        cot = shifted_cot(cot_ref, 2 - col_tap)
        for row_tap in range(3):
            window = [v[2 - row_tap : 2 - row_tap + R2].reshape(R2 * W2, 2 * C) for v in cot]
            store_terms(
                place_ref, keep_ref, send_ref, 3 * row_tap + col_tap, product(flow, window, NN), 16
            )


def block_kernel(
    place_ref, feat_ref, row_first_ref, row_second_ref, col_first_ref, col_second_ref,
    taps_high, taps_low, cot_ref, grad_high_ref, grad_low_ref,
    ext_ref, wide_ref, even_high, even_low, odd_high, odd_low, grad_ref,
):
    ext_ref[...] = jnp.zeros_like(ext_ref)
    for t in range(FR):
        lanes = slice(t * C, (t + 1) * C)
        ext_ref[2 : 2 + R, 3 : 3 + W, lanes] = feat_ref[t]
        for row in range(2):
            above, below = row_halo(place_ref, row_first_ref, row_second_ref, t, slice(row * W, (row + 1) * W))
            ext_ref[row, 3 : 3 + W, lanes] = above
            ext_ref[R + 2 + row, 3 : 3 + W, lanes] = below
            place = slice(row * COL, row * COL + R + 4)
            left, right = col_halo(place_ref, col_first_ref, col_second_ref, t, place)
            ext_ref[:, 1 + row, lanes] = left
            ext_ref[:, 3 + W + row, lanes] = right
    for t in range(FR):
        lanes = slice(t * C, (t + 1) * C)
        for row in range(R2 + 2):
            line = cot_ref[t, row] * 0.5
            for target in (2 * row - 1, 2 * row):
                if 0 <= target < R + 2:
                    wide_ref[t, target, pl.ds(0, W2 + 2, stride=2), :] = line
                    wide_ref[t, target, pl.ds(1, W2 + 2, stride=2), :] = line
    rows = R + 4
    for e in range(3):
        shifted = ext_ref[:, e : e + PITCH, :].reshape(rows * PITCH, 2 * C)
        high, low = split(shifted)
        even_high[e] = high
        even_low[e] = low
        odd_high[e] = high[PITCH : PITCH + EXT]
        odd_low[e] = low[PITCH : PITCH + EXT]
    step = EXT // 3
    for part in range(3):
        start = part * step
        total = jnp.zeros((step, 2 * C), f32)
        for row_tap in range(3):
            for e in range(3):
                if row_tap == 1:
                    window = (odd_high[e, start : start + step], odd_low[e, start : start + step])
                else:
                    first = start + row_tap * PITCH
                    window = (even_high[e, first : first + step], even_low[e, first : first + step])
                tap = 3 * row_tap + e
                total = total + product(window, (taps_high[tap], taps_low[tap]), NN)
        sigma = jax.nn.sigmoid(total)
        slope = sigma * (1.0 + total * (1.0 - sigma))
        lines = step // PITCH
        grad_ref[part * lines : (part + 1) * lines] = slope.reshape(lines, PITCH, 2 * C)
    for t in range(FR):
        lanes = slice(t * C, (t + 1) * C)
        grad_ref[:, :, lanes] = grad_ref[:, :, lanes] * wide_ref[t]
    for e in range(3):
        high, low = split(grad_ref[:, 3 - e : 3 - e + W, :])
        grad_high_ref[e] = high
        grad_low_ref[e] = low


def block_terms_kernel(place_ref, feat_high, feat_low, grad_high_ref, grad_low_ref, keep_ref, send_ref):
    feat = feat_high[...], feat_low[...]
    for row_tap in range(3):
        for e in range(3):
            window = [
                ref[e, 2 - row_tap : 2 - row_tap + R].reshape(R * W, 2 * C)
                for ref in (grad_high_ref, grad_low_ref)
            ]
            store_terms(
                place_ref, keep_ref, send_ref, 3 * row_tap + e, product(feat, window, NN), 8
            )


def adjoint_kernel(grad_high_ref, grad_low_ref, taps_high, taps_low, cot_ref, weight_two_ref, feat_out, flow_out):
    total = jnp.zeros((R * W, 2 * C), f32)
    for row_tap in range(3):
        for e in range(3):
            window = [
                ref[e, 2 - row_tap : 2 - row_tap + R].reshape(R * W, 2 * C)
                for ref in (grad_high_ref, grad_low_ref)
            ]
            tap = 3 * row_tap + e
            total = total + product(window, (taps_high[tap], taps_low[tap]), NT)
    for t in range(FR):
        feat_out[t] = total[:, t * C : (t + 1) * C].reshape(R, W, C)
    total = jnp.zeros((R2 * W2, 2 * CF), f32)
    for e in range(3):
        cot = shifted_cot(cot_ref, 2 - e)
        for row_tap in range(3):
            window = [v[2 - row_tap : 2 - row_tap + R2].reshape(R2 * W2, 2 * C) for v in cot]
            total = total + product(window, split(both_frames(weight_two_ref, 3 * row_tap + e)), NT)
    for t in range(FR):
        flow_out[t] = total[:, t * CF : (t + 1) * CF].reshape(R2, W2, CF)


def gather_kernel(place_ref, own_ref, one_ref, two_ref, three_ref, grad_one_ref, grad_two_ref):
    scale_one = 1.0 / (FR * R * W * 256) ** 0.5
    scale_two = 1.0 / (FR * R2 * W2 * 256) ** 0.5
    for k, ref in enumerate((own_ref, one_ref, two_ref, three_ref)):
        first = 7 * lax.rem(place_ref[2] - k + 4, 4)

        def put(j, ref=ref, first=first):
            grad_one_ref[first + j] = ref[j, :8] * scale_one
            grad_two_ref[first + j] = ref[j, 8:] * scale_two

        for j in range(6):
            put(j)
        pl.when(first < 21)(functools.partial(put, 6))


def params(mebibytes=48):
    return pltpu.CompilerParams(vmem_limit_bytes=mebibytes * 2**20)


def small(kernel, name, out_shape, count, scratch=(), space=VMEM):
    return pl.pallas_call(
        kernel,
        out_shape=out_shape,
        in_specs=[SMEM] + [space] * count,
        out_specs=(VMEM,) * len(out_shape),
        scratch_shapes=scratch,
        compiler_params=params(48 if space is VMEM else 64),
        cost_estimate=pl.CostEstimate(flops=10**6, bytes_accessed=10**6, transcendentals=0),
        name=name,
    )


def flow_terms(*args):
    return pl.pallas_call(
        flow_terms_kernel,
        out_shape=(jax.ShapeDtypeStruct((4, 4, 2, 7, 16, C), f32),) * 2
        + (jax.ShapeDtypeStruct((FR, R2 + 2, W2 + 2, C), f32),),
        in_specs=[SMEM] + [VMEM] * 7,
        out_specs=(VMEM,) * 3,
        compiler_params=params(),
        cost_estimate=pl.CostEstimate(flops=2 * 10**9, bytes_accessed=5 * 10**6, transcendentals=0),
        name="flow_terms",
    )(*args)


def block_gradient(*args):
    return pl.pallas_call(
        block_kernel,
        out_shape=(jax.ShapeDtypeStruct((3, R + 2, W, 2 * C), bf16),) * 2,
        in_specs=[SMEM] + [VMEM] * 8,
        out_specs=(VMEM,) * 2,
        scratch_shapes=[
            pltpu.VMEM((R + 4, PITCH + 8, 2 * C), f32),
            pltpu.VMEM((FR, R + 2, PITCH, C), f32),
            pltpu.VMEM((3, (R + 4) * PITCH, 2 * C), bf16),
            pltpu.VMEM((3, (R + 4) * PITCH, 2 * C), bf16),
            pltpu.VMEM((3, EXT, 2 * C), bf16),
            pltpu.VMEM((3, EXT, 2 * C), bf16),
            pltpu.VMEM((R + 2, PITCH, 2 * C), f32),
        ],
        compiler_params=params(),
        cost_estimate=pl.CostEstimate(flops=5 * 10**9, bytes_accessed=6 * 10**6, transcendentals=200000),
        name="block_gradient",
    )(*args)


def block_terms(*args):
    return pl.pallas_call(
        block_terms_kernel,
        out_shape=(jax.ShapeDtypeStruct((4, 4, 2, 7, 8, C), f32),) * 2,
        in_specs=[SMEM] + [VMEM] * 4,
        out_specs=(VMEM,) * 2,
        compiler_params=params(),
        cost_estimate=pl.CostEstimate(flops=10**9, bytes_accessed=10**6, transcendentals=0),
        name="block_terms",
    )(*args)


def adjoints(*args):
    return pl.pallas_call(
        adjoint_kernel,
        out_shape=(
            jax.ShapeDtypeStruct((FR, R, W, C), f32),
            jax.ShapeDtypeStruct((FR, R2, W2, CF), f32),
        ),
        in_specs=[VMEM] * 6,
        out_specs=(VMEM,) * 2,
        compiler_params=params(),
        cost_estimate=pl.CostEstimate(flops=4 * 10**9, bytes_accessed=10**7, transcendentals=0),
        name="adjoints",
    )(*args)


def ring(steps, count=4):
    return [(i, (i + steps) % count) for i in range(count)]


def crossed(steps, axes):
    both = []
    for x in range(4):
        for y in range(4):
            for core in range(2):
                along_x = axes[core] == "x"
                x_to, y_to = ((x + steps) % 4, y) if along_x else (x, (y + steps) % 4)
                both.append((8 * x + 2 * y + core, 8 * x_to + 2 * y_to + core))
    return both


def pairs(start, count=16):
    return [p for i in range(start, count - 1, 2) for p in ((i, i + 1), (i + 1, i))]


def spread(parts, axes):
    if axes == "zl":
        return [lax.ppermute(parts[k], "zl", ring(k)) for k in (2, 1, 3)]
    return [lax.ppermute(parts[k], ("x", "y", "core"), crossed(k, axes)) for k in (2, 1, 3)]


def summed(own, arrived):
    return (own + arrived[0]) + (arrived[1] + arrived[2])


def local(features, weight_one, flow_feats, weight_two, cotangent):
    place = [lax.axis_index(a) for a in ("core", "y", "x", "zh")] + [lax.axis_index("zl") % 2]
    place = jnp.stack(place).astype(jnp.int32)
    kernel_one = weight_one.reshape(27, C, C)
    kernel_two = weight_two.reshape(27, CF, C)
    edges = (jax.ShapeDtypeStruct((FR, 2 * W + W2, C), f32),) * 2
    edges = small(
        row_edges_kernel,
        "row_edges",
        edges,
        2,
        [pltpu.VMEM((FR, 2, W, C), f32)] * 2
        + [pltpu.VMEM((FR, 1, W2, C), f32)] * 2
        + [pltpu.SemaphoreType.DMA((4,))],
        HBM,
    )(place, features, cotangent)
    edges, kernel_one = lax.optimization_barrier((edges, kernel_one))
    rows = [lax.ppermute(edges[k], HA, pairs(k)) for k in range(2)]
    taps = jax.ShapeDtypeStruct((9, 2 * C, 2 * C), bf16)
    feats = jax.ShapeDtypeStruct((2 * C, R * W), bf16)
    prepared = small(prepare_kernel, "prepare", (taps, taps, feats, feats), 2)(place, kernel_one, features)
    rows, prepared = lax.optimization_barrier((rows, prepared))
    shape = (FR, 2 * COL + 16, C)
    edges = small(
        col_edges_kernel,
        "col_edges",
        (jax.ShapeDtypeStruct(shape, f32),) * 2,
        4,
        [pltpu.VMEM((2,) + shape, f32)],
    )(place, features, cotangent, *rows)
    edges, flow_feats = lax.optimization_barrier((edges, flow_feats))
    cols = [lax.ppermute(edges[k], WA, pairs(k)) for k in range(2)]
    flows = (jax.ShapeDtypeStruct((2 * CF, R2 * W2), bf16),) * 2
    flows = small(prepare_flow_kernel, "prepare_flow", flows, 1)(place, flow_feats)
    cols, flows = lax.optimization_barrier((cols, flows))
    swap = [(0, 1), (1, 0)]
    taps, feats = prepared[:2], prepared[2:]
    keep, send, cot = flow_terms(place, *flows, cotangent, *rows, *cols)
    terms_two = keep + lax.ppermute(send, "core", swap)
    grad_high, grad_low = block_gradient(place, features, *rows, *cols, *taps, cot)
    terms_two, grad_high, grad_low = lax.optimization_barrier((terms_two, grad_high, grad_low))
    arrived_two = spread(terms_two, ("x", "y"))
    keep, send = block_terms(place, *feats, grad_high, grad_low)
    terms_one = keep + lax.ppermute(send, "core", swap)
    arrived_one = spread(terms_one, ("x", "y"))
    terms_one, grad_high, grad_low = lax.optimization_barrier((terms_one, grad_high, grad_low))
    grad_features, grad_flow = adjoints(grad_high, grad_low, *taps, cot, kernel_two)
    arrived_one, arrived_two, grad_features, grad_flow = lax.optimization_barrier(
        (arrived_one, arrived_two, grad_features, grad_flow)
    )
    terms_one = summed(terms_one[0], arrived_one)
    terms_two = summed(terms_two[0], arrived_two)
    terms = jnp.concatenate([terms_one, terms_two], axis=-2)
    chunk = summed(terms[0], spread(terms, ("y", "x")))
    chunk = chunk[0] + lax.ppermute(chunk[1], "zh", swap)
    chunk = summed(chunk, spread([chunk] * 4, "zl"))
    pieces = [chunk] + [lax.ppermute(chunk, "x", ring(k)) for k in (1, 2, 3)]
    shares = tuple(jax.ShapeDtypeStruct((27, depth, C), f32) for depth in (8, 16))
    grad_one, grad_two = small(gather_kernel, "gather", shares, 4)(place, *pieces)
    grad_one = grad_one.reshape(3, 3, 3, 8, C)
    grad_two = grad_two.reshape(3, 3, 3, 16, C)
    return (grad_features, grad_one, grad_flow, grad_two)


def solution(mesh):
    fine = Mesh(mesh.devices.reshape(4, 4, 2, 4, 2), ("x", "zl", "zh", "y", "core"))
    grid = P(None, HA, WA, None)
    share = P(None, None, None, WA, None)
    return jax.shard_map(
        local,
        mesh=fine,
        in_specs=(grid, P(), grid, P(), grid),
        out_specs=(grid, share, grid, share),
        check_vma=False,
    )
```

```python
import functools

import jax
import jax.numpy as jnp
from jax import lax
from jax.experimental import pallas as pl
from jax.experimental.pallas import tpu as pltpu
from jax.sharding import Mesh
from jax.sharding import PartitionSpec as P

FR, R, W, C = 2, 16, 32, 128
R2, W2, CF = 8, 16, 256
PITCH = 40
EXT = (R + 2) * PITCH
COL = 20
HA, WA = ("x", "zl"), ("zh", "y", "core")

f32, bf16 = jnp.float32, jnp.bfloat16
VMEM = pl.BlockSpec(memory_space=pltpu.VMEM)
HBM = pl.BlockSpec(memory_space=pltpu.HBM)


def split(values):
    high = values.astype(bf16)
    return high, (values - high.astype(f32)).astype(bf16)


def dot(left, right, dims):
    return lax.dot_general(left, right, (dims, ((), ())), preferred_element_type=f32)


def product(left, right, dims):
    return dot(left[0], right[0], dims) + (dot(left[0], right[1], dims) + dot(left[1], right[0], dims))


def tall_product(left, right, dims):
    rows = left[0].shape[0]
    both = dot(jnp.concatenate(left, axis=0), right[0], dims)
    return both[:rows] + (both[rows:] + dot(left[0], right[1], dims))


NN = ((1,), (0,))
NT = ((1,), (1,))


def both_frames(kernel, tap):
    first = jnp.concatenate([kernel[9 + tap], kernel[tap]], axis=1)
    second = jnp.concatenate([kernel[18 + tap], kernel[9 + tap]], axis=1)
    return jnp.concatenate([first, second], axis=0)


def store_terms(keep_ref, send_ref, tap, value, depth):
    half = value.shape[0] // 2
    taps = (
        (0, value[:half, C:]),
        (1, value[:half, :C] + value[half:, C:]),
        (2, value[half:, :C]),
    )
    core, y, x, zh = [lax.axis_index(a) for a in ("core", "y", "x", "zh")]
    for time_tap, part in taps:
        number = 9 * time_tap + tap
        slot_x = lax.rem(number // 7 - x + 4, 4)
        for owner in range(8):
            slot_y = lax.rem(owner % 4 - y + 4, 4)
            slot_zh = lax.rem(owner // 4 - zh + 2, 2)
            slots = [jnp.where(core == 0, slot_x, slot_y), jnp.where(core == 0, slot_y, slot_x)]
            first = part[2 * owner * depth : (2 * owner + 1) * depth]
            second = part[(2 * owner + 1) * depth : (2 * owner + 2) * depth]
            keep_ref[slots[0], slots[1], slot_zh, number % 7] = jnp.where(core == 0, first, second)
            send_ref[slots[1], slots[0], slot_zh, number % 7] = jnp.where(core == 0, second, first)


def row_edges_kernel(
    feat_ref, cot_ref, first_ref, second_ref, feat_top, feat_bottom, cot_top, cot_bottom, sems
):
    copies = [
        pltpu.make_async_copy(feat_ref.at[:, 0:2], feat_top, sems.at[0]),
        pltpu.make_async_copy(feat_ref.at[:, R - 2 : R], feat_bottom, sems.at[1]),
        pltpu.make_async_copy(cot_ref.at[:, 0:1], cot_top, sems.at[2]),
        pltpu.make_async_copy(cot_ref.at[:, R2 - 1 : R2], cot_bottom, sems.at[3]),
    ]
    for copy in copies:
        copy.start()
    for copy in copies:
        copy.wait()
    odd = lax.rem(lax.axis_index("zl"), 2) == 1
    for t in range(FR):
        for row in range(2):
            top, bottom = feat_top[t, row], feat_bottom[t, row]
            lines = slice(row * W, (row + 1) * W)
            first_ref[t, lines] = jnp.where(odd, top, bottom)
            second_ref[t, lines] = jnp.where(odd, bottom, top)
        top, bottom = cot_top[t, 0], cot_bottom[t, 0]
        first_ref[t, 2 * W :] = jnp.where(odd, top, bottom)
        second_ref[t, 2 * W :] = jnp.where(odd, bottom, top)


def prepare_features_kernel(feat_ref, cot_ref, feat_high, feat_low, near_cot_ref):
    near_cot_ref[...] = cot_ref[...]
    for t in range(FR):
        lines = slice(t * C, (t + 1) * C)
        feat_high[lines], feat_low[lines] = split(feat_ref[t].reshape(R * W, C).T)


def prepare_kernel(weight_ref, flow_ref, taps_high, taps_low, flow_high, flow_low):
    for tap in range(9):
        taps_high[tap], taps_low[tap] = split(both_frames(weight_ref, tap))
    for t in range(FR):
        lines = slice(t * CF, (t + 1) * CF)
        flow_high[lines], flow_low[lines] = split(flow_ref[t].reshape(R2 * W2, CF).T)


def row_halo(first_ref, second_ref, t, lines):
    odd = lax.rem(lax.axis_index("zl"), 2) == 1
    first, second = first_ref[t, lines], second_ref[t, lines]
    return jnp.where(odd, first, second), jnp.where(odd, second, first)


def col_edges_kernel(feat_ref, cot_ref, row_first_ref, row_second_ref, first_ref, second_ref, edge_ref):
    for t in range(FR):
        halos = [row_halo(row_first_ref, row_second_ref, t, slice(r * W, (r + 1) * W)) for r in range(2)]
        for side, start in ((0, 0), (1, W - 2)):
            for col in range(2):
                at, place = start + col, col * COL
                for row in range(2):
                    edge_ref[side, t, place + row : place + row + 1] = halos[row][0][at : at + 1]
                    low = place + R + 2 + row
                    edge_ref[side, t, low : low + 1] = halos[row][1][at : at + 1]
                edge_ref[side, t, place + 2 : place + 2 + R] = feat_ref[t, :, at, :]
        above, below = row_halo(row_first_ref, row_second_ref, t, slice(2 * W, 2 * W + W2))
        for side, at in ((0, 0), (1, W2 - 1)):
            place = 2 * COL
            edge_ref[side, t, place : place + 1] = above[at : at + 1]
            edge_ref[side, t, place + 1 : place + 1 + R2] = cot_ref[t, :, at, :]
            edge_ref[side, t, place + 1 + R2 : place + 2 + R2] = below[at : at + 1]
    odd = lax.axis_index("core") == 1
    first_ref[...] = jnp.where(odd, edge_ref[0], edge_ref[1])
    second_ref[...] = jnp.where(odd, edge_ref[1], edge_ref[0])


def col_halo(first_ref, second_ref, t, lines):
    odd = lax.axis_index("core") == 1
    first, second = first_ref[t, lines], second_ref[t, lines]
    return jnp.where(odd, first, second), jnp.where(odd, second, first)


def shifted_cot(cot_ref, e):
    both = jnp.concatenate([cot_ref[0, :, e : e + W2, :], cot_ref[1, :, e : e + W2, :]], axis=-1)
    return split(both)


def flow_terms_kernel(
    flow_high, flow_low, local_ref, row_first_ref, row_second_ref, col_first_ref, col_second_ref,
    keep_ref, send_ref, cot_ref,
):
    for t in range(FR):
        above, below = row_halo(row_first_ref, row_second_ref, t, slice(2 * W, 2 * W + W2))
        cot_ref[t, 0, 1 : 1 + W2] = above
        cot_ref[t, 1 : 1 + R2, 1 : 1 + W2] = local_ref[t]
        cot_ref[t, 1 + R2, 1 : 1 + W2] = below
        lines = slice(2 * COL, 2 * COL + R2 + 2)
        left, right = col_halo(col_first_ref, col_second_ref, t, lines)
        cot_ref[t, :, 0] = left
        cot_ref[t, :, 1 + W2] = right
    flow = jnp.concatenate([flow_high[...], flow_high[...], flow_low[...]], axis=1)
    for col_tap in range(3):
        cot = shifted_cot(cot_ref, 2 - col_tap)
        for row_tap in range(3):
            window = [v[2 - row_tap : 2 - row_tap + R2].reshape(R2 * W2, 2 * C) for v in cot]
            window = jnp.concatenate([window[0], window[1], window[0]], axis=0)
            store_terms(keep_ref, send_ref, 3 * row_tap + col_tap, dot(flow, window, NN), 16)


def block_kernel(
    feat_ref, row_first_ref, row_second_ref, col_first_ref, col_second_ref,
    taps_high, taps_low, cot_ref, grad_high_ref, grad_low_ref,
    ext_ref, wide_ref, even_high, even_low, odd_high, odd_low, grad_ref,
):
    ext_ref[...] = jnp.zeros_like(ext_ref)
    for t in range(FR):
        lanes = slice(t * C, (t + 1) * C)
        ext_ref[2 : 2 + R, 3 : 3 + W, lanes] = feat_ref[t]
        for row in range(2):
            above, below = row_halo(row_first_ref, row_second_ref, t, slice(row * W, (row + 1) * W))
            ext_ref[row, 3 : 3 + W, lanes] = above
            ext_ref[R + 2 + row, 3 : 3 + W, lanes] = below
            place = slice(row * COL, row * COL + R + 4)
            left, right = col_halo(col_first_ref, col_second_ref, t, place)
            ext_ref[:, 1 + row, lanes] = left
            ext_ref[:, 3 + W + row, lanes] = right
    for t in range(FR):
        lanes = slice(t * C, (t + 1) * C)
        for row in range(R2 + 2):
            line = cot_ref[t, row] * 0.5
            for target in (2 * row - 1, 2 * row):
                if 0 <= target < R + 2:
                    wide_ref[t, target, pl.ds(0, W2 + 2, stride=2), :] = line
                    wide_ref[t, target, pl.ds(1, W2 + 2, stride=2), :] = line
    rows = R + 4
    for e in range(3):
        shifted = ext_ref[:, e : e + PITCH, :].reshape(rows * PITCH, 2 * C)
        high, low = split(shifted)
        even_high[e] = high
        even_low[e] = low
        odd_high[e] = high[PITCH : PITCH + EXT]
        odd_low[e] = low[PITCH : PITCH + EXT]
    step = EXT // 3
    for part in range(3):
        start = part * step
        total = jnp.zeros((step, 2 * C), f32)
        for row_tap in range(3):
            for e in range(3):
                if row_tap == 1:
                    window = (odd_high[e, start : start + step], odd_low[e, start : start + step])
                else:
                    first = start + row_tap * PITCH
                    window = (even_high[e, first : first + step], even_low[e, first : first + step])
                tap = 3 * row_tap + e
                total = total + product(window, (taps_high[tap], taps_low[tap]), NN)
        sigma = jax.nn.sigmoid(total)
        slope = sigma * (1.0 + total * (1.0 - sigma))
        lines = step // PITCH
        grad_ref[part * lines : (part + 1) * lines] = slope.reshape(lines, PITCH, 2 * C)
    for t in range(FR):
        lanes = slice(t * C, (t + 1) * C)
        grad_ref[:, :, lanes] = grad_ref[:, :, lanes] * wide_ref[t]
    for e in range(3):
        high, low = split(grad_ref[:, 3 - e : 3 - e + W, :])
        grad_high_ref[e] = high
        grad_low_ref[e] = low


def block_terms_kernel(feat_high, feat_low, grad_high_ref, grad_low_ref, keep_ref, send_ref):
    feat = feat_high[...], feat_low[...]
    for row_tap in range(3):
        for e in range(3):
            window = [
                ref[e, 2 - row_tap : 2 - row_tap + R].reshape(R * W, 2 * C)
                for ref in (grad_high_ref, grad_low_ref)
            ]
            store_terms(keep_ref, send_ref, 3 * row_tap + e, tall_product(feat, window, NN), 8)


def feature_adjoint_kernel(grad_high_ref, grad_low_ref, taps_high, taps_low, feat_out):
    total = jnp.zeros((R * W, 2 * C), f32)
    for row_tap in range(3):
        for e in range(3):
            window = [
                ref[e, 2 - row_tap : 2 - row_tap + R].reshape(R * W, 2 * C)
                for ref in (grad_high_ref, grad_low_ref)
            ]
            tap = 3 * row_tap + e
            total = total + tall_product(window, (taps_high[tap], taps_low[tap]), NT)
    for t in range(FR):
        feat_out[t] = total[:, t * C : (t + 1) * C].reshape(R, W, C)


def flow_adjoint_kernel(cot_ref, weight_two_ref, flow_out):
    total = jnp.zeros((R2 * W2, 2 * CF), f32)
    for e in range(3):
        cot = shifted_cot(cot_ref, 2 - e)
        for row_tap in range(3):
            window = [v[2 - row_tap : 2 - row_tap + R2].reshape(R2 * W2, 2 * C) for v in cot]
            total = total + tall_product(window, split(both_frames(weight_two_ref, 3 * row_tap + e)), NT)
    for t in range(FR):
        flow_out[t] = total[:, t * CF : (t + 1) * CF].reshape(R2, W2, CF)


def first_sum_kernel(*refs):
    ones, twos, outs = refs[:4], refs[4:8], refs[8:]
    for slot, out in enumerate(outs):
        for depth, parts in ((slice(0, 8), ones), (slice(8, 24), twos)):
            own, second, first, third = parts
            out[:, :, depth] = (own[0, slot] + second[slot]) + (first[slot] + third[slot])


def second_sum_kernel(own, second, first, third, keep, send):
    keep[...] = (own[0] + second[0]) + (first[0] + third[0])
    send[...] = (own[1] + second[1]) + (first[1] + third[1])


def gather_kernel(own_ref, one_ref, two_ref, three_ref, grad_one_ref, grad_two_ref):
    scale_one = 1.0 / (FR * R * W * 256) ** 0.5
    scale_two = 1.0 / (FR * R2 * W2 * 256) ** 0.5
    for k, ref in enumerate((own_ref, one_ref, two_ref, three_ref)):
        first = 7 * lax.rem(lax.axis_index("x") - k + 4, 4)

        def put(j, ref=ref, first=first):
            grad_one_ref[first + j] = ref[j, :8] * scale_one
            grad_two_ref[first + j] = ref[j, 8:] * scale_two

        for j in range(6):
            put(j)
        pl.when(first < 21)(functools.partial(put, 6))


def params(mebibytes=48):
    return pltpu.CompilerParams(vmem_limit_bytes=mebibytes * 2**20)


def small(kernel, name, out_shape, count, scratch=(), space=VMEM):
    return pl.pallas_call(
        kernel,
        out_shape=out_shape,
        in_specs=[space] * count,
        out_specs=(VMEM,) * len(out_shape),
        scratch_shapes=scratch,
        compiler_params=params(48 if space is VMEM else 64),
        cost_estimate=pl.CostEstimate(flops=10**6, bytes_accessed=10**6, transcendentals=0),
        name=name,
    )


def flow_terms(*args):
    return pl.pallas_call(
        flow_terms_kernel,
        out_shape=(jax.ShapeDtypeStruct((4, 4, 2, 7, 16, C), f32),) * 2
        + (jax.ShapeDtypeStruct((FR, R2 + 2, W2 + 2, C), f32),),
        in_specs=[VMEM] * 7,
        out_specs=(VMEM,) * 3,
        compiler_params=params(),
        cost_estimate=pl.CostEstimate(flops=2 * 10**9, bytes_accessed=5 * 10**6, transcendentals=0),
        name="flow_terms",
    )(*args)


def block_gradient(*args):
    return pl.pallas_call(
        block_kernel,
        out_shape=(jax.ShapeDtypeStruct((3, R + 2, W, 2 * C), bf16),) * 2,
        in_specs=[VMEM] * 8,
        out_specs=(VMEM,) * 2,
        scratch_shapes=[
            pltpu.VMEM((R + 4, PITCH + 8, 2 * C), f32),
            pltpu.VMEM((FR, R + 2, PITCH, C), f32),
            pltpu.VMEM((3, (R + 4) * PITCH, 2 * C), bf16),
            pltpu.VMEM((3, (R + 4) * PITCH, 2 * C), bf16),
            pltpu.VMEM((3, EXT, 2 * C), bf16),
            pltpu.VMEM((3, EXT, 2 * C), bf16),
            pltpu.VMEM((R + 2, PITCH, 2 * C), f32),
        ],
        compiler_params=params(),
        cost_estimate=pl.CostEstimate(flops=5 * 10**9, bytes_accessed=6 * 10**6, transcendentals=200000),
        name="block_gradient",
    )(*args)


def block_terms(*args):
    return pl.pallas_call(
        block_terms_kernel,
        out_shape=(jax.ShapeDtypeStruct((4, 4, 2, 7, 8, C), f32),) * 2,
        in_specs=[VMEM] * 4,
        out_specs=(VMEM,) * 2,
        compiler_params=params(),
        cost_estimate=pl.CostEstimate(flops=10**9, bytes_accessed=10**6, transcendentals=0),
        name="block_terms",
    )(*args)


def adjoint(kernel, name, shape, *args):
    return pl.pallas_call(
        kernel,
        out_shape=jax.ShapeDtypeStruct(shape, f32),
        in_specs=[VMEM] * len(args),
        out_specs=VMEM,
        compiler_params=params(),
        cost_estimate=pl.CostEstimate(flops=2 * 10**9, bytes_accessed=5 * 10**6, transcendentals=0),
        name=name,
    )(*args)


def ring(steps, count=4):
    return [(i, (i + steps) % count) for i in range(count)]


def crossed(steps, axes):
    both = []
    for x in range(4):
        for y in range(4):
            for core in range(2):
                along_x = axes[core] == "x"
                x_to, y_to = ((x + steps) % 4, y) if along_x else (x, (y + steps) % 4)
                both.append((8 * x + 2 * y + core, 8 * x_to + 2 * y_to + core))
    return both


def pairs(start, count=16):
    return [p for i in range(start, count - 1, 2) for p in ((i, i + 1), (i + 1, i))]


def spread(parts, axes):
    if axes == "zl":
        return [lax.ppermute(parts[k], "zl", ring(k)) for k in (2, 1, 3)]
    return [lax.ppermute(parts[k], ("x", "y", "core"), crossed(k, axes)) for k in (2, 1, 3)]


def summed(own, arrived):
    return (own + arrived[0]) + (arrived[1] + arrived[2])


def local(features, weight_one, flow_feats, weight_two, cotangent):
    kernel_one = weight_one.reshape(27, C, C)
    kernel_two = weight_two.reshape(27, CF, C)
    edges = (jax.ShapeDtypeStruct((FR, 2 * W + W2, C), f32),) * 2
    edges = small(
        row_edges_kernel,
        "row_edges",
        edges,
        2,
        [pltpu.VMEM((FR, 2, W, C), f32)] * 2
        + [pltpu.VMEM((FR, 1, W2, C), f32)] * 2
        + [pltpu.SemaphoreType.DMA((4,))],
        HBM,
    )(features, cotangent)
    rows = [lax.ppermute(edges[k], HA, pairs(k)) for k in (1, 0)][::-1]
    feats = (jax.ShapeDtypeStruct((2 * C, R * W), bf16),) * 2
    near = (jax.ShapeDtypeStruct((FR, R2, W2, C), f32),)
    *feats, near = small(prepare_features_kernel, "prepare_features", feats + near, 2)(features, cotangent)
    rows, feats, near = lax.optimization_barrier((rows, feats, near))
    shape = (FR, 56, C)
    edges = small(
        col_edges_kernel,
        "col_edges",
        (jax.ShapeDtypeStruct(shape, f32),) * 2,
        4,
        [pltpu.VMEM((2,) + shape, f32)],
    )(features, near, *rows)
    edges, flow_feats = lax.optimization_barrier((edges, flow_feats))
    cols = [lax.ppermute(edges[k], WA, pairs(k)) for k in (1, 0)][::-1]
    taps = (jax.ShapeDtypeStruct((9, 2 * C, 2 * C), bf16),) * 2
    flows = (jax.ShapeDtypeStruct((2 * CF, R2 * W2), bf16),) * 2
    prepared = small(prepare_kernel, "prepare", taps + flows, 2)(kernel_one, flow_feats)
    cols, prepared = lax.optimization_barrier((cols, prepared))
    swap = [(0, 1), (1, 0)]
    taps, flows = prepared[:2], prepared[2:]
    keep, send, cot = flow_terms(*flows, near, *rows, *cols)
    terms_two = keep + lax.ppermute(send, "core", swap)
    grad_high, grad_low = block_gradient(features, *rows, *cols, *taps, cot)
    terms_two, grad_high, grad_low = lax.optimization_barrier((terms_two, grad_high, grad_low))
    arrived_two = spread(terms_two, ("x", "y"))
    keep, send = block_terms(*feats, grad_high, grad_low)
    terms_one = keep + lax.ppermute(send, "core", swap)
    arrived_one = spread(terms_one, ("x", "y"))
    terms_one, cot, kernel_two = lax.optimization_barrier((terms_one, cot, kernel_two))
    grad_flow = adjoint(flow_adjoint_kernel, "flow_adjoint", (FR, R2, W2, CF), cot, kernel_two)
    arrived_one, arrived_two, grad_flow = lax.optimization_barrier((arrived_one, arrived_two, grad_flow))
    parts = (jax.ShapeDtypeStruct((2, 7, 24, C), f32),) * 4
    parts = small(first_sum_kernel, "first_sum", parts, 8)(terms_one, *arrived_one, terms_two, *arrived_two)
    chunk = (jax.ShapeDtypeStruct((7, 24, C), f32),) * 2
    keep, send = small(second_sum_kernel, "second_sum", chunk, 4)(parts[0], *spread(parts, ("y", "x")))
    arrived = lax.ppermute(send, "zh", swap)
    keep, grad_high, grad_low = lax.optimization_barrier((keep, grad_high, grad_low))
    grad_features = adjoint(
        feature_adjoint_kernel, "feature_adjoint", (FR, R, W, C), grad_high, grad_low, *taps
    )
    arrived, grad_features = lax.optimization_barrier((arrived, grad_features))
    chunk = keep + arrived
    chunk = summed(chunk, spread([chunk] * 4, "zl"))
    pieces = [chunk] + [lax.ppermute(chunk, "x", ring(k)) for k in (1, 2, 3)]
    shares = tuple(jax.ShapeDtypeStruct((27, depth, C), f32) for depth in (8, 16))
    grad_one, grad_two = small(gather_kernel, "gather", shares, 4)(*pieces)
    grad_one = grad_one.reshape(3, 3, 3, 8, C)
    grad_two = grad_two.reshape(3, 3, 3, 16, C)
    return (grad_features, grad_one, grad_flow, grad_two)


def solution(mesh):
    fine = Mesh(mesh.devices.reshape(4, 4, 2, 4, 2), ("x", "zl", "zh", "y", "core"))
    grid = P(None, HA, WA, None)
    share = P(None, None, None, WA, None)
    return jax.shard_map(
        local,
        mesh=fine,
        in_specs=(grid, P(), grid, P(), grid),
        out_specs=(grid, share, grid, share),
        check_vma=False,
    )
```

```python
import functools

import jax
import jax.numpy as jnp
from jax import lax
from jax.experimental import pallas as pl
from jax.experimental.pallas import tpu as pltpu
from jax.sharding import Mesh
from jax.sharding import PartitionSpec as P

FR, R, W, C = 2, 16, 32, 128
R2, W2, CF = 8, 16, 256
PITCH = 40
EXT = (R + 2) * PITCH
COL = 20
HA, WA = ("x", "zl"), ("zh", "y", "core")

f32, bf16 = jnp.float32, jnp.bfloat16
VMEM = pl.BlockSpec(memory_space=pltpu.VMEM)
HBM = pl.BlockSpec(memory_space=pltpu.HBM)


def split(values):
    high = values.astype(bf16)
    return high, (values - high.astype(f32)).astype(bf16)


def dot(left, right, dims):
    return lax.dot_general(left, right, (dims, ((), ())), preferred_element_type=f32)


def product(left, right, dims):
    return dot(left[0], right[0], dims) + (dot(left[0], right[1], dims) + dot(left[1], right[0], dims))


def tall_product(left, right, dims):
    rows = left[0].shape[0]
    both = dot(jnp.concatenate(left, axis=0), right[0], dims)
    return both[:rows] + (both[rows:] + dot(left[0], right[1], dims))


NN = ((1,), (0,))
NT = ((1,), (1,))


def both_frames(kernel, tap):
    first = jnp.concatenate([kernel[9 + tap], kernel[tap]], axis=1)
    second = jnp.concatenate([kernel[18 + tap], kernel[9 + tap]], axis=1)
    return jnp.concatenate([first, second], axis=0)


def store_terms(keep_ref, send_ref, tap, value, depth):
    half = value.shape[0] // 2
    taps = (
        (0, value[:half, C:]),
        (1, value[:half, :C] + value[half:, C:]),
        (2, value[half:, :C]),
    )
    core, y, x, zh = [lax.axis_index(a) for a in ("core", "y", "x", "zh")]
    for time_tap, part in taps:
        number = 9 * time_tap + tap
        slot_x = x ^ (number // 7)
        for owner in range(8):
            slot_y = y ^ (owner % 4)
            slot_zh = zh ^ (owner // 4)
            slots = [jnp.where(core == 0, slot_x, slot_y), jnp.where(core == 0, slot_y, slot_x)]
            first = part[2 * owner * depth : (2 * owner + 1) * depth]
            second = part[(2 * owner + 1) * depth : (2 * owner + 2) * depth]
            keep_ref[slots[0], slots[1], slot_zh, number % 7] = jnp.where(core == 0, first, second)
            send_ref[slots[1], slots[0], slot_zh, number % 7] = jnp.where(core == 0, second, first)


def row_edges_kernel(
    feat_ref, cot_ref, first_ref, second_ref, feat_top, feat_bottom, cot_top, cot_bottom, sems
):
    copies = [
        pltpu.make_async_copy(feat_ref.at[:, 0:2], feat_top, sems.at[0]),
        pltpu.make_async_copy(feat_ref.at[:, R - 2 : R], feat_bottom, sems.at[1]),
        pltpu.make_async_copy(cot_ref.at[:, 0:1], cot_top, sems.at[2]),
        pltpu.make_async_copy(cot_ref.at[:, R2 - 1 : R2], cot_bottom, sems.at[3]),
    ]
    for copy in copies:
        copy.start()
    for copy in copies:
        copy.wait()
    odd = lax.rem(lax.axis_index("zl"), 2) == 1
    for t in range(FR):
        for row in range(2):
            top, bottom = feat_top[t, row], feat_bottom[t, row]
            lines = slice(row * W, (row + 1) * W)
            first_ref[t, lines] = jnp.where(odd, top, bottom)
            second_ref[t, lines] = jnp.where(odd, bottom, top)
        top, bottom = cot_top[t, 0], cot_bottom[t, 0]
        first_ref[t, 2 * W :] = jnp.where(odd, top, bottom)
        second_ref[t, 2 * W :] = jnp.where(odd, bottom, top)


def prepare_features_kernel(feat_ref, cot_ref, feat_high, feat_low, near_cot_ref):
    near_cot_ref[...] = cot_ref[...]
    for t in range(FR):
        lines = slice(t * C, (t + 1) * C)
        feat_high[lines], feat_low[lines] = split(feat_ref[t].reshape(R * W, C).T)


def prepare_kernel(weight_ref, flow_ref, taps_high, taps_low, flow_high, flow_low):
    for tap in range(9):
        taps_high[tap], taps_low[tap] = split(both_frames(weight_ref, tap))
    for t in range(FR):
        lines = slice(t * CF, (t + 1) * CF)
        flow_high[lines], flow_low[lines] = split(flow_ref[t].reshape(R2 * W2, CF).T)


def row_halo(first_ref, second_ref, t, lines):
    odd = lax.rem(lax.axis_index("zl"), 2) == 1
    first, second = first_ref[t, lines], second_ref[t, lines]
    return jnp.where(odd, first, second), jnp.where(odd, second, first)


def col_edges_kernel(feat_ref, cot_ref, row_first_ref, row_second_ref, first_ref, second_ref, edge_ref):
    for t in range(FR):
        halos = [row_halo(row_first_ref, row_second_ref, t, slice(r * W, (r + 1) * W)) for r in range(2)]
        for side, start in ((0, 0), (1, W - 2)):
            for col in range(2):
                at, place = start + col, col * COL
                for row in range(2):
                    edge_ref[side, t, place + row : place + row + 1] = halos[row][0][at : at + 1]
                    low = place + R + 2 + row
                    edge_ref[side, t, low : low + 1] = halos[row][1][at : at + 1]
                edge_ref[side, t, place + 2 : place + 2 + R] = feat_ref[t, :, at, :]
        above, below = row_halo(row_first_ref, row_second_ref, t, slice(2 * W, 2 * W + W2))
        for side, at in ((0, 0), (1, W2 - 1)):
            place = 2 * COL
            edge_ref[side, t, place : place + 1] = above[at : at + 1]
            edge_ref[side, t, place + 1 : place + 1 + R2] = cot_ref[t, :, at, :]
            edge_ref[side, t, place + 1 + R2 : place + 2 + R2] = below[at : at + 1]
    odd = lax.axis_index("core") == 1
    first_ref[...] = jnp.where(odd, edge_ref[0], edge_ref[1])
    second_ref[...] = jnp.where(odd, edge_ref[1], edge_ref[0])


def col_halo(first_ref, second_ref, t, lines):
    odd = lax.axis_index("core") == 1
    first, second = first_ref[t, lines], second_ref[t, lines]
    return jnp.where(odd, first, second), jnp.where(odd, second, first)


def shifted_cot(cot_ref, e):
    both = jnp.concatenate([cot_ref[0, :, e : e + W2, :], cot_ref[1, :, e : e + W2, :]], axis=-1)
    return split(both)


def flow_terms_kernel(
    flow_high, flow_low, local_ref, row_first_ref, row_second_ref, col_first_ref, col_second_ref,
    keep_ref, send_ref, cot_ref,
):
    for t in range(FR):
        above, below = row_halo(row_first_ref, row_second_ref, t, slice(2 * W, 2 * W + W2))
        cot_ref[t, 0, 1 : 1 + W2] = above
        cot_ref[t, 1 : 1 + R2, 1 : 1 + W2] = local_ref[t]
        cot_ref[t, 1 + R2, 1 : 1 + W2] = below
        lines = slice(2 * COL, 2 * COL + R2 + 2)
        left, right = col_halo(col_first_ref, col_second_ref, t, lines)
        cot_ref[t, :, 0] = left
        cot_ref[t, :, 1 + W2] = right
    flow = jnp.concatenate([flow_high[...], flow_high[...], flow_low[...]], axis=1)
    for col_tap in range(3):
        cot = shifted_cot(cot_ref, 2 - col_tap)
        for row_tap in range(3):
            window = [v[2 - row_tap : 2 - row_tap + R2].reshape(R2 * W2, 2 * C) for v in cot]
            window = jnp.concatenate([window[0], window[1], window[0]], axis=0)
            store_terms(keep_ref, send_ref, 3 * row_tap + col_tap, dot(flow, window, NN), 16)


def block_kernel(
    feat_ref, row_first_ref, row_second_ref, col_first_ref, col_second_ref,
    taps_high, taps_low, cot_ref, grad_high_ref, grad_low_ref,
    ext_ref, wide_ref, even_high, even_low, odd_high, odd_low, grad_ref,
):
    ext_ref[...] = jnp.zeros_like(ext_ref)
    for t in range(FR):
        lanes = slice(t * C, (t + 1) * C)
        ext_ref[2 : 2 + R, 3 : 3 + W, lanes] = feat_ref[t]
        for row in range(2):
            above, below = row_halo(row_first_ref, row_second_ref, t, slice(row * W, (row + 1) * W))
            ext_ref[row, 3 : 3 + W, lanes] = above
            ext_ref[R + 2 + row, 3 : 3 + W, lanes] = below
            place = slice(row * COL, row * COL + R + 4)
            left, right = col_halo(col_first_ref, col_second_ref, t, place)
            ext_ref[:, 1 + row, lanes] = left
            ext_ref[:, 3 + W + row, lanes] = right
    for t in range(FR):
        lanes = slice(t * C, (t + 1) * C)
        for row in range(R2 + 2):
            line = cot_ref[t, row] * 0.5
            for target in (2 * row - 1, 2 * row):
                if 0 <= target < R + 2:
                    wide_ref[t, target, pl.ds(0, W2 + 2, stride=2), :] = line
                    wide_ref[t, target, pl.ds(1, W2 + 2, stride=2), :] = line
    rows = R + 4
    for e in range(3):
        shifted = ext_ref[:, e : e + PITCH, :].reshape(rows * PITCH, 2 * C)
        high, low = split(shifted)
        even_high[e] = high
        even_low[e] = low
        odd_high[e] = high[PITCH : PITCH + EXT]
        odd_low[e] = low[PITCH : PITCH + EXT]
    step = EXT // 3
    for part in range(3):
        start = part * step
        total = jnp.zeros((step, 2 * C), f32)
        for row_tap in range(3):
            for e in range(3):
                if row_tap == 1:
                    window = (odd_high[e, start : start + step], odd_low[e, start : start + step])
                else:
                    first = start + row_tap * PITCH
                    window = (even_high[e, first : first + step], even_low[e, first : first + step])
                tap = 3 * row_tap + e
                total = total + product(window, (taps_high[tap], taps_low[tap]), NN)
        sigma = jax.nn.sigmoid(total)
        slope = sigma * (1.0 + total * (1.0 - sigma))
        lines = step // PITCH
        grad_ref[part * lines : (part + 1) * lines] = slope.reshape(lines, PITCH, 2 * C)
    for t in range(FR):
        lanes = slice(t * C, (t + 1) * C)
        grad_ref[:, :, lanes] = grad_ref[:, :, lanes] * wide_ref[t]
    for e in range(3):
        high, low = split(grad_ref[:, 3 - e : 3 - e + W, :])
        grad_high_ref[e] = high
        grad_low_ref[e] = low


def block_terms_kernel(feat_high, feat_low, grad_high_ref, grad_low_ref, keep_ref, send_ref):
    feat = feat_high[...], feat_low[...]
    for row_tap in range(3):
        for e in range(3):
            window = [
                ref[e, 2 - row_tap : 2 - row_tap + R].reshape(R * W, 2 * C)
                for ref in (grad_high_ref, grad_low_ref)
            ]
            store_terms(keep_ref, send_ref, 3 * row_tap + e, tall_product(feat, window, NN), 8)


def feature_adjoint_kernel(grad_high_ref, grad_low_ref, taps_high, taps_low, feat_out):
    total = jnp.zeros((R * W, 2 * C), f32)
    for row_tap in range(3):
        for e in range(3):
            window = [
                ref[e, 2 - row_tap : 2 - row_tap + R].reshape(R * W, 2 * C)
                for ref in (grad_high_ref, grad_low_ref)
            ]
            tap = 3 * row_tap + e
            total = total + tall_product(window, (taps_high[tap], taps_low[tap]), NT)
    for t in range(FR):
        feat_out[t] = total[:, t * C : (t + 1) * C].reshape(R, W, C)


def flow_adjoint_kernel(cot_ref, weight_two_ref, flow_out):
    total = jnp.zeros((R2 * W2, 2 * CF), f32)
    for e in range(3):
        cot = shifted_cot(cot_ref, 2 - e)
        for row_tap in range(3):
            window = [v[2 - row_tap : 2 - row_tap + R2].reshape(R2 * W2, 2 * C) for v in cot]
            total = total + tall_product(window, split(both_frames(weight_two_ref, 3 * row_tap + e)), NT)
    for t in range(FR):
        flow_out[t] = total[:, t * CF : (t + 1) * CF].reshape(R2, W2, CF)


def first_sum_kernel(*refs):
    ones, twos, outs = refs[:4], refs[4:8], refs[8:]
    for slot, out in enumerate(outs):
        for depth, parts in ((slice(0, 8), ones), (slice(8, 24), twos)):
            own, second, first, third = parts
            out[:, :, depth] = (own[0, slot] + second[slot]) + (first[slot] + third[slot])


def second_sum_kernel(own, second, first, third, keep, send):
    keep[...] = (own[0] + second[0]) + (first[0] + third[0])
    send[...] = (own[1] + second[1]) + (first[1] + third[1])


def gather_kernel(own_ref, one_ref, two_ref, three_ref, grad_one_ref, grad_two_ref):
    scale_one = 1.0 / (FR * R * W * 256) ** 0.5
    scale_two = 1.0 / (FR * R2 * W2 * 256) ** 0.5
    for k, ref in enumerate((own_ref, one_ref, two_ref, three_ref)):
        first = 7 * (lax.axis_index("x") ^ k)

        def put(j, ref=ref, first=first):
            grad_one_ref[first + j] = ref[j, :8] * scale_one
            grad_two_ref[first + j] = ref[j, 8:] * scale_two

        for j in range(6):
            put(j)
        pl.when(first < 21)(functools.partial(put, 6))


def params(mebibytes=24):
    return pltpu.CompilerParams(vmem_limit_bytes=mebibytes * 2**20)


def small(kernel, name, out_shape, count, scratch=(), space=VMEM):
    return pl.pallas_call(
        kernel,
        out_shape=out_shape,
        in_specs=[space] * count,
        out_specs=(VMEM,) * len(out_shape),
        scratch_shapes=scratch,
        compiler_params=params(24 if space is VMEM else 64),
        cost_estimate=pl.CostEstimate(flops=10**6, bytes_accessed=10**6, transcendentals=0),
        name=name,
    )


def flow_terms(*args):
    return pl.pallas_call(
        flow_terms_kernel,
        out_shape=(jax.ShapeDtypeStruct((4, 4, 2, 7, 16, C), f32),) * 2
        + (jax.ShapeDtypeStruct((FR, R2 + 2, W2 + 2, C), f32),),
        in_specs=[VMEM] * 7,
        out_specs=(VMEM,) * 3,
        compiler_params=params(),
        cost_estimate=pl.CostEstimate(flops=2 * 10**9, bytes_accessed=5 * 10**6, transcendentals=0),
        name="flow_terms",
    )(*args)


def block_gradient(*args):
    return pl.pallas_call(
        block_kernel,
        out_shape=(jax.ShapeDtypeStruct((3, R + 2, W, 2 * C), bf16),) * 2,
        in_specs=[VMEM] * 8,
        out_specs=(VMEM,) * 2,
        scratch_shapes=[
            pltpu.VMEM((R + 4, PITCH + 8, 2 * C), f32),
            pltpu.VMEM((FR, R + 2, PITCH, C), f32),
            pltpu.VMEM((3, (R + 4) * PITCH, 2 * C), bf16),
            pltpu.VMEM((3, (R + 4) * PITCH, 2 * C), bf16),
            pltpu.VMEM((3, EXT, 2 * C), bf16),
            pltpu.VMEM((3, EXT, 2 * C), bf16),
            pltpu.VMEM((R + 2, PITCH, 2 * C), f32),
        ],
        compiler_params=params(),
        cost_estimate=pl.CostEstimate(flops=5 * 10**9, bytes_accessed=6 * 10**6, transcendentals=200000),
        name="block_gradient",
    )(*args)


def block_terms(*args):
    return pl.pallas_call(
        block_terms_kernel,
        out_shape=(jax.ShapeDtypeStruct((4, 4, 2, 7, 8, C), f32),) * 2,
        in_specs=[VMEM] * 4,
        out_specs=(VMEM,) * 2,
        compiler_params=params(),
        cost_estimate=pl.CostEstimate(flops=10**9, bytes_accessed=10**6, transcendentals=0),
        name="block_terms",
    )(*args)


def adjoint(kernel, name, shape, *args):
    return pl.pallas_call(
        kernel,
        out_shape=jax.ShapeDtypeStruct(shape, f32),
        in_specs=[VMEM] * len(args),
        out_specs=VMEM,
        compiler_params=params(),
        cost_estimate=pl.CostEstimate(flops=2 * 10**9, bytes_accessed=5 * 10**6, transcendentals=0),
        name=name,
    )(*args)


def swaps(mask, count=4):
    return [(i, i ^ mask) for i in range(count)]


def crossed(mask, axes):
    both = []
    for x in range(4):
        for y in range(4):
            for core in range(2):
                x_to, y_to = (x ^ mask, y) if axes[core] == "x" else (x, y ^ mask)
                both.append((8 * x + 2 * y + core, 8 * x_to + 2 * y_to + core))
    return both


def pairs(start, count=16):
    return [p for i in range(start, count - 1, 2) for p in ((i, i + 1), (i + 1, i))]


def spread(parts, axes):
    if axes == "zl":
        return [lax.ppermute(parts[k], "zl", swaps(k)) for k in (3, 2, 1)]
    return [lax.ppermute(parts[k], ("x", "y", "core"), crossed(k, axes)) for k in (2, 1, 3)]


def summed(own, arrived):
    third, second, first = arrived
    return (own + first) + (second + third)


def local(features, weight_one, flow_feats, weight_two, cotangent):
    kernel_one = weight_one.reshape(27, C, C)
    kernel_two = weight_two.reshape(27, CF, C)
    edges = (jax.ShapeDtypeStruct((FR, 2 * W + W2, C), f32),) * 2
    edges = small(
        row_edges_kernel,
        "row_edges",
        edges,
        2,
        [pltpu.VMEM((FR, 2, W, C), f32)] * 2
        + [pltpu.VMEM((FR, 1, W2, C), f32)] * 2
        + [pltpu.SemaphoreType.DMA((4,))],
        HBM,
    )(features, cotangent)
    rows = [lax.ppermute(edges[k], HA, pairs(k)) for k in (1, 0)][::-1]
    feats = (jax.ShapeDtypeStruct((2 * C, R * W), bf16),) * 2
    near = (jax.ShapeDtypeStruct((FR, R2, W2, C), f32),)
    *feats, near = small(prepare_features_kernel, "prepare_features", feats + near, 2)(features, cotangent)
    rows, feats, near = lax.optimization_barrier((rows, feats, near))
    shape = (FR, 56, C)
    edges = small(
        col_edges_kernel,
        "col_edges",
        (jax.ShapeDtypeStruct(shape, f32),) * 2,
        4,
        [pltpu.VMEM((2,) + shape, f32)],
    )(features, near, *rows)
    edges, flow_feats = lax.optimization_barrier((edges, flow_feats))
    cols = [lax.ppermute(edges[k], WA, pairs(k)) for k in (1, 0)][::-1]
    taps = (jax.ShapeDtypeStruct((9, 2 * C, 2 * C), bf16),) * 2
    flows = (jax.ShapeDtypeStruct((2 * CF, R2 * W2), bf16),) * 2
    prepared = small(prepare_kernel, "prepare", taps + flows, 2)(kernel_one, flow_feats)
    cols, prepared = lax.optimization_barrier((cols, prepared))
    swap = [(0, 1), (1, 0)]
    taps, flows = prepared[:2], prepared[2:]
    keep, send, cot = flow_terms(*flows, near, *rows, *cols)
    terms_two = keep + lax.ppermute(send, "core", swap)
    grad_high, grad_low = block_gradient(features, *rows, *cols, *taps, cot)
    terms_two, grad_high, grad_low = lax.optimization_barrier((terms_two, grad_high, grad_low))
    arrived_two = spread(terms_two, ("x", "y"))
    keep, send = block_terms(*feats, grad_high, grad_low)
    terms_one = keep + lax.ppermute(send, "core", swap)
    arrived_one = spread(terms_one, ("x", "y"))
    terms_one, cot, kernel_two = lax.optimization_barrier((terms_one, cot, kernel_two))
    grad_flow = adjoint(flow_adjoint_kernel, "flow_adjoint", (FR, R2, W2, CF), cot, kernel_two)
    arrived_one, arrived_two, grad_flow = lax.optimization_barrier((arrived_one, arrived_two, grad_flow))
    parts = (jax.ShapeDtypeStruct((2, 7, 24, C), f32),) * 4
    parts = small(first_sum_kernel, "first_sum", parts, 8)(terms_one, *arrived_one, terms_two, *arrived_two)
    chunk = (jax.ShapeDtypeStruct((7, 24, C), f32),) * 2
    keep, send = small(second_sum_kernel, "second_sum", chunk, 4)(parts[0], *spread(parts, ("y", "x")))
    arrived = lax.ppermute(send, ("zl", "zh"), [(i, 7 - i) for i in range(8)])
    keep, grad_high, grad_low = lax.optimization_barrier((keep, grad_high, grad_low))
    grad_features = adjoint(
        feature_adjoint_kernel, "feature_adjoint", (FR, R, W, C), grad_high, grad_low, *taps
    )
    arrived, grad_features = lax.optimization_barrier((arrived, grad_features))
    chunk = keep + arrived
    chunk = summed(chunk, spread([chunk] * 4, "zl"))
    pieces = [chunk] + [lax.ppermute(chunk, "x", swaps(k)) for k in (1, 2, 3)]
    shares = tuple(jax.ShapeDtypeStruct((27, depth, C), f32) for depth in (8, 16))
    grad_one, grad_two = small(gather_kernel, "gather", shares, 4)(*pieces)
    grad_one = grad_one.reshape(3, 3, 3, 8, C)
    grad_two = grad_two.reshape(3, 3, 3, 16, C)
    return (grad_features, grad_one, grad_flow, grad_two)


def solution(mesh):
    fine = Mesh(mesh.devices.reshape(4, 4, 2, 4, 2), ("x", "zl", "zh", "y", "core"))
    grid = P(None, HA, WA, None)
    share = P(None, None, None, WA, None)
    return jax.shard_map(
        local,
        mesh=fine,
        in_specs=(grid, P(), grid, P(), grid),
        out_specs=(grid, share, grid, share),
        check_vma=False,
    )
```

```python
import functools

import jax
import jax.numpy as jnp
from jax import lax
from jax.experimental import pallas as pl
from jax.experimental.pallas import tpu as pltpu
from jax.sharding import Mesh
from jax.sharding import PartitionSpec as P

FR, R, W, C = 2, 16, 32, 128
R2, W2, CF = 8, 16, 256
PITCH = 40
EXT = (R + 2) * PITCH
COL = 20
HA, WA = ("x", "zl"), ("zh", "y", "core")

f32, bf16 = jnp.float32, jnp.bfloat16
VMEM = pl.BlockSpec(memory_space=pltpu.VMEM)
HBM = pl.BlockSpec(memory_space=pltpu.HBM)


def split(values):
    high = values.astype(bf16)
    return high, (values - high.astype(f32)).astype(bf16)


def dot(left, right, dims):
    return lax.dot_general(left, right, (dims, ((), ())), preferred_element_type=f32)


def product(left, right, dims):
    return dot(left[0], right[0], dims) + (dot(left[0], right[1], dims) + dot(left[1], right[0], dims))


def tall_product(left, right, dims):
    rows = left[0].shape[0]
    both = dot(jnp.concatenate(left, axis=0), right[0], dims)
    return both[:rows] + (both[rows:] + dot(left[0], right[1], dims))


NN = ((1,), (0,))
NT = ((1,), (1,))


def both_frames(kernel, tap):
    first = jnp.concatenate([kernel[9 + tap], kernel[tap]], axis=1)
    second = jnp.concatenate([kernel[18 + tap], kernel[9 + tap]], axis=1)
    return jnp.concatenate([first, second], axis=0)


def store_terms(keep_ref, send_ref, tap, value, depth):
    half = value.shape[0] // 2
    taps = (
        (0, value[:half, C:]),
        (1, value[:half, :C] + value[half:, C:]),
        (2, value[half:, :C]),
    )
    core, y, x, zh = [lax.axis_index(a) for a in ("core", "y", "x", "zh")]
    for time_tap, part in taps:
        number = 9 * time_tap + tap
        slot_x = x ^ (number // 7)
        for owner in range(8):
            slot_y = y ^ (owner % 4)
            slot_zh = zh ^ (owner // 4)
            slots = [jnp.where(core == 0, slot_x, slot_y), jnp.where(core == 0, slot_y, slot_x)]
            first = part[2 * owner * depth : (2 * owner + 1) * depth]
            second = part[(2 * owner + 1) * depth : (2 * owner + 2) * depth]
            keep_ref[slots[0], slots[1], slot_zh, number % 7] = jnp.where(core == 0, first, second)
            send_ref[slots[1], slots[0], slot_zh, number % 7] = jnp.where(core == 0, second, first)


def row_edges_kernel(
    feat_ref, cot_ref, first_ref, second_ref, feat_top, feat_bottom, cot_top, cot_bottom, sems
):
    copies = [
        pltpu.make_async_copy(feat_ref.at[:, 0:2], feat_top, sems.at[0]),
        pltpu.make_async_copy(feat_ref.at[:, R - 2 : R], feat_bottom, sems.at[1]),
        pltpu.make_async_copy(cot_ref.at[:, 0:1], cot_top, sems.at[2]),
        pltpu.make_async_copy(cot_ref.at[:, R2 - 1 : R2], cot_bottom, sems.at[3]),
    ]
    for copy in copies:
        copy.start()
    for copy in copies:
        copy.wait()
    odd = lax.rem(lax.axis_index("zl"), 2) == 1
    for t in range(FR):
        for row in range(2):
            top, bottom = feat_top[t, row], feat_bottom[t, row]
            lines = slice(row * W, (row + 1) * W)
            first_ref[t, lines] = jnp.where(odd, top, bottom)
            second_ref[t, lines] = jnp.where(odd, bottom, top)
        top, bottom = cot_top[t, 0], cot_bottom[t, 0]
        first_ref[t, 2 * W :] = jnp.where(odd, top, bottom)
        second_ref[t, 2 * W :] = jnp.where(odd, bottom, top)


def prepare_features_kernel(feat_ref, cot_ref, feat_high, feat_low, near_cot_ref):
    near_cot_ref[...] = cot_ref[...]
    for t in range(FR):
        lines = slice(t * C, (t + 1) * C)
        feat_high[lines], feat_low[lines] = split(feat_ref[t].reshape(R * W, C).T)


def prepare_kernel(weight_ref, flow_ref, taps_high, taps_low, flow_high, flow_low):
    for tap in range(9):
        taps_high[tap], taps_low[tap] = split(both_frames(weight_ref, tap))
    for t in range(FR):
        lines = slice(t * CF, (t + 1) * CF)
        flow_high[lines], flow_low[lines] = split(flow_ref[t].reshape(R2 * W2, CF).T)


def row_halo(first_ref, second_ref, t, lines):
    odd = lax.rem(lax.axis_index("zl"), 2) == 1
    first, second = first_ref[t, lines], second_ref[t, lines]
    return jnp.where(odd, first, second), jnp.where(odd, second, first)


def col_edges_kernel(feat_ref, cot_ref, row_second_ref, row_first_ref, first_ref, second_ref, edge_ref):
    for t in range(FR):
        halos = [row_halo(row_first_ref, row_second_ref, t, slice(r * W, (r + 1) * W)) for r in range(2)]
        for side, start in ((0, 0), (1, W - 2)):
            for col in range(2):
                at, place = start + col, col * COL
                for row in range(2):
                    edge_ref[side, t, place + row : place + row + 1] = halos[row][0][at : at + 1]
                    low = place + R + 2 + row
                    edge_ref[side, t, low : low + 1] = halos[row][1][at : at + 1]
                edge_ref[side, t, place + 2 : place + 2 + R] = feat_ref[t, :, at, :]
        above, below = row_halo(row_first_ref, row_second_ref, t, slice(2 * W, 2 * W + W2))
        for side, at in ((0, 0), (1, W2 - 1)):
            place = 2 * COL
            edge_ref[side, t, place : place + 1] = above[at : at + 1]
            edge_ref[side, t, place + 1 : place + 1 + R2] = cot_ref[t, :, at, :]
            edge_ref[side, t, place + 1 + R2 : place + 2 + R2] = below[at : at + 1]
    odd = lax.axis_index("core") == 1
    first_ref[...] = jnp.where(odd, edge_ref[0], edge_ref[1])
    second_ref[...] = jnp.where(odd, edge_ref[1], edge_ref[0])


def col_halo(first_ref, second_ref, t, lines):
    odd = lax.axis_index("core") == 1
    first, second = first_ref[t, lines], second_ref[t, lines]
    return jnp.where(odd, first, second), jnp.where(odd, second, first)


def shifted_cot(cot_ref, e):
    both = jnp.concatenate([cot_ref[0, :, e : e + W2, :], cot_ref[1, :, e : e + W2, :]], axis=-1)
    return split(both)


def flow_terms_kernel(
    flow_high, flow_low, local_ref, row_second_ref, row_first_ref, col_second_ref, col_first_ref,
    keep_ref, send_ref, cot_ref,
):
    for t in range(FR):
        above, below = row_halo(row_first_ref, row_second_ref, t, slice(2 * W, 2 * W + W2))
        cot_ref[t, 0, 1 : 1 + W2] = above
        cot_ref[t, 1 : 1 + R2, 1 : 1 + W2] = local_ref[t]
        cot_ref[t, 1 + R2, 1 : 1 + W2] = below
        lines = slice(2 * COL, 2 * COL + R2 + 2)
        left, right = col_halo(col_first_ref, col_second_ref, t, lines)
        cot_ref[t, :, 0] = left
        cot_ref[t, :, 1 + W2] = right
    flow = jnp.concatenate([flow_high[...], flow_high[...], flow_low[...]], axis=1)
    for col_tap in range(3):
        cot = shifted_cot(cot_ref, 2 - col_tap)
        for row_tap in range(3):
            window = [v[2 - row_tap : 2 - row_tap + R2].reshape(R2 * W2, 2 * C) for v in cot]
            window = jnp.concatenate([window[0], window[1], window[0]], axis=0)
            store_terms(keep_ref, send_ref, 3 * row_tap + col_tap, dot(flow, window, NN), 16)


def block_kernel(
    feat_ref, row_second_ref, row_first_ref, col_second_ref, col_first_ref,
    taps_high, taps_low, cot_ref, grad_high_ref, grad_low_ref,
    ext_ref, wide_ref, even_high, even_low, odd_high, odd_low, grad_ref,
):
    ext_ref[...] = jnp.zeros_like(ext_ref)
    for t in range(FR):
        lanes = slice(t * C, (t + 1) * C)
        ext_ref[2 : 2 + R, 3 : 3 + W, lanes] = feat_ref[t]
        for row in range(2):
            above, below = row_halo(row_first_ref, row_second_ref, t, slice(row * W, (row + 1) * W))
            ext_ref[row, 3 : 3 + W, lanes] = above
            ext_ref[R + 2 + row, 3 : 3 + W, lanes] = below
            place = slice(row * COL, row * COL + R + 4)
            left, right = col_halo(col_first_ref, col_second_ref, t, place)
            ext_ref[:, 1 + row, lanes] = left
            ext_ref[:, 3 + W + row, lanes] = right
    for t in range(FR):
        lanes = slice(t * C, (t + 1) * C)
        for row in range(R2 + 2):
            line = cot_ref[t, row] * 0.5
            for target in (2 * row - 1, 2 * row):
                if 0 <= target < R + 2:
                    wide_ref[t, target, pl.ds(0, W2 + 2, stride=2), :] = line
                    wide_ref[t, target, pl.ds(1, W2 + 2, stride=2), :] = line
    rows = R + 4
    for e in range(3):
        shifted = ext_ref[:, e : e + PITCH, :].reshape(rows * PITCH, 2 * C)
        high, low = split(shifted)
        even_high[e] = high
        even_low[e] = low
        odd_high[e] = high[PITCH : PITCH + EXT]
        odd_low[e] = low[PITCH : PITCH + EXT]
    step = EXT // 3
    for part in range(3):
        start = part * step
        total = jnp.zeros((step, 2 * C), f32)
        for row_tap in range(3):
            for e in range(3):
                if row_tap == 1:
                    window = (odd_high[e, start : start + step], odd_low[e, start : start + step])
                else:
                    first = start + row_tap * PITCH
                    window = (even_high[e, first : first + step], even_low[e, first : first + step])
                tap = 3 * row_tap + e
                total = total + product(window, (taps_high[tap], taps_low[tap]), NN)
        sigma = jax.nn.sigmoid(total)
        slope = sigma * (1.0 + total * (1.0 - sigma))
        lines = step // PITCH
        grad_ref[part * lines : (part + 1) * lines] = slope.reshape(lines, PITCH, 2 * C)
    for t in range(FR):
        lanes = slice(t * C, (t + 1) * C)
        grad_ref[:, :, lanes] = grad_ref[:, :, lanes] * wide_ref[t]
    for e in range(3):
        high, low = split(grad_ref[:, 3 - e : 3 - e + W, :])
        grad_high_ref[e] = high
        grad_low_ref[e] = low


def block_terms_kernel(feat_high, feat_low, grad_high_ref, grad_low_ref, keep_ref, send_ref):
    feat = feat_high[...], feat_low[...]
    for row_tap in range(3):
        for e in range(3):
            window = [
                ref[e, 2 - row_tap : 2 - row_tap + R].reshape(R * W, 2 * C)
                for ref in (grad_high_ref, grad_low_ref)
            ]
            store_terms(keep_ref, send_ref, 3 * row_tap + e, tall_product(feat, window, NN), 8)


def feature_adjoint_kernel(grad_high_ref, grad_low_ref, taps_high, taps_low, feat_out):
    total = jnp.zeros((R * W, 2 * C), f32)
    for row_tap in range(3):
        for e in range(3):
            window = [
                ref[e, 2 - row_tap : 2 - row_tap + R].reshape(R * W, 2 * C)
                for ref in (grad_high_ref, grad_low_ref)
            ]
            tap = 3 * row_tap + e
            total = total + tall_product(window, (taps_high[tap], taps_low[tap]), NT)
    for t in range(FR):
        feat_out[t] = total[:, t * C : (t + 1) * C].reshape(R, W, C)


def flow_adjoint_kernel(cot_ref, weight_two_ref, flow_out):
    total = jnp.zeros((R2 * W2, 2 * CF), f32)
    for e in range(3):
        cot = shifted_cot(cot_ref, 2 - e)
        for row_tap in range(3):
            window = [v[2 - row_tap : 2 - row_tap + R2].reshape(R2 * W2, 2 * C) for v in cot]
            total = total + tall_product(window, split(both_frames(weight_two_ref, 3 * row_tap + e)), NT)
    for t in range(FR):
        flow_out[t] = total[:, t * CF : (t + 1) * CF].reshape(R2, W2, CF)


def first_sum_kernel(*refs):
    ones, twos, outs = refs[:4], refs[4:8], refs[8:]
    for slot, out in enumerate(outs):
        for depth, parts in ((slice(0, 8), ones), (slice(8, 24), twos)):
            own, second, first, third = parts
            out[:, :, depth] = (own[0, slot] + second[slot]) + (first[slot] + third[slot])


def second_sum_kernel(own, second, first, third, keep, send):
    keep[...] = (own[0] + second[0]) + (first[0] + third[0])
    send[...] = (own[1] + second[1]) + (first[1] + third[1])


def gather_kernel(own_ref, one_ref, two_ref, three_ref, grad_one_ref, grad_two_ref):
    scale_one = 1.0 / (FR * R * W * 256) ** 0.5
    scale_two = 1.0 / (FR * R2 * W2 * 256) ** 0.5
    for k, ref in enumerate((own_ref, one_ref, two_ref, three_ref)):
        first = 7 * (lax.axis_index("x") ^ k)

        def put(j, ref=ref, first=first):
            grad_one_ref[first + j] = ref[j, :8] * scale_one
            grad_two_ref[first + j] = ref[j, 8:] * scale_two

        for j in range(6):
            put(j)
        pl.when(first < 21)(functools.partial(put, 6))


def params(mebibytes=24):
    return pltpu.CompilerParams(vmem_limit_bytes=mebibytes * 2**20)


def small(kernel, name, out_shape, count, scratch=(), space=VMEM):
    return pl.pallas_call(
        kernel,
        out_shape=out_shape,
        in_specs=[space] * count,
        out_specs=(VMEM,) * len(out_shape),
        scratch_shapes=scratch,
        compiler_params=params(24 if space is VMEM else 64),
        cost_estimate=pl.CostEstimate(flops=10**6, bytes_accessed=10**6, transcendentals=0),
        name=name,
    )


def flow_terms(*args):
    return pl.pallas_call(
        flow_terms_kernel,
        out_shape=(jax.ShapeDtypeStruct((4, 4, 2, 7, 16, C), f32),) * 2
        + (jax.ShapeDtypeStruct((FR, R2 + 2, W2 + 2, C), f32),),
        in_specs=[VMEM] * 7,
        out_specs=(VMEM,) * 3,
        compiler_params=params(),
        cost_estimate=pl.CostEstimate(flops=2 * 10**9, bytes_accessed=5 * 10**6, transcendentals=0),
        name="flow_terms",
    )(*args)


def block_gradient(*args):
    return pl.pallas_call(
        block_kernel,
        out_shape=(jax.ShapeDtypeStruct((3, R + 2, W, 2 * C), bf16),) * 2,
        in_specs=[VMEM] * 8,
        out_specs=(VMEM,) * 2,
        scratch_shapes=[
            pltpu.VMEM((R + 4, PITCH + 8, 2 * C), f32),
            pltpu.VMEM((FR, R + 2, PITCH, C), f32),
            pltpu.VMEM((3, (R + 4) * PITCH, 2 * C), bf16),
            pltpu.VMEM((3, (R + 4) * PITCH, 2 * C), bf16),
            pltpu.VMEM((3, EXT, 2 * C), bf16),
            pltpu.VMEM((3, EXT, 2 * C), bf16),
            pltpu.VMEM((R + 2, PITCH, 2 * C), f32),
        ],
        compiler_params=params(),
        cost_estimate=pl.CostEstimate(flops=5 * 10**9, bytes_accessed=6 * 10**6, transcendentals=200000),
        name="block_gradient",
    )(*args)


def block_terms(*args):
    return pl.pallas_call(
        block_terms_kernel,
        out_shape=(jax.ShapeDtypeStruct((4, 4, 2, 7, 8, C), f32),) * 2,
        in_specs=[VMEM] * 4,
        out_specs=(VMEM,) * 2,
        compiler_params=params(),
        cost_estimate=pl.CostEstimate(flops=10**9, bytes_accessed=10**6, transcendentals=0),
        name="block_terms",
    )(*args)


def adjoint(kernel, name, shape, *args):
    return pl.pallas_call(
        kernel,
        out_shape=jax.ShapeDtypeStruct(shape, f32),
        in_specs=[VMEM] * len(args),
        out_specs=VMEM,
        compiler_params=params(),
        cost_estimate=pl.CostEstimate(flops=2 * 10**9, bytes_accessed=5 * 10**6, transcendentals=0),
        name=name,
    )(*args)


def swaps(mask, count=4):
    return [(i, i ^ mask) for i in range(count)]


def crossed(mask, axes):
    both = []
    for x in range(4):
        for y in range(4):
            for core in range(2):
                x_to, y_to = (x ^ mask, y) if axes[core] == "x" else (x, y ^ mask)
                both.append((8 * x + 2 * y + core, 8 * x_to + 2 * y_to + core))
    return both


def pairs(start, count=16):
    return [p for i in range(start, count - 1, 2) for p in ((i, i + 1), (i + 1, i))]


def spread(parts, axes):
    if axes == "zl":
        return [lax.ppermute(parts[k], "zl", swaps(k)) for k in (3, 2, 1)]
    return [lax.ppermute(parts[k], ("x", "y", "core"), crossed(k, axes)) for k in (2, 1, 3)]


def summed(own, arrived):
    third, second, first = arrived
    return (own + first) + (second + third)


def local(features, weight_one, flow_feats, weight_two, cotangent):
    kernel_one = weight_one.reshape(27, C, C)
    kernel_two = weight_two.reshape(27, CF, C)
    edges = (jax.ShapeDtypeStruct((FR, 2 * W + W2, C), f32),) * 2
    edges = small(
        row_edges_kernel,
        "row_edges",
        edges,
        2,
        [pltpu.VMEM((FR, 2, W, C), f32)] * 2
        + [pltpu.VMEM((FR, 1, W2, C), f32)] * 2
        + [pltpu.SemaphoreType.DMA((4,))],
        HBM,
    )(features, cotangent)
    rows = [lax.ppermute(edges[k], HA, pairs(k)) for k in (1, 0)]
    feats = (jax.ShapeDtypeStruct((2 * C, R * W), bf16),) * 2
    near = (jax.ShapeDtypeStruct((FR, R2, W2, C), f32),)
    *feats, near = small(prepare_features_kernel, "prepare_features", feats + near, 2)(features, cotangent)
    rows, feats, near = lax.optimization_barrier((rows, feats, near))
    shape = (FR, 56, C)
    edges = small(
        col_edges_kernel,
        "col_edges",
        (jax.ShapeDtypeStruct(shape, f32),) * 2,
        4,
        [pltpu.VMEM((2,) + shape, f32)],
    )(features, near, *rows)
    edges, flow_feats = lax.optimization_barrier((edges, flow_feats))
    cols = [lax.ppermute(edges[k], WA, pairs(k)) for k in (1, 0)]
    taps = (jax.ShapeDtypeStruct((9, 2 * C, 2 * C), bf16),) * 2
    flows = (jax.ShapeDtypeStruct((2 * CF, R2 * W2), bf16),) * 2
    prepared = small(prepare_kernel, "prepare", taps + flows, 2)(kernel_one, flow_feats)
    cols, prepared = lax.optimization_barrier((cols, prepared))
    swap = [(0, 1), (1, 0)]
    taps, flows = prepared[:2], prepared[2:]
    keep, send, cot = flow_terms(*flows, near, *rows, *cols)
    terms_two = keep + lax.ppermute(send, "core", swap)
    grad_high, grad_low = block_gradient(features, *rows, *cols, *taps, cot)
    terms_two, grad_high, grad_low = lax.optimization_barrier((terms_two, grad_high, grad_low))
    arrived_two = spread(terms_two, ("x", "y"))
    keep, send = block_terms(*feats, grad_high, grad_low)
    terms_one = keep + lax.ppermute(send, "core", swap)
    arrived_one = spread(terms_one, ("x", "y"))
    terms_one, cot, kernel_two = lax.optimization_barrier((terms_one, cot, kernel_two))
    grad_flow = adjoint(flow_adjoint_kernel, "flow_adjoint", (FR, R2, W2, CF), cot, kernel_two)
    arrived_one, arrived_two, grad_flow = lax.optimization_barrier((arrived_one, arrived_two, grad_flow))
    parts = (jax.ShapeDtypeStruct((2, 7, 24, C), f32),) * 4
    parts = small(first_sum_kernel, "first_sum", parts, 8)(terms_one, *arrived_one, terms_two, *arrived_two)
    chunk = (jax.ShapeDtypeStruct((7, 24, C), f32),) * 2
    keep, send = small(second_sum_kernel, "second_sum", chunk, 4)(parts[0], *spread(parts, ("y", "x")))
    arrived = lax.ppermute(send, ("zl", "zh"), [(i, 7 - i) for i in range(8)])
    keep, grad_high, grad_low = lax.optimization_barrier((keep, grad_high, grad_low))
    grad_features = adjoint(
        feature_adjoint_kernel, "feature_adjoint", (FR, R, W, C), grad_high, grad_low, *taps
    )
    arrived, grad_features = lax.optimization_barrier((arrived, grad_features))
    chunk = keep + arrived
    chunk = summed(chunk, spread([chunk] * 4, "zl"))
    pieces = [chunk] + [lax.ppermute(chunk, "x", swaps(k)) for k in (1, 2, 3)]
    shares = tuple(jax.ShapeDtypeStruct((27, depth, C), f32) for depth in (8, 16))
    grad_one, grad_two = small(gather_kernel, "gather", shares, 4)(*pieces)
    grad_one = grad_one.reshape(3, 3, 3, 8, C)
    grad_two = grad_two.reshape(3, 3, 3, 16, C)
    return (grad_features, grad_one, grad_flow, grad_two)


def solution(mesh):
    fine = Mesh(mesh.devices.reshape(4, 4, 2, 4, 2), ("x", "zl", "zh", "y", "core"))
    grid = P(None, HA, WA, None)
    share = P(None, None, None, WA, None)
    return jax.shard_map(
        local,
        mesh=fine,
        in_specs=(grid, P(), grid, P(), grid),
        out_specs=(grid, share, grid, share),
        check_vma=False,
    )
```

```python
import functools

import jax
import jax.numpy as jnp
from jax import lax
from jax.experimental import pallas as pl
from jax.experimental.pallas import tpu as pltpu
from jax.sharding import Mesh
from jax.sharding import PartitionSpec as P

FR, R, W, C = 2, 16, 32, 128
R2, W2, CF = 8, 16, 256
PITCH = 40
EXT = (R + 2) * PITCH
COL = 20
HA, WA = ("x", "zl"), ("zh", "y", "core")

f32, bf16 = jnp.float32, jnp.bfloat16
VMEM = pl.BlockSpec(memory_space=pltpu.VMEM)
HBM = pl.BlockSpec(memory_space=pltpu.HBM)


def split(values):
    high = values.astype(bf16)
    return high, (values - high.astype(f32)).astype(bf16)


def dot(left, right, dims):
    return lax.dot_general(left, right, (dims, ((), ())), preferred_element_type=f32)


def product(left, right, dims):
    return dot(left[0], right[0], dims) + (dot(left[0], right[1], dims) + dot(left[1], right[0], dims))


def tall_product(left, right, dims):
    rows = left[0].shape[0]
    both = dot(jnp.concatenate(left, axis=0), right[0], dims)
    return both[:rows] + (both[rows:] + dot(left[0], right[1], dims))


NN = ((1,), (0,))
NT = ((1,), (1,))


def both_frames(kernel, tap):
    first = jnp.concatenate([kernel[9 + tap], kernel[tap]], axis=1)
    second = jnp.concatenate([kernel[18 + tap], kernel[9 + tap]], axis=1)
    return jnp.concatenate([first, second], axis=0)


def store_terms(keep_ref, send_ref, tap, value, depth):
    half = value.shape[0] // 2
    taps = (
        (0, value[:half, C:]),
        (1, value[:half, :C] + value[half:, C:]),
        (2, value[half:, :C]),
    )
    core, y, x, zh = [lax.axis_index(a) for a in ("core", "y", "x", "zh")]
    for time_tap, part in taps:
        number = 9 * time_tap + tap
        slot_x = x ^ (number // 7)
        for owner in range(8):
            slot_y = y ^ (owner % 4)
            slot_zh = zh ^ (owner // 4)
            slots = [jnp.where(core == 0, slot_x, slot_y), jnp.where(core == 0, slot_y, slot_x)]
            first = part[2 * owner * depth : (2 * owner + 1) * depth]
            second = part[(2 * owner + 1) * depth : (2 * owner + 2) * depth]
            keep_ref[slots[0], slots[1], slot_zh, number % 7] = jnp.where(core == 0, first, second)
            send_ref[slots[1], slots[0], slot_zh, number % 7] = jnp.where(core == 0, second, first)


def row_edges_kernel(
    feat_ref, cot_ref, first_ref, second_ref, feat_top, feat_bottom, cot_top, cot_bottom, sems
):
    copies = [
        pltpu.make_async_copy(feat_ref.at[:, 0:2], feat_top, sems.at[0]),
        pltpu.make_async_copy(feat_ref.at[:, R - 2 : R], feat_bottom, sems.at[1]),
        pltpu.make_async_copy(cot_ref.at[:, 0:1], cot_top, sems.at[2]),
        pltpu.make_async_copy(cot_ref.at[:, R2 - 1 : R2], cot_bottom, sems.at[3]),
    ]
    for copy in copies:
        copy.start()
    for copy in copies:
        copy.wait()
    odd = lax.rem(lax.axis_index("zl"), 2) == 1
    for t in range(FR):
        for row in range(2):
            top, bottom = feat_top[t, row], feat_bottom[t, row]
            lines = slice(row * W, (row + 1) * W)
            first_ref[t, lines] = jnp.where(odd, top, bottom)
            second_ref[t, lines] = jnp.where(odd, bottom, top)
        top, bottom = cot_top[t, 0], cot_bottom[t, 0]
        first_ref[t, 2 * W :] = jnp.where(odd, top, bottom)
        second_ref[t, 2 * W :] = jnp.where(odd, bottom, top)


def prepare_features_kernel(feat_ref, cot_ref, feat_high, feat_low, near_cot_ref):
    near_cot_ref[...] = cot_ref[...]
    for t in range(FR):
        lines = slice(t * C, (t + 1) * C)
        feat_high[lines], feat_low[lines] = split(feat_ref[t].reshape(R * W, C).T)


def prepare_kernel(weight_ref, flow_ref, taps_high, taps_low, flow_high, flow_low):
    for tap in range(9):
        taps_high[tap], taps_low[tap] = split(both_frames(weight_ref, tap))
    for t in range(FR):
        lines = slice(t * CF, (t + 1) * CF)
        flow_high[lines], flow_low[lines] = split(flow_ref[t].reshape(R2 * W2, CF).T)


def row_halo(first_ref, second_ref, t, lines):
    odd = lax.rem(lax.axis_index("zl"), 2) == 1
    first, second = first_ref[t, lines], second_ref[t, lines]
    return jnp.where(odd, first, second), jnp.where(odd, second, first)


def col_edges_kernel(feat_ref, cot_ref, row_second_ref, row_first_ref, first_ref, second_ref, edge_ref):
    for t in range(FR):
        halos = [row_halo(row_first_ref, row_second_ref, t, slice(r * W, (r + 1) * W)) for r in range(2)]
        for side, start in ((0, 0), (1, W - 2)):
            for col in range(2):
                at, place = start + col, col * COL
                for row in range(2):
                    edge_ref[side, t, place + row : place + row + 1] = halos[row][0][at : at + 1]
                    low = place + R + 2 + row
                    edge_ref[side, t, low : low + 1] = halos[row][1][at : at + 1]
                edge_ref[side, t, place + 2 : place + 2 + R] = feat_ref[t, :, at, :]
        above, below = row_halo(row_first_ref, row_second_ref, t, slice(2 * W, 2 * W + W2))
        for side, at in ((0, 0), (1, W2 - 1)):
            place = 2 * COL
            edge_ref[side, t, place : place + 1] = above[at : at + 1]
            edge_ref[side, t, place + 1 : place + 1 + R2] = cot_ref[t, :, at, :]
            edge_ref[side, t, place + 1 + R2 : place + 2 + R2] = below[at : at + 1]
    odd = lax.axis_index("core") == 1
    first_ref[...] = jnp.where(odd, edge_ref[0], edge_ref[1])
    second_ref[...] = jnp.where(odd, edge_ref[1], edge_ref[0])


def col_halo(first_ref, second_ref, t, lines):
    odd = lax.axis_index("core") == 1
    first, second = first_ref[t, lines], second_ref[t, lines]
    return jnp.where(odd, first, second), jnp.where(odd, second, first)


def shifted_cot(cot_ref, e):
    both = jnp.concatenate([cot_ref[0, :, e : e + W2, :], cot_ref[1, :, e : e + W2, :]], axis=-1)
    return split(both)


def flow_terms_kernel(
    flow_high, flow_low, local_ref, row_second_ref, row_first_ref, col_second_ref, col_first_ref,
    keep_ref, send_ref, cot_ref,
):
    for t in range(FR):
        above, below = row_halo(row_first_ref, row_second_ref, t, slice(2 * W, 2 * W + W2))
        cot_ref[t, 0, 1 : 1 + W2] = above
        cot_ref[t, 1 : 1 + R2, 1 : 1 + W2] = local_ref[t]
        cot_ref[t, 1 + R2, 1 : 1 + W2] = below
        lines = slice(2 * COL, 2 * COL + R2 + 2)
        left, right = col_halo(col_first_ref, col_second_ref, t, lines)
        cot_ref[t, :, 0] = left
        cot_ref[t, :, 1 + W2] = right
    flow = jnp.concatenate([flow_high[...], flow_high[...], flow_low[...]], axis=1)
    for col_tap in range(3):
        cot = shifted_cot(cot_ref, 2 - col_tap)
        for row_tap in range(3):
            window = [v[2 - row_tap : 2 - row_tap + R2].reshape(R2 * W2, 2 * C) for v in cot]
            window = jnp.concatenate([window[0], window[1], window[0]], axis=0)
            store_terms(keep_ref, send_ref, 3 * row_tap + col_tap, dot(flow, window, NN), 16)


def block_kernel(
    feat_ref, row_second_ref, row_first_ref, col_second_ref, col_first_ref,
    taps_high, taps_low, cot_ref, grad_high_ref, grad_low_ref,
    ext_ref, wide_ref, even_high, even_low, odd_high, odd_low, grad_ref,
):
    ext_ref[...] = jnp.zeros_like(ext_ref)
    for t in range(FR):
        lanes = slice(t * C, (t + 1) * C)
        ext_ref[2 : 2 + R, 3 : 3 + W, lanes] = feat_ref[t]
        for row in range(2):
            above, below = row_halo(row_first_ref, row_second_ref, t, slice(row * W, (row + 1) * W))
            ext_ref[row, 3 : 3 + W, lanes] = above
            ext_ref[R + 2 + row, 3 : 3 + W, lanes] = below
            place = slice(row * COL, row * COL + R + 4)
            left, right = col_halo(col_first_ref, col_second_ref, t, place)
            ext_ref[:, 1 + row, lanes] = left
            ext_ref[:, 3 + W + row, lanes] = right
    for t in range(FR):
        lanes = slice(t * C, (t + 1) * C)
        for row in range(R2 + 2):
            line = cot_ref[t, row] * 0.5
            for target in (2 * row - 1, 2 * row):
                if 0 <= target < R + 2:
                    wide_ref[t, target, pl.ds(0, W2 + 2, stride=2), :] = line
                    wide_ref[t, target, pl.ds(1, W2 + 2, stride=2), :] = line
    rows = R + 4
    for e in range(3):
        shifted = ext_ref[:, e : e + PITCH, :].reshape(rows * PITCH, 2 * C)
        high, low = split(shifted)
        even_high[e] = high
        even_low[e] = low
        odd_high[e] = high[PITCH : PITCH + EXT]
        odd_low[e] = low[PITCH : PITCH + EXT]
    step = EXT // 3
    for part in range(3):
        start = part * step
        total = jnp.zeros((step, 2 * C), f32)
        for row_tap in range(3):
            for e in range(3):
                if row_tap == 1:
                    window = (odd_high[e, start : start + step], odd_low[e, start : start + step])
                else:
                    first = start + row_tap * PITCH
                    window = (even_high[e, first : first + step], even_low[e, first : first + step])
                tap = 3 * row_tap + e
                total = total + product(window, (taps_high[tap], taps_low[tap]), NN)
        sigma = jax.nn.sigmoid(total)
        slope = sigma * (1.0 + total * (1.0 - sigma))
        lines = step // PITCH
        grad_ref[part * lines : (part + 1) * lines] = slope.reshape(lines, PITCH, 2 * C)
    for t in range(FR):
        lanes = slice(t * C, (t + 1) * C)
        grad_ref[:, :, lanes] = grad_ref[:, :, lanes] * wide_ref[t]
    for e in range(3):
        high, low = split(grad_ref[:, 3 - e : 3 - e + W, :])
        grad_high_ref[e] = high
        grad_low_ref[e] = low


def block_terms_kernel(feat_high, feat_low, grad_high_ref, grad_low_ref, keep_ref, send_ref):
    feat = feat_high[...], feat_low[...]
    for row_tap in range(3):
        for e in range(3):
            window = [
                ref[e, 2 - row_tap : 2 - row_tap + R].reshape(R * W, 2 * C)
                for ref in (grad_high_ref, grad_low_ref)
            ]
            store_terms(keep_ref, send_ref, 3 * row_tap + e, tall_product(feat, window, NN), 8)


def feature_adjoint_kernel(grad_high_ref, grad_low_ref, taps_high, taps_low, feat_out):
    total = jnp.zeros((R * W, 2 * C), f32)
    for row_tap in range(3):
        for e in range(3):
            window = [
                ref[e, 2 - row_tap : 2 - row_tap + R].reshape(R * W, 2 * C)
                for ref in (grad_high_ref, grad_low_ref)
            ]
            tap = 3 * row_tap + e
            total = total + tall_product(window, (taps_high[tap], taps_low[tap]), NT)
    for t in range(FR):
        feat_out[t] = total[:, t * C : (t + 1) * C].reshape(R, W, C)


def flow_adjoint_kernel(cot_ref, weight_two_ref, flow_out):
    total = jnp.zeros((R2 * W2, 2 * CF), f32)
    for e in range(3):
        cot = shifted_cot(cot_ref, 2 - e)
        for row_tap in range(3):
            window = [v[2 - row_tap : 2 - row_tap + R2].reshape(R2 * W2, 2 * C) for v in cot]
            total = total + tall_product(window, split(both_frames(weight_two_ref, 3 * row_tap + e)), NT)
    for t in range(FR):
        flow_out[t] = total[:, t * CF : (t + 1) * CF].reshape(R2, W2, CF)


def halving_kernel(own, first_half, second_half, keep, first_send, second_send):
    keep[:2] = own[0, :2] + first_half[0]
    first_send[...] = own[3, :2] + first_half[1]
    keep[2:] = own[0, 2:] + second_half[1]
    second_send[...] = own[1, 2:] + second_half[0]


def first_sum_kernel(keep_one, ones_first, ones_second, keep_two, twos_first, twos_second, *outs):
    for slot, out in enumerate(outs):
        ones, twos = (ones_first, twos_first) if slot < 2 else (ones_second, twos_second)
        out[:, :, :8] = keep_one[slot] + ones[slot % 2]
        out[:, :, 8:] = keep_two[slot] + twos[slot % 2]


def second_sum_kernel(own, second, first, third, keep, send):
    keep[...] = (own[0] + second[0]) + (first[0] + third[0])
    send[...] = (own[1] + second[1]) + (first[1] + third[1])


def gather_kernel(own_ref, one_ref, two_ref, three_ref, grad_one_ref, grad_two_ref):
    scale_one = 1.0 / (FR * R * W * 256) ** 0.5
    scale_two = 1.0 / (FR * R2 * W2 * 256) ** 0.5
    for k, ref in enumerate((own_ref, one_ref, two_ref, three_ref)):
        first = 7 * (lax.axis_index("x") ^ k)

        def put(j, ref=ref, first=first):
            grad_one_ref[first + j] = ref[j, :8] * scale_one
            grad_two_ref[first + j] = ref[j, 8:] * scale_two

        for j in range(6):
            put(j)
        pl.when(first < 21)(functools.partial(put, 6))


def params(mebibytes=24):
    return pltpu.CompilerParams(vmem_limit_bytes=mebibytes * 2**20)


def small(kernel, name, out_shape, count, scratch=(), space=VMEM):
    return pl.pallas_call(
        kernel,
        out_shape=out_shape,
        in_specs=[space] * count,
        out_specs=(VMEM,) * len(out_shape),
        scratch_shapes=scratch,
        compiler_params=params(24 if space is VMEM else 64),
        cost_estimate=pl.CostEstimate(flops=10**6, bytes_accessed=10**6, transcendentals=0),
        name=name,
    )


def flow_terms(*args):
    return pl.pallas_call(
        flow_terms_kernel,
        out_shape=(jax.ShapeDtypeStruct((4, 4, 2, 7, 16, C), f32),) * 2
        + (jax.ShapeDtypeStruct((FR, R2 + 2, W2 + 2, C), f32),),
        in_specs=[VMEM] * 7,
        out_specs=(VMEM,) * 3,
        compiler_params=params(),
        cost_estimate=pl.CostEstimate(flops=2 * 10**9, bytes_accessed=5 * 10**6, transcendentals=0),
        name="flow_terms",
    )(*args)


def block_gradient(*args):
    return pl.pallas_call(
        block_kernel,
        out_shape=(jax.ShapeDtypeStruct((3, R + 2, W, 2 * C), bf16),) * 2,
        in_specs=[VMEM] * 8,
        out_specs=(VMEM,) * 2,
        scratch_shapes=[
            pltpu.VMEM((R + 4, PITCH + 8, 2 * C), f32),
            pltpu.VMEM((FR, R + 2, PITCH, C), f32),
            pltpu.VMEM((3, (R + 4) * PITCH, 2 * C), bf16),
            pltpu.VMEM((3, (R + 4) * PITCH, 2 * C), bf16),
            pltpu.VMEM((3, EXT, 2 * C), bf16),
            pltpu.VMEM((3, EXT, 2 * C), bf16),
            pltpu.VMEM((R + 2, PITCH, 2 * C), f32),
        ],
        compiler_params=params(),
        cost_estimate=pl.CostEstimate(flops=5 * 10**9, bytes_accessed=6 * 10**6, transcendentals=200000),
        name="block_gradient",
    )(*args)


def block_terms(*args):
    return pl.pallas_call(
        block_terms_kernel,
        out_shape=(jax.ShapeDtypeStruct((4, 4, 2, 7, 8, C), f32),) * 2,
        in_specs=[VMEM] * 4,
        out_specs=(VMEM,) * 2,
        compiler_params=params(),
        cost_estimate=pl.CostEstimate(flops=10**9, bytes_accessed=10**6, transcendentals=0),
        name="block_terms",
    )(*args)


def adjoint(kernel, name, shape, *args):
    return pl.pallas_call(
        kernel,
        out_shape=jax.ShapeDtypeStruct(shape, f32),
        in_specs=[VMEM] * len(args),
        out_specs=VMEM,
        compiler_params=params(),
        cost_estimate=pl.CostEstimate(flops=2 * 10**9, bytes_accessed=5 * 10**6, transcendentals=0),
        name=name,
    )(*args)


def swaps(mask, count=4):
    return [(i, i ^ mask) for i in range(count)]


def crossed(mask, axes):
    both = []
    for x in range(4):
        for y in range(4):
            for core in range(2):
                x_to, y_to = (x ^ mask, y) if axes[core] == "x" else (x, y ^ mask)
                both.append((8 * x + 2 * y + core, 8 * x_to + 2 * y_to + core))
    return both


def pairs(start, count=16):
    return [p for i in range(start, count - 1, 2) for p in ((i, i + 1), (i + 1, i))]


def spread(parts, axes):
    if axes == "zl":
        return [lax.ppermute(parts[k], "zl", swaps(k)) for k in (3, 2, 1)]
    return cross([parts[k] for k in (2, 1, 3)], axes, (2, 1, 3))


def cross(parts, axes, masks):
    return [lax.ppermute(v, ("x", "y", "core"), crossed(k, axes)) for v, k in zip(parts, masks)]


def halved(terms, arrived):
    slots, _, *rest = terms.shape
    shapes = [jax.ShapeDtypeStruct((count, *rest), f32) for count in (4, 2, 2)]
    return small(halving_kernel, "halving", tuple(shapes), 3)(terms, *arrived)


def summed(own, arrived):
    third, second, first = arrived
    return (own + first) + (second + third)


def local(features, weight_one, flow_feats, weight_two, cotangent):
    kernel_one = weight_one.reshape(27, C, C)
    kernel_two = weight_two.reshape(27, CF, C)
    edges = (jax.ShapeDtypeStruct((FR, 2 * W + W2, C), f32),) * 2
    edges = small(
        row_edges_kernel,
        "row_edges",
        edges,
        2,
        [pltpu.VMEM((FR, 2, W, C), f32)] * 2
        + [pltpu.VMEM((FR, 1, W2, C), f32)] * 2
        + [pltpu.SemaphoreType.DMA((4,))],
        HBM,
    )(features, cotangent)
    rows = [lax.ppermute(edges[k], HA, pairs(k)) for k in (1, 0)]
    feats = (jax.ShapeDtypeStruct((2 * C, R * W), bf16),) * 2
    near = (jax.ShapeDtypeStruct((FR, R2, W2, C), f32),)
    *feats, near = small(prepare_features_kernel, "prepare_features", feats + near, 2)(features, cotangent)
    rows, feats, near = lax.optimization_barrier((rows, feats, near))
    shape = (FR, 56, C)
    edges = small(
        col_edges_kernel,
        "col_edges",
        (jax.ShapeDtypeStruct(shape, f32),) * 2,
        4,
        [pltpu.VMEM((2,) + shape, f32)],
    )(features, near, *rows)
    edges, flow_feats = lax.optimization_barrier((edges, flow_feats))
    cols = [lax.ppermute(edges[k], WA, pairs(k)) for k in (1, 0)]
    taps = (jax.ShapeDtypeStruct((9, 2 * C, 2 * C), bf16),) * 2
    flows = (jax.ShapeDtypeStruct((2 * CF, R2 * W2), bf16),) * 2
    prepared = small(prepare_kernel, "prepare", taps + flows, 2)(kernel_one, flow_feats)
    cols, prepared = lax.optimization_barrier((cols, prepared))
    swap = [(0, 1), (1, 0)]
    taps, flows = prepared[:2], prepared[2:]
    keep, send, cot = flow_terms(*flows, near, *rows, *cols)
    terms_two = keep + lax.ppermute(send, "core", swap)
    grad_high, grad_low = block_gradient(features, *rows, *cols, *taps, cot)
    terms_two, grad_high, grad_low = lax.optimization_barrier((terms_two, grad_high, grad_low))
    axes = ("x", "y")
    arrived_two = cross((terms_two[1:3, :2], terms_two[2:4, 2:]), axes, (1, 3))
    keep, send = block_terms(*feats, grad_high, grad_low)
    terms_one = keep + lax.ppermute(send, "core", swap)
    arrived_one = cross((terms_one[1:3, :2], terms_one[2:4, 2:]), axes, (1, 3))
    terms_one, cot, kernel_two = lax.optimization_barrier((terms_one, cot, kernel_two))
    grad_flow = adjoint(flow_adjoint_kernel, "flow_adjoint", (FR, R2, W2, CF), cot, kernel_two)
    arrived_two, grad_flow = lax.optimization_barrier((arrived_two, grad_flow))
    keep_two, *sends = halved(terms_two, arrived_two)
    arrived_two = cross(sends, axes, (3, 1))
    keep_one, *sends = halved(terms_one, arrived_one)
    arrived_one = cross(sends, axes, (3, 1))
    parts = (jax.ShapeDtypeStruct((2, 7, 24, C), f32),) * 4
    parts = small(first_sum_kernel, "first_sum", parts, 6)(keep_one, *arrived_one, keep_two, *arrived_two)
    chunk = (jax.ShapeDtypeStruct((7, 24, C), f32),) * 2
    keep, send = small(second_sum_kernel, "second_sum", chunk, 4)(parts[0], *spread(parts, ("y", "x")))
    arrived = lax.ppermute(send, ("zl", "zh"), [(i, 7 - i) for i in range(8)])
    keep, grad_high, grad_low = lax.optimization_barrier((keep, grad_high, grad_low))
    grad_features = adjoint(
        feature_adjoint_kernel, "feature_adjoint", (FR, R, W, C), grad_high, grad_low, *taps
    )
    arrived, grad_features = lax.optimization_barrier((arrived, grad_features))
    chunk = keep + arrived
    chunk = summed(chunk, spread([chunk] * 4, "zl"))
    pieces = [chunk] + [lax.ppermute(chunk, "x", swaps(k)) for k in (1, 2, 3)]
    shares = tuple(jax.ShapeDtypeStruct((27, depth, C), f32) for depth in (8, 16))
    grad_one, grad_two = small(gather_kernel, "gather", shares, 4)(*pieces)
    grad_one = grad_one.reshape(3, 3, 3, 8, C)
    grad_two = grad_two.reshape(3, 3, 3, 16, C)
    return (grad_features, grad_one, grad_flow, grad_two)


def solution(mesh):
    fine = Mesh(mesh.devices.reshape(4, 4, 2, 4, 2), ("x", "zl", "zh", "y", "core"))
    grid = P(None, HA, WA, None)
    share = P(None, None, None, WA, None)
    return jax.shard_map(
        local,
        mesh=fine,
        in_specs=(grid, P(), grid, P(), grid),
        out_specs=(grid, share, grid, share),
        check_vma=False,
    )
```

```python
import functools

import jax
import jax.numpy as jnp
from jax import lax
from jax.experimental import pallas as pl
from jax.experimental.pallas import tpu as pltpu
from jax.sharding import Mesh
from jax.sharding import PartitionSpec as P

FR, R, W, C = 2, 16, 32, 128
R2, W2, CF = 8, 16, 256
PITCH = 40
EXT = (R + 2) * PITCH
COL = 20
HA, WA = ("x", "zl"), ("zh", "y", "core")

f32, bf16 = jnp.float32, jnp.bfloat16
VMEM = pl.BlockSpec(memory_space=pltpu.VMEM)
HBM = pl.BlockSpec(memory_space=pltpu.HBM)


def split(values):
    high = values.astype(bf16)
    return high, (values - high.astype(f32)).astype(bf16)


def dot(left, right, dims):
    return lax.dot_general(left, right, (dims, ((), ())), preferred_element_type=f32)


def product(left, right, dims):
    return dot(left[0], right[0], dims) + (dot(left[0], right[1], dims) + dot(left[1], right[0], dims))


def tall_product(left, right, dims):
    rows = left[0].shape[0]
    both = dot(jnp.concatenate(left, axis=0), right[0], dims)
    return both[:rows] + (both[rows:] + dot(left[0], right[1], dims))


NN = ((1,), (0,))
NT = ((1,), (1,))


def both_frames(kernel, tap):
    first = jnp.concatenate([kernel[9 + tap], kernel[tap]], axis=1)
    second = jnp.concatenate([kernel[18 + tap], kernel[9 + tap]], axis=1)
    return jnp.concatenate([first, second], axis=0)


def store_terms(keep_ref, send_ref, tap, value, depth):
    half = value.shape[0] // 2
    taps = (
        (0, value[:half, C:]),
        (1, value[:half, :C] + value[half:, C:]),
        (2, value[half:, :C]),
    )
    core, y, x, zh = [lax.axis_index(a) for a in ("core", "y", "x", "zh")]
    for time_tap, part in taps:
        number = 9 * time_tap + tap
        slot_x = x ^ (number // 7)
        for owner in range(8):
            slot_y = y ^ (owner % 4)
            slot_zh = zh ^ (owner // 4)
            slots = [jnp.where(core == 0, slot_x, slot_y), jnp.where(core == 0, slot_y, slot_x)]
            first = part[2 * owner * depth : (2 * owner + 1) * depth]
            second = part[(2 * owner + 1) * depth : (2 * owner + 2) * depth]
            keep_ref[slots[0], slots[1], slot_zh, number % 7] = jnp.where(core == 0, first, second)
            send_ref[slots[1], slots[0], slot_zh, number % 7] = jnp.where(core == 0, second, first)


def row_edges_kernel(
    feat_ref, cot_ref, first_ref, second_ref, feat_top, feat_bottom, cot_top, cot_bottom, sems
):
    copies = [
        pltpu.make_async_copy(feat_ref.at[:, 0:2], feat_top, sems.at[0]),
        pltpu.make_async_copy(feat_ref.at[:, R - 2 : R], feat_bottom, sems.at[1]),
        pltpu.make_async_copy(cot_ref.at[:, 0:1], cot_top, sems.at[2]),
        pltpu.make_async_copy(cot_ref.at[:, R2 - 1 : R2], cot_bottom, sems.at[3]),
    ]
    for copy in copies:
        copy.start()
    for copy in copies:
        copy.wait()
    odd = lax.rem(lax.axis_index("zl"), 2) == 1
    for t in range(FR):
        for row in range(2):
            top, bottom = feat_top[t, row], feat_bottom[t, row]
            lines = slice(row * W, (row + 1) * W)
            first_ref[t, lines] = jnp.where(odd, top, bottom)
            second_ref[t, lines] = jnp.where(odd, bottom, top)
        top, bottom = cot_top[t, 0], cot_bottom[t, 0]
        first_ref[t, 2 * W :] = jnp.where(odd, top, bottom)
        second_ref[t, 2 * W :] = jnp.where(odd, bottom, top)


def prepare_features_kernel(feat_ref, cot_ref, feat_high, feat_low, near_cot_ref):
    near_cot_ref[...] = cot_ref[...]
    for t in range(FR):
        lines = slice(t * C, (t + 1) * C)
        feat_high[lines], feat_low[lines] = split(feat_ref[t].reshape(R * W, C).T)


def prepare_kernel(weight_ref, flow_ref, taps_high, taps_low, flow_high, flow_low):
    for tap in range(9):
        taps_high[tap], taps_low[tap] = split(both_frames(weight_ref, tap))
    for t in range(FR):
        lines = slice(t * CF, (t + 1) * CF)
        flow_high[lines], flow_low[lines] = split(flow_ref[t].reshape(R2 * W2, CF).T)


def row_halo(first_ref, second_ref, t, lines):
    odd = lax.rem(lax.axis_index("zl"), 2) == 1
    first, second = first_ref[t, lines], second_ref[t, lines]
    return jnp.where(odd, first, second), jnp.where(odd, second, first)


def col_edges_kernel(feat_ref, cot_ref, row_second_ref, row_first_ref, first_ref, second_ref, edge_ref):
    for t in range(FR):
        halos = [row_halo(row_first_ref, row_second_ref, t, slice(r * W, (r + 1) * W)) for r in range(2)]
        for side, start in ((0, 0), (1, W - 2)):
            for col in range(2):
                at, place = start + col, col * COL
                for row in range(2):
                    edge_ref[side, t, place + row : place + row + 1] = halos[row][0][at : at + 1]
                    low = place + R + 2 + row
                    edge_ref[side, t, low : low + 1] = halos[row][1][at : at + 1]
                edge_ref[side, t, place + 2 : place + 2 + R] = feat_ref[t, :, at, :]
        above, below = row_halo(row_first_ref, row_second_ref, t, slice(2 * W, 2 * W + W2))
        for side, at in ((0, 0), (1, W2 - 1)):
            place = 2 * COL
            edge_ref[side, t, place : place + 1] = above[at : at + 1]
            edge_ref[side, t, place + 1 : place + 1 + R2] = cot_ref[t, :, at, :]
            edge_ref[side, t, place + 1 + R2 : place + 2 + R2] = below[at : at + 1]
    odd = lax.axis_index("core") == 1
    first_ref[...] = jnp.where(odd, edge_ref[0], edge_ref[1])
    second_ref[...] = jnp.where(odd, edge_ref[1], edge_ref[0])


def col_halo(first_ref, second_ref, t, lines):
    odd = lax.axis_index("core") == 1
    first, second = first_ref[t, lines], second_ref[t, lines]
    return jnp.where(odd, first, second), jnp.where(odd, second, first)


def shifted_cot(cot_ref, e):
    both = jnp.concatenate([cot_ref[0, :, e : e + W2, :], cot_ref[1, :, e : e + W2, :]], axis=-1)
    return split(both)


def flow_terms_kernel(
    flow_high, flow_low, local_ref, row_second_ref, row_first_ref, col_second_ref, col_first_ref,
    keep_ref, send_ref, cot_ref,
):
    for t in range(FR):
        above, below = row_halo(row_first_ref, row_second_ref, t, slice(2 * W, 2 * W + W2))
        cot_ref[t, 0, 1 : 1 + W2] = above
        cot_ref[t, 1 : 1 + R2, 1 : 1 + W2] = local_ref[t]
        cot_ref[t, 1 + R2, 1 : 1 + W2] = below
        lines = slice(2 * COL, 2 * COL + R2 + 2)
        left, right = col_halo(col_first_ref, col_second_ref, t, lines)
        cot_ref[t, :, 0] = left
        cot_ref[t, :, 1 + W2] = right
    flow = jnp.concatenate([flow_high[...], flow_high[...], flow_low[...]], axis=1)
    for col_tap in range(3):
        cot = shifted_cot(cot_ref, 2 - col_tap)
        for row_tap in range(3):
            window = [v[2 - row_tap : 2 - row_tap + R2].reshape(R2 * W2, 2 * C) for v in cot]
            window = jnp.concatenate([window[0], window[1], window[0]], axis=0)
            store_terms(keep_ref, send_ref, 3 * row_tap + col_tap, dot(flow, window, NN), 16)


def block_kernel(
    feat_ref, row_second_ref, row_first_ref, col_second_ref, col_first_ref,
    taps_high, taps_low, cot_ref, grad_high_ref, grad_low_ref,
    ext_ref, wide_ref, even_high, even_low, odd_high, odd_low, grad_ref,
):
    ext_ref[...] = jnp.zeros_like(ext_ref)
    for t in range(FR):
        lanes = slice(t * C, (t + 1) * C)
        ext_ref[2 : 2 + R, 3 : 3 + W, lanes] = feat_ref[t]
        for row in range(2):
            above, below = row_halo(row_first_ref, row_second_ref, t, slice(row * W, (row + 1) * W))
            ext_ref[row, 3 : 3 + W, lanes] = above
            ext_ref[R + 2 + row, 3 : 3 + W, lanes] = below
            place = slice(row * COL, row * COL + R + 4)
            left, right = col_halo(col_first_ref, col_second_ref, t, place)
            ext_ref[:, 1 + row, lanes] = left
            ext_ref[:, 3 + W + row, lanes] = right
    for t in range(FR):
        lanes = slice(t * C, (t + 1) * C)
        for row in range(R2 + 2):
            line = cot_ref[t, row] * 0.5
            for target in (2 * row - 1, 2 * row):
                if 0 <= target < R + 2:
                    wide_ref[t, target, pl.ds(0, W2 + 2, stride=2), :] = line
                    wide_ref[t, target, pl.ds(1, W2 + 2, stride=2), :] = line
    rows = R + 4
    for e in range(3):
        shifted = ext_ref[:, e : e + PITCH, :].reshape(rows * PITCH, 2 * C)
        high, low = split(shifted)
        even_high[e] = high
        even_low[e] = low
        odd_high[e] = high[PITCH : PITCH + EXT]
        odd_low[e] = low[PITCH : PITCH + EXT]
    step = EXT // 3
    for part in range(3):
        start = part * step
        total = jnp.zeros((step, 2 * C), f32)
        for row_tap in range(3):
            for e in range(3):
                if row_tap == 1:
                    window = (odd_high[e, start : start + step], odd_low[e, start : start + step])
                else:
                    first = start + row_tap * PITCH
                    window = (even_high[e, first : first + step], even_low[e, first : first + step])
                tap = 3 * row_tap + e
                total = total + product(window, (taps_high[tap], taps_low[tap]), NN)
        sigma = jax.nn.sigmoid(total)
        slope = sigma * (1.0 + total * (1.0 - sigma))
        lines = step // PITCH
        grad_ref[part * lines : (part + 1) * lines] = slope.reshape(lines, PITCH, 2 * C)
    for t in range(FR):
        lanes = slice(t * C, (t + 1) * C)
        grad_ref[:, :, lanes] = grad_ref[:, :, lanes] * wide_ref[t]
    for e in range(3):
        high, low = split(grad_ref[:, 3 - e : 3 - e + W, :])
        grad_high_ref[e] = high
        grad_low_ref[e] = low


def block_terms_kernel(feat_high, feat_low, grad_high_ref, grad_low_ref, keep_ref, send_ref):
    feat = feat_high[...], feat_low[...]
    for row_tap in range(3):
        for e in range(3):
            window = [
                ref[e, 2 - row_tap : 2 - row_tap + R].reshape(R * W, 2 * C)
                for ref in (grad_high_ref, grad_low_ref)
            ]
            store_terms(keep_ref, send_ref, 3 * row_tap + e, tall_product(feat, window, NN), 8)


def feature_adjoint_kernel(grad_high_ref, grad_low_ref, taps_high, taps_low, feat_out):
    total = jnp.zeros((R * W, 2 * C), f32)
    for row_tap in range(3):
        for e in range(3):
            window = [
                ref[e, 2 - row_tap : 2 - row_tap + R].reshape(R * W, 2 * C)
                for ref in (grad_high_ref, grad_low_ref)
            ]
            tap = 3 * row_tap + e
            total = total + tall_product(window, (taps_high[tap], taps_low[tap]), NT)
    for t in range(FR):
        feat_out[t] = total[:, t * C : (t + 1) * C].reshape(R, W, C)


def flow_adjoint_kernel(cot_ref, weight_two_ref, flow_out):
    total = jnp.zeros((R2 * W2, 2 * CF), f32)
    for e in range(3):
        cot = shifted_cot(cot_ref, 2 - e)
        for row_tap in range(3):
            window = [v[2 - row_tap : 2 - row_tap + R2].reshape(R2 * W2, 2 * C) for v in cot]
            total = total + tall_product(window, split(both_frames(weight_two_ref, 3 * row_tap + e)), NT)
    for t in range(FR):
        flow_out[t] = total[:, t * CF : (t + 1) * CF].reshape(R2, W2, CF)


def first_sum_kernel(*refs):
    ones, twos, outs = refs[:4], refs[4:8], refs[8:]
    for slot, out in enumerate(outs):
        for depth, parts in ((slice(0, 8), ones), (slice(8, 24), twos)):
            own, first, third, second = parts
            out[:, :, depth] = (own[0, slot] + first[slot]) + (second[slot] + third[slot])


def second_sum_kernel(own, first, third, second, keep, send):
    keep[...] = (own[0] + first[0]) + (second[0] + third[0])
    send[...] = (own[1] + first[1]) + (second[1] + third[1])


def gather_kernel(own_ref, one_ref, two_ref, three_ref, grad_one_ref, grad_two_ref):
    scale_one = 1.0 / (FR * R * W * 256) ** 0.5
    scale_two = 1.0 / (FR * R2 * W2 * 256) ** 0.5
    for k, ref in enumerate((own_ref, one_ref, two_ref, three_ref)):
        first = 7 * (lax.axis_index("x") ^ k)

        def put(j, ref=ref, first=first):
            grad_one_ref[first + j] = ref[j, :8] * scale_one
            grad_two_ref[first + j] = ref[j, 8:] * scale_two

        for j in range(6):
            put(j)
        pl.when(first < 21)(functools.partial(put, 6))


def params(mebibytes=24):
    return pltpu.CompilerParams(vmem_limit_bytes=mebibytes * 2**20)


def small(kernel, name, out_shape, count, scratch=(), space=VMEM):
    return pl.pallas_call(
        kernel,
        out_shape=out_shape,
        in_specs=[space] * count,
        out_specs=(VMEM,) * len(out_shape),
        scratch_shapes=scratch,
        compiler_params=params(24 if space is VMEM else 64),
        cost_estimate=pl.CostEstimate(flops=10**6, bytes_accessed=10**6, transcendentals=0),
        name=name,
    )


def flow_terms(*args):
    return pl.pallas_call(
        flow_terms_kernel,
        out_shape=(jax.ShapeDtypeStruct((4, 4, 2, 7, 16, C), f32),) * 2
        + (jax.ShapeDtypeStruct((FR, R2 + 2, W2 + 2, C), f32),),
        in_specs=[VMEM] * 7,
        out_specs=(VMEM,) * 3,
        compiler_params=params(),
        cost_estimate=pl.CostEstimate(flops=2 * 10**9, bytes_accessed=5 * 10**6, transcendentals=0),
        name="flow_terms",
    )(*args)


def block_gradient(*args):
    return pl.pallas_call(
        block_kernel,
        out_shape=(jax.ShapeDtypeStruct((3, R + 2, W, 2 * C), bf16),) * 2,
        in_specs=[VMEM] * 8,
        out_specs=(VMEM,) * 2,
        scratch_shapes=[
            pltpu.VMEM((R + 4, PITCH + 8, 2 * C), f32),
            pltpu.VMEM((FR, R + 2, PITCH, C), f32),
            pltpu.VMEM((3, (R + 4) * PITCH, 2 * C), bf16),
            pltpu.VMEM((3, (R + 4) * PITCH, 2 * C), bf16),
            pltpu.VMEM((3, EXT, 2 * C), bf16),
            pltpu.VMEM((3, EXT, 2 * C), bf16),
            pltpu.VMEM((R + 2, PITCH, 2 * C), f32),
        ],
        compiler_params=params(),
        cost_estimate=pl.CostEstimate(flops=5 * 10**9, bytes_accessed=6 * 10**6, transcendentals=200000),
        name="block_gradient",
    )(*args)


def block_terms(*args):
    return pl.pallas_call(
        block_terms_kernel,
        out_shape=(jax.ShapeDtypeStruct((4, 4, 2, 7, 8, C), f32),) * 2,
        in_specs=[VMEM] * 4,
        out_specs=(VMEM,) * 2,
        compiler_params=params(),
        cost_estimate=pl.CostEstimate(flops=10**9, bytes_accessed=10**6, transcendentals=0),
        name="block_terms",
    )(*args)


def adjoint(kernel, name, shape, *args):
    return pl.pallas_call(
        kernel,
        out_shape=jax.ShapeDtypeStruct(shape, f32),
        in_specs=[VMEM] * len(args),
        out_specs=VMEM,
        compiler_params=params(),
        cost_estimate=pl.CostEstimate(flops=2 * 10**9, bytes_accessed=5 * 10**6, transcendentals=0),
        name=name,
    )(*args)


def swaps(mask, count=4):
    return [(i, i ^ mask) for i in range(count)]


def crossed(mask, axes):
    both = []
    for x in range(4):
        for y in range(4):
            for core in range(2):
                x_to, y_to = (x ^ mask, y) if axes[core] == "x" else (x, y ^ mask)
                both.append((8 * x + 2 * y + core, 8 * x_to + 2 * y_to + core))
    return both


def pairs(start, count=16):
    return [p for i in range(start, count - 1, 2) for p in ((i, i + 1), (i + 1, i))]


def spread(parts, axes):
    if axes == "zl":
        return [lax.ppermute(parts[k], "zl", swaps(k)) for k in (3, 2, 1)]
    return [lax.ppermute(parts[k], ("x", "y", "core"), crossed(k, axes)) for k in (1, 3, 2)]


def summed(own, arrived):
    third, second, first = arrived
    return (own + first) + (second + third)


def local(features, weight_one, flow_feats, weight_two, cotangent):
    kernel_one = weight_one.reshape(27, C, C)
    kernel_two = weight_two.reshape(27, CF, C)
    edges = (jax.ShapeDtypeStruct((FR, 2 * W + W2, C), f32),) * 2
    edges = small(
        row_edges_kernel,
        "row_edges",
        edges,
        2,
        [pltpu.VMEM((FR, 2, W, C), f32)] * 2
        + [pltpu.VMEM((FR, 1, W2, C), f32)] * 2
        + [pltpu.SemaphoreType.DMA((4,))],
        HBM,
    )(features, cotangent)
    rows = [lax.ppermute(edges[k], HA, pairs(k)) for k in (1, 0)]
    feats = (jax.ShapeDtypeStruct((2 * C, R * W), bf16),) * 2
    near = (jax.ShapeDtypeStruct((FR, R2, W2, C), f32),)
    *feats, near = small(prepare_features_kernel, "prepare_features", feats + near, 2)(features, cotangent)
    rows, feats, near = lax.optimization_barrier((rows, feats, near))
    shape = (FR, 56, C)
    edges = small(
        col_edges_kernel,
        "col_edges",
        (jax.ShapeDtypeStruct(shape, f32),) * 2,
        4,
        [pltpu.VMEM((2,) + shape, f32)],
    )(features, near, *rows)
    edges, flow_feats = lax.optimization_barrier((edges, flow_feats))
    cols = [lax.ppermute(edges[k], WA, pairs(k)) for k in (1, 0)]
    taps = (jax.ShapeDtypeStruct((9, 2 * C, 2 * C), bf16),) * 2
    flows = (jax.ShapeDtypeStruct((2 * CF, R2 * W2), bf16),) * 2
    prepared = small(prepare_kernel, "prepare", taps + flows, 2)(kernel_one, flow_feats)
    cols, prepared = lax.optimization_barrier((cols, prepared))
    swap = [(0, 1), (1, 0)]
    taps, flows = prepared[:2], prepared[2:]
    keep, send, cot = flow_terms(*flows, near, *rows, *cols)
    terms_two = keep + lax.ppermute(send, "core", swap)
    grad_high, grad_low = block_gradient(features, *rows, *cols, *taps, cot)
    terms_two, grad_high, grad_low = lax.optimization_barrier((terms_two, grad_high, grad_low))
    arrived_two = spread(terms_two, ("x", "y"))
    keep, send = block_terms(*feats, grad_high, grad_low)
    terms_one = keep + lax.ppermute(send, "core", swap)
    arrived_one = spread(terms_one, ("x", "y"))
    terms_one, cot, kernel_two = lax.optimization_barrier((terms_one, cot, kernel_two))
    grad_flow = adjoint(flow_adjoint_kernel, "flow_adjoint", (FR, R2, W2, CF), cot, kernel_two)
    arrived_one, arrived_two, grad_flow = lax.optimization_barrier((arrived_one, arrived_two, grad_flow))
    parts = (jax.ShapeDtypeStruct((2, 7, 24, C), f32),) * 4
    parts = small(first_sum_kernel, "first_sum", parts, 8)(terms_one, *arrived_one, terms_two, *arrived_two)
    chunk = (jax.ShapeDtypeStruct((7, 24, C), f32),) * 2
    keep, send = small(second_sum_kernel, "second_sum", chunk, 4)(parts[0], *spread(parts, ("y", "x")))
    arrived = lax.ppermute(send, ("zl", "zh"), [(i, 7 - i) for i in range(8)])
    keep, grad_high, grad_low = lax.optimization_barrier((keep, grad_high, grad_low))
    grad_features = adjoint(
        feature_adjoint_kernel, "feature_adjoint", (FR, R, W, C), grad_high, grad_low, *taps
    )
    arrived, grad_features = lax.optimization_barrier((arrived, grad_features))
    chunk = keep + arrived
    chunk = summed(chunk, spread([chunk] * 4, "zl"))
    pieces = [chunk] + [lax.ppermute(chunk, "x", swaps(k)) for k in (1, 2, 3)]
    shares = tuple(jax.ShapeDtypeStruct((27, depth, C), f32) for depth in (8, 16))
    grad_one, grad_two = small(gather_kernel, "gather", shares, 4)(*pieces)
    grad_one = grad_one.reshape(3, 3, 3, 8, C)
    grad_two = grad_two.reshape(3, 3, 3, 16, C)
    return (grad_features, grad_one, grad_flow, grad_two)


def solution(mesh):
    fine = Mesh(mesh.devices.reshape(4, 4, 2, 4, 2), ("x", "zl", "zh", "y", "core"))
    grid = P(None, HA, WA, None)
    share = P(None, None, None, WA, None)
    return jax.shard_map(
        local,
        mesh=fine,
        in_specs=(grid, P(), grid, P(), grid),
        out_specs=(grid, share, grid, share),
        check_vma=False,
    )
```

```python
import functools

import jax
import jax.numpy as jnp
from jax import lax
from jax.experimental import pallas as pl
from jax.experimental.pallas import tpu as pltpu
from jax.sharding import Mesh
from jax.sharding import PartitionSpec as P

FR, R, W, C = 2, 16, 32, 128
R2, W2, CF = 8, 16, 256
PITCH = 40
EXT = (R + 2) * PITCH
COL = 20
HA, WA = ("x", "zl"), ("zh", "y", "core")

f32, bf16 = jnp.float32, jnp.bfloat16
VMEM = pl.BlockSpec(memory_space=pltpu.VMEM)
HBM = pl.BlockSpec(memory_space=pltpu.HBM)


def split(values):
    high = values.astype(bf16)
    return high, (values - high.astype(f32)).astype(bf16)


def dot(left, right, dims):
    return lax.dot_general(left, right, (dims, ((), ())), preferred_element_type=f32)


def product(left, right, dims):
    return dot(left[0], right[0], dims) + (dot(left[0], right[1], dims) + dot(left[1], right[0], dims))


def tall_product(left, right, dims):
    rows = left[0].shape[0]
    both = dot(jnp.concatenate(left, axis=0), right[0], dims)
    return both[:rows] + (both[rows:] + dot(left[0], right[1], dims))


NN = ((1,), (0,))
NT = ((1,), (1,))


def both_frames(kernel, tap):
    first = jnp.concatenate([kernel[9 + tap], kernel[tap]], axis=1)
    second = jnp.concatenate([kernel[18 + tap], kernel[9 + tap]], axis=1)
    return jnp.concatenate([first, second], axis=0)


def store_terms(keep_ref, send_ref, tap, value, depth):
    half = value.shape[0] // 2
    taps = (
        (0, value[:half, C:]),
        (1, value[:half, :C] + value[half:, C:]),
        (2, value[half:, :C]),
    )
    core, y, x, zh = [lax.axis_index(a) for a in ("core", "y", "x", "zh")]
    for time_tap, part in taps:
        number = 9 * time_tap + tap
        slot_x = x ^ (number // 7)
        for owner in range(8):
            slot_y = y ^ (owner % 4)
            slot_zh = zh ^ (owner // 4)
            slots = [jnp.where(core == 0, slot_x, slot_y), jnp.where(core == 0, slot_y, slot_x)]
            first = part[2 * owner * depth : (2 * owner + 1) * depth]
            second = part[(2 * owner + 1) * depth : (2 * owner + 2) * depth]
            keep_ref[slots[0], slots[1], slot_zh, number % 7] = jnp.where(core == 0, first, second)
            send_ref[slots[1], slots[0], slot_zh, number % 7] = jnp.where(core == 0, second, first)


def row_edges_kernel(
    feat_ref, cot_ref, first_ref, second_ref, feat_top, feat_bottom, cot_top, cot_bottom, sems
):
    copies = [
        pltpu.make_async_copy(feat_ref.at[:, 0:2], feat_top, sems.at[0]),
        pltpu.make_async_copy(feat_ref.at[:, R - 2 : R], feat_bottom, sems.at[1]),
        pltpu.make_async_copy(cot_ref.at[:, 0:1], cot_top, sems.at[2]),
        pltpu.make_async_copy(cot_ref.at[:, R2 - 1 : R2], cot_bottom, sems.at[3]),
    ]
    for copy in copies:
        copy.start()
    for copy in copies:
        copy.wait()
    odd = lax.rem(lax.axis_index("zl"), 2) == 1
    for t in range(FR):
        for row in range(2):
            top, bottom = feat_top[t, row], feat_bottom[t, row]
            lines = slice(row * W, (row + 1) * W)
            first_ref[t, lines] = jnp.where(odd, top, bottom)
            second_ref[t, lines] = jnp.where(odd, bottom, top)
        top, bottom = cot_top[t, 0], cot_bottom[t, 0]
        first_ref[t, 2 * W :] = jnp.where(odd, top, bottom)
        second_ref[t, 2 * W :] = jnp.where(odd, bottom, top)


def prepare_features_kernel(feat_ref, cot_ref, feat_high, feat_low, near_cot_ref):
    near_cot_ref[...] = cot_ref[...]
    for t in range(FR):
        lines = slice(t * C, (t + 1) * C)
        feat_high[lines], feat_low[lines] = split(feat_ref[t].reshape(R * W, C).T)


def prepare_kernel(weight_ref, flow_ref, taps_high, taps_low, flow_high, flow_low):
    for tap in range(9):
        taps_high[tap], taps_low[tap] = split(both_frames(weight_ref, tap))
    for t in range(FR):
        lines = slice(t * CF, (t + 1) * CF)
        flow_high[lines], flow_low[lines] = split(flow_ref[t].reshape(R2 * W2, CF).T)


def row_halo(first_ref, second_ref, t, lines):
    odd = lax.rem(lax.axis_index("zl"), 2) == 1
    first, second = first_ref[t, lines], second_ref[t, lines]
    return jnp.where(odd, first, second), jnp.where(odd, second, first)


def col_edges_kernel(feat_ref, cot_ref, row_second_ref, row_first_ref, first_ref, second_ref, edge_ref):
    for t in range(FR):
        halos = [row_halo(row_first_ref, row_second_ref, t, slice(r * W, (r + 1) * W)) for r in range(2)]
        for side, start in ((0, 0), (1, W - 2)):
            for col in range(2):
                at, place = start + col, col * COL
                for row in range(2):
                    edge_ref[side, t, place + row : place + row + 1] = halos[row][0][at : at + 1]
                    low = place + R + 2 + row
                    edge_ref[side, t, low : low + 1] = halos[row][1][at : at + 1]
                edge_ref[side, t, place + 2 : place + 2 + R] = feat_ref[t, :, at, :]
        above, below = row_halo(row_first_ref, row_second_ref, t, slice(2 * W, 2 * W + W2))
        for side, at in ((0, 0), (1, W2 - 1)):
            place = 2 * COL
            edge_ref[side, t, place : place + 1] = above[at : at + 1]
            edge_ref[side, t, place + 1 : place + 1 + R2] = cot_ref[t, :, at, :]
            edge_ref[side, t, place + 1 + R2 : place + 2 + R2] = below[at : at + 1]
    odd = lax.axis_index("core") == 1
    first_ref[...] = jnp.where(odd, edge_ref[0], edge_ref[1])
    second_ref[...] = jnp.where(odd, edge_ref[1], edge_ref[0])


def col_halo(first_ref, second_ref, t, lines):
    odd = lax.axis_index("core") == 1
    first, second = first_ref[t, lines], second_ref[t, lines]
    return jnp.where(odd, first, second), jnp.where(odd, second, first)


def shifted_cot(cot_ref, e):
    both = jnp.concatenate([cot_ref[0, :, e : e + W2, :], cot_ref[1, :, e : e + W2, :]], axis=-1)
    return split(both)


def flow_terms_kernel(
    flow_high, flow_low, local_ref, row_second_ref, row_first_ref, col_second_ref, col_first_ref,
    keep_ref, send_ref, cot_ref,
):
    for t in range(FR):
        above, below = row_halo(row_first_ref, row_second_ref, t, slice(2 * W, 2 * W + W2))
        cot_ref[t, 0, 1 : 1 + W2] = above
        cot_ref[t, 1 : 1 + R2, 1 : 1 + W2] = local_ref[t]
        cot_ref[t, 1 + R2, 1 : 1 + W2] = below
        lines = slice(2 * COL, 2 * COL + R2 + 2)
        left, right = col_halo(col_first_ref, col_second_ref, t, lines)
        cot_ref[t, :, 0] = left
        cot_ref[t, :, 1 + W2] = right
    flow = jnp.concatenate([flow_high[...], flow_high[...], flow_low[...]], axis=1)
    for col_tap in range(3):
        cot = shifted_cot(cot_ref, 2 - col_tap)
        for row_tap in range(3):
            window = [v[2 - row_tap : 2 - row_tap + R2].reshape(R2 * W2, 2 * C) for v in cot]
            window = jnp.concatenate([window[0], window[1], window[0]], axis=0)
            store_terms(keep_ref, send_ref, 3 * row_tap + col_tap, dot(flow, window, NN), 16)


def block_kernel(
    feat_ref, row_second_ref, row_first_ref, col_second_ref, col_first_ref,
    taps_high, taps_low, cot_ref, grad_high_ref, grad_low_ref,
    ext_ref, wide_ref, even_high, even_low, odd_high, odd_low, grad_ref,
):
    ext_ref[...] = jnp.zeros_like(ext_ref)
    for t in range(FR):
        lanes = slice(t * C, (t + 1) * C)
        ext_ref[2 : 2 + R, 3 : 3 + W, lanes] = feat_ref[t]
        for row in range(2):
            above, below = row_halo(row_first_ref, row_second_ref, t, slice(row * W, (row + 1) * W))
            ext_ref[row, 3 : 3 + W, lanes] = above
            ext_ref[R + 2 + row, 3 : 3 + W, lanes] = below
            place = slice(row * COL, row * COL + R + 4)
            left, right = col_halo(col_first_ref, col_second_ref, t, place)
            ext_ref[:, 1 + row, lanes] = left
            ext_ref[:, 3 + W + row, lanes] = right
    for t in range(FR):
        lanes = slice(t * C, (t + 1) * C)
        for row in range(R2 + 2):
            line = cot_ref[t, row] * 0.5
            for target in (2 * row - 1, 2 * row):
                if 0 <= target < R + 2:
                    wide_ref[t, target, pl.ds(0, W2 + 2, stride=2), :] = line
                    wide_ref[t, target, pl.ds(1, W2 + 2, stride=2), :] = line
    rows = R + 4
    for e in range(3):
        shifted = ext_ref[:, e : e + PITCH, :].reshape(rows * PITCH, 2 * C)
        high, low = split(shifted)
        even_high[e] = high
        even_low[e] = low
        odd_high[e] = high[PITCH : PITCH + EXT]
        odd_low[e] = low[PITCH : PITCH + EXT]
    step = EXT // 3
    for part in range(3):
        start = part * step
        total = jnp.zeros((step, 2 * C), f32)
        for row_tap in range(3):
            for e in range(3):
                if row_tap == 1:
                    window = (odd_high[e, start : start + step], odd_low[e, start : start + step])
                else:
                    first = start + row_tap * PITCH
                    window = (even_high[e, first : first + step], even_low[e, first : first + step])
                tap = 3 * row_tap + e
                total = total + product(window, (taps_high[tap], taps_low[tap]), NN)
        sigma = jax.nn.sigmoid(total)
        slope = sigma * (1.0 + total * (1.0 - sigma))
        lines = step // PITCH
        grad_ref[part * lines : (part + 1) * lines] = slope.reshape(lines, PITCH, 2 * C)
    for t in range(FR):
        lanes = slice(t * C, (t + 1) * C)
        grad_ref[:, :, lanes] = grad_ref[:, :, lanes] * wide_ref[t]
    for e in range(3):
        high, low = split(grad_ref[:, 3 - e : 3 - e + W, :])
        grad_high_ref[e] = high
        grad_low_ref[e] = low


def block_terms_kernel(feat_high, feat_low, grad_high_ref, grad_low_ref, keep_ref, send_ref):
    feat = feat_high[...], feat_low[...]
    for row_tap in range(3):
        for e in range(3):
            window = [
                ref[e, 2 - row_tap : 2 - row_tap + R].reshape(R * W, 2 * C)
                for ref in (grad_high_ref, grad_low_ref)
            ]
            store_terms(keep_ref, send_ref, 3 * row_tap + e, tall_product(feat, window, NN), 8)


def feature_adjoint_kernel(grad_high_ref, grad_low_ref, taps_high, taps_low, feat_out):
    total = jnp.zeros((R * W, 2 * C), f32)
    for row_tap in range(3):
        for e in range(3):
            window = [
                ref[e, 2 - row_tap : 2 - row_tap + R].reshape(R * W, 2 * C)
                for ref in (grad_high_ref, grad_low_ref)
            ]
            tap = 3 * row_tap + e
            total = total + tall_product(window, (taps_high[tap], taps_low[tap]), NT)
    for t in range(FR):
        feat_out[t] = total[:, t * C : (t + 1) * C].reshape(R, W, C)


def flow_adjoint_kernel(cot_ref, weight_two_ref, flow_out):
    total = jnp.zeros((R2 * W2, 2 * CF), f32)
    for e in range(3):
        cot = shifted_cot(cot_ref, 2 - e)
        for row_tap in range(3):
            window = [v[2 - row_tap : 2 - row_tap + R2].reshape(R2 * W2, 2 * C) for v in cot]
            total = total + tall_product(window, split(both_frames(weight_two_ref, 3 * row_tap + e)), NT)
    for t in range(FR):
        flow_out[t] = total[:, t * CF : (t + 1) * CF].reshape(R2, W2, CF)


def first_sum_kernel(*refs):
    ones, twos, outs = refs[:4], refs[4:8], refs[8:]
    for slot, out in enumerate(outs):
        for depth, parts in ((slice(0, 8), ones), (slice(8, 24), twos)):
            own, second, first, third = parts
            out[:, :, depth] = (own[0, slot] + second[slot]) + (first[slot] + third[slot])


def second_sum_kernel(own, second, first, third, keep, send):
    keep[...] = (own[0] + second[0]) + (first[0] + third[0])
    send[...] = (own[1] + second[1]) + (first[1] + third[1])


def gather_kernel(own_ref, one_ref, two_ref, three_ref, grad_one_ref, grad_two_ref):
    scale_one = 1.0 / (FR * R * W * 256) ** 0.5
    scale_two = 1.0 / (FR * R2 * W2 * 256) ** 0.5
    for k, ref in enumerate((own_ref, one_ref, two_ref, three_ref)):
        first = 7 * (lax.axis_index("x") ^ k)

        def put(j, ref=ref, first=first):
            grad_one_ref[first + j] = ref[j, :8] * scale_one
            grad_two_ref[first + j] = ref[j, 8:] * scale_two

        for j in range(6):
            put(j)
        pl.when(first < 21)(functools.partial(put, 6))


def params(mebibytes=24):
    return pltpu.CompilerParams(vmem_limit_bytes=mebibytes * 2**20)


def small(kernel, name, out_shape, count, scratch=(), space=VMEM):
    return pl.pallas_call(
        kernel,
        out_shape=out_shape,
        in_specs=[space] * count,
        out_specs=(VMEM,) * len(out_shape),
        scratch_shapes=scratch,
        compiler_params=params(24 if space is VMEM else 53),
        cost_estimate=pl.CostEstimate(flops=10**6, bytes_accessed=10**6, transcendentals=0),
        name=name,
    )


def flow_terms(*args):
    return pl.pallas_call(
        flow_terms_kernel,
        out_shape=(jax.ShapeDtypeStruct((4, 4, 2, 7, 16, C), f32),) * 2
        + (jax.ShapeDtypeStruct((FR, R2 + 2, W2 + 2, C), f32),),
        in_specs=[VMEM] * 7,
        out_specs=(VMEM,) * 3,
        compiler_params=params(),
        cost_estimate=pl.CostEstimate(flops=2 * 10**9, bytes_accessed=5 * 10**6, transcendentals=0),
        name="flow_terms",
    )(*args)


def block_gradient(*args):
    return pl.pallas_call(
        block_kernel,
        out_shape=(jax.ShapeDtypeStruct((3, R + 2, W, 2 * C), bf16),) * 2,
        in_specs=[VMEM] * 8,
        out_specs=(VMEM,) * 2,
        scratch_shapes=[
            pltpu.VMEM((R + 4, PITCH + 8, 2 * C), f32),
            pltpu.VMEM((FR, R + 2, PITCH, C), f32),
            pltpu.VMEM((3, (R + 4) * PITCH, 2 * C), bf16),
            pltpu.VMEM((3, (R + 4) * PITCH, 2 * C), bf16),
            pltpu.VMEM((3, EXT, 2 * C), bf16),
            pltpu.VMEM((3, EXT, 2 * C), bf16),
            pltpu.VMEM((R + 2, PITCH, 2 * C), f32),
        ],
        compiler_params=params(),
        cost_estimate=pl.CostEstimate(flops=5 * 10**9, bytes_accessed=6 * 10**6, transcendentals=200000),
        name="block_gradient",
    )(*args)


def block_terms(*args):
    return pl.pallas_call(
        block_terms_kernel,
        out_shape=(jax.ShapeDtypeStruct((4, 4, 2, 7, 8, C), f32),) * 2,
        in_specs=[VMEM] * 4,
        out_specs=(VMEM,) * 2,
        compiler_params=params(),
        cost_estimate=pl.CostEstimate(flops=10**9, bytes_accessed=10**6, transcendentals=0),
        name="block_terms",
    )(*args)


def adjoint(kernel, name, shape, *args):
    return pl.pallas_call(
        kernel,
        out_shape=jax.ShapeDtypeStruct(shape, f32),
        in_specs=[VMEM] * len(args),
        out_specs=VMEM,
        compiler_params=params(),
        cost_estimate=pl.CostEstimate(flops=2 * 10**9, bytes_accessed=5 * 10**6, transcendentals=0),
        name=name,
    )(*args)


def swaps(mask, count=4):
    return [(i, i ^ mask) for i in range(count)]


def crossed(mask, axes):
    both = []
    for x in range(4):
        for y in range(4):
            for core in range(2):
                x_to, y_to = (x ^ mask, y) if axes[core] == "x" else (x, y ^ mask)
                both.append((8 * x + 2 * y + core, 8 * x_to + 2 * y_to + core))
    return both


def pairs(start, count=16):
    return [p for i in range(start, count - 1, 2) for p in ((i, i + 1), (i + 1, i))]


def spread(parts, axes):
    if axes == "zl":
        return [lax.ppermute(parts[k], "zl", swaps(k)) for k in (3, 2, 1)]
    return [lax.ppermute(parts[k], ("x", "y", "core"), crossed(k, axes)) for k in (2, 1, 3)]


def summed(own, arrived):
    third, second, first = arrived
    return (own + first) + (second + third)


def local(features, weight_one, flow_feats, weight_two, cotangent):
    kernel_one = weight_one.reshape(27, C, C)
    kernel_two = weight_two.reshape(27, CF, C)
    edges = (jax.ShapeDtypeStruct((FR, 2 * W + W2, C), f32),) * 2
    edges = small(
        row_edges_kernel,
        "row_edges",
        edges,
        2,
        [pltpu.VMEM((FR, 2, W, C), f32)] * 2
        + [pltpu.VMEM((FR, 1, W2, C), f32)] * 2
        + [pltpu.SemaphoreType.DMA((4,))],
        HBM,
    )(features, cotangent)
    rows = [lax.ppermute(edges[k], HA, pairs(k)) for k in (1, 0)]
    feats = (jax.ShapeDtypeStruct((2 * C, R * W), bf16),) * 2
    near = (jax.ShapeDtypeStruct((FR, R2, W2, C), f32),)
    *feats, near = small(prepare_features_kernel, "prepare_features", feats + near, 2)(features, cotangent)
    rows, feats, near = lax.optimization_barrier((rows, feats, near))
    shape = (FR, 56, C)
    edges = small(
        col_edges_kernel,
        "col_edges",
        (jax.ShapeDtypeStruct(shape, f32),) * 2,
        4,
        [pltpu.VMEM((2,) + shape, f32)],
    )(features, near, *rows)
    edges, flow_feats = lax.optimization_barrier((edges, flow_feats))
    cols = [lax.ppermute(edges[k], WA, pairs(k)) for k in (1, 0)]
    taps = (jax.ShapeDtypeStruct((9, 2 * C, 2 * C), bf16),) * 2
    flows = (jax.ShapeDtypeStruct((2 * CF, R2 * W2), bf16),) * 2
    prepared = small(prepare_kernel, "prepare", taps + flows, 2)(kernel_one, flow_feats)
    cols, prepared = lax.optimization_barrier((cols, prepared))
    swap = [(0, 1), (1, 0)]
    taps, flows = prepared[:2], prepared[2:]
    keep, send, cot = flow_terms(*flows, near, *rows, *cols)
    terms_two = keep + lax.ppermute(send, "core", swap)
    grad_high, grad_low = block_gradient(features, *rows, *cols, *taps, cot)
    terms_two, grad_high, grad_low = lax.optimization_barrier((terms_two, grad_high, grad_low))
    arrived_two = spread(terms_two, ("x", "y"))
    keep, send = block_terms(*feats, grad_high, grad_low)
    terms_one = keep + lax.ppermute(send, "core", swap)
    arrived_one = spread(terms_one, ("x", "y"))
    terms_one, cot, kernel_two = lax.optimization_barrier((terms_one, cot, kernel_two))
    grad_flow = adjoint(flow_adjoint_kernel, "flow_adjoint", (FR, R2, W2, CF), cot, kernel_two)
    arrived_one, arrived_two, grad_flow = lax.optimization_barrier((arrived_one, arrived_two, grad_flow))
    parts = (jax.ShapeDtypeStruct((2, 7, 24, C), f32),) * 4
    parts = small(first_sum_kernel, "first_sum", parts, 8)(terms_one, *arrived_one, terms_two, *arrived_two)
    chunk = (jax.ShapeDtypeStruct((7, 24, C), f32),) * 2
    keep, send = small(second_sum_kernel, "second_sum", chunk, 4)(parts[0], *spread(parts, ("y", "x")))
    arrived = lax.ppermute(send, ("zl", "zh"), [(i, 7 - i) for i in range(8)])
    keep, grad_high, grad_low = lax.optimization_barrier((keep, grad_high, grad_low))
    grad_features = adjoint(
        feature_adjoint_kernel, "feature_adjoint", (FR, R, W, C), grad_high, grad_low, *taps
    )
    arrived, grad_features = lax.optimization_barrier((arrived, grad_features))
    chunk = keep + arrived
    chunk = summed(chunk, spread([chunk] * 4, "zl"))
    pieces = [chunk] + [lax.ppermute(chunk, "x", swaps(k)) for k in (1, 2, 3)]
    shares = tuple(jax.ShapeDtypeStruct((27, depth, C), f32) for depth in (8, 16))
    grad_one, grad_two = small(gather_kernel, "gather", shares, 4)(*pieces)
    grad_one = grad_one.reshape(3, 3, 3, 8, C)
    grad_two = grad_two.reshape(3, 3, 3, 16, C)
    return (grad_features, grad_one, grad_flow, grad_two)


def solution(mesh):
    fine = Mesh(mesh.devices.reshape(4, 4, 2, 4, 2), ("x", "zl", "zh", "y", "core"))
    grid = P(None, HA, WA, None)
    share = P(None, None, None, WA, None)
    return jax.shard_map(
        local,
        mesh=fine,
        in_specs=(grid, P(), grid, P(), grid),
        out_specs=(grid, share, grid, share),
        check_vma=False,
    )
```

```python
import functools

import jax
import jax.numpy as jnp
from jax import lax
from jax.experimental import pallas as pl
from jax.experimental.pallas import tpu as pltpu
from jax.sharding import Mesh
from jax.sharding import PartitionSpec as P

FR, R, W, C = 2, 16, 32, 128
R2, W2, CF = 8, 16, 256
PITCH = 40
EXT = (R + 2) * PITCH
COL = 20
HA, WA = ("x", "zl"), ("zh", "y", "core")

f32, bf16 = jnp.float32, jnp.bfloat16
VMEM = pl.BlockSpec(memory_space=pltpu.VMEM)
HBM = pl.BlockSpec(memory_space=pltpu.HBM)


def split(values):
    high = values.astype(bf16)
    return high, (values - high.astype(f32)).astype(bf16)


def dot(left, right, dims):
    return lax.dot_general(left, right, (dims, ((), ())), preferred_element_type=f32)


def product(left, right, dims):
    return dot(left[0], right[0], dims) + (dot(left[0], right[1], dims) + dot(left[1], right[0], dims))


def tall_product(left, right, dims):
    rows = left[0].shape[0]
    both = dot(jnp.concatenate(left, axis=0), right[0], dims)
    return both[:rows] + (both[rows:] + dot(left[0], right[1], dims))


NN = ((1,), (0,))
NT = ((1,), (1,))


def both_frames(kernel, tap):
    first = jnp.concatenate([kernel[9 + tap], kernel[tap]], axis=1)
    second = jnp.concatenate([kernel[18 + tap], kernel[9 + tap]], axis=1)
    return jnp.concatenate([first, second], axis=0)


def store_terms(keep_ref, send_ref, tap, value, depth):
    half = value.shape[0] // 2
    taps = (
        (0, value[:half, C:]),
        (1, value[:half, :C] + value[half:, C:]),
        (2, value[half:, :C]),
    )
    core, y, x, zh = [lax.axis_index(a) for a in ("core", "y", "x", "zh")]
    for time_tap, part in taps:
        number = 9 * time_tap + tap
        slot_x = x ^ (number // 7)
        for owner in range(8):
            slot_y = y ^ (owner % 4)
            slot_zh = zh ^ (owner // 4)
            slots = [jnp.where(core == 0, slot_x, slot_y), jnp.where(core == 0, slot_y, slot_x)]
            first = part[2 * owner * depth : (2 * owner + 1) * depth]
            second = part[(2 * owner + 1) * depth : (2 * owner + 2) * depth]
            keep_ref[slots[0], slots[1], slot_zh, number % 7] = jnp.where(core == 0, first, second)
            send_ref[slots[1], slots[0], slot_zh, number % 7] = jnp.where(core == 0, second, first)


def row_edges_kernel(
    feat_ref, cot_ref, first_ref, second_ref, feat_top, feat_bottom, cot_top, cot_bottom, sems
):
    copies = [
        pltpu.make_async_copy(feat_ref.at[:, 0:2], feat_top, sems.at[0]),
        pltpu.make_async_copy(feat_ref.at[:, R - 2 : R], feat_bottom, sems.at[1]),
        pltpu.make_async_copy(cot_ref.at[:, 0:1], cot_top, sems.at[2]),
        pltpu.make_async_copy(cot_ref.at[:, R2 - 1 : R2], cot_bottom, sems.at[3]),
    ]
    for copy in copies:
        copy.start()
    for copy in copies:
        copy.wait()
    odd = lax.rem(lax.axis_index("zl"), 2) == 1
    for t in range(FR):
        for row in range(2):
            top, bottom = feat_top[t, row], feat_bottom[t, row]
            lines = slice(row * W, (row + 1) * W)
            first_ref[t, lines] = jnp.where(odd, top, bottom)
            second_ref[t, lines] = jnp.where(odd, bottom, top)
        top, bottom = cot_top[t, 0], cot_bottom[t, 0]
        first_ref[t, 2 * W :] = jnp.where(odd, top, bottom)
        second_ref[t, 2 * W :] = jnp.where(odd, bottom, top)


def prepare_features_kernel(feat_ref, cot_ref, feat_high, feat_low, near_cot_ref):
    near_cot_ref[...] = cot_ref[...]
    for t in range(FR):
        lines = slice(t * C, (t + 1) * C)
        feat_high[lines], feat_low[lines] = split(feat_ref[t].reshape(R * W, C).T)


def prepare_kernel(weight_ref, flow_ref, taps_high, taps_low, flow_high, flow_low):
    for tap in range(9):
        taps_high[tap], taps_low[tap] = split(both_frames(weight_ref, tap))
    for t in range(FR):
        lines = slice(t * CF, (t + 1) * CF)
        flow_high[lines], flow_low[lines] = split(flow_ref[t].reshape(R2 * W2, CF).T)


def row_halo(first_ref, second_ref, t, lines):
    odd = lax.rem(lax.axis_index("zl"), 2) == 1
    first, second = first_ref[t, lines], second_ref[t, lines]
    return jnp.where(odd, first, second), jnp.where(odd, second, first)


def col_edges_kernel(feat_ref, cot_ref, row_second_ref, row_first_ref, first_ref, second_ref, edge_ref):
    for t in range(FR):
        halos = [row_halo(row_first_ref, row_second_ref, t, slice(r * W, (r + 1) * W)) for r in range(2)]
        for side, start in ((0, 0), (1, W - 2)):
            for col in range(2):
                at, place = start + col, col * COL
                for row in range(2):
                    edge_ref[side, t, place + row : place + row + 1] = halos[row][0][at : at + 1]
                    low = place + R + 2 + row
                    edge_ref[side, t, low : low + 1] = halos[row][1][at : at + 1]
                edge_ref[side, t, place + 2 : place + 2 + R] = feat_ref[t, :, at, :]
        above, below = row_halo(row_first_ref, row_second_ref, t, slice(2 * W, 2 * W + W2))
        for side, at in ((0, 0), (1, W2 - 1)):
            place = 2 * COL
            edge_ref[side, t, place : place + 1] = above[at : at + 1]
            edge_ref[side, t, place + 1 : place + 1 + R2] = cot_ref[t, :, at, :]
            edge_ref[side, t, place + 1 + R2 : place + 2 + R2] = below[at : at + 1]
    odd = lax.axis_index("core") == 1
    first_ref[...] = jnp.where(odd, edge_ref[0], edge_ref[1])
    second_ref[...] = jnp.where(odd, edge_ref[1], edge_ref[0])


def col_halo(first_ref, second_ref, t, lines):
    odd = lax.axis_index("core") == 1
    first, second = first_ref[t, lines], second_ref[t, lines]
    return jnp.where(odd, first, second), jnp.where(odd, second, first)


def shifted_cot(cot_ref, e):
    both = jnp.concatenate([cot_ref[0, :, e : e + W2, :], cot_ref[1, :, e : e + W2, :]], axis=-1)
    return split(both)


def flow_terms_kernel(
    flow_high, flow_low, local_ref, row_second_ref, row_first_ref, col_second_ref, col_first_ref,
    keep_ref, send_ref, cot_ref,
):
    for t in range(FR):
        above, below = row_halo(row_first_ref, row_second_ref, t, slice(2 * W, 2 * W + W2))
        cot_ref[t, 0, 1 : 1 + W2] = above
        cot_ref[t, 1 : 1 + R2, 1 : 1 + W2] = local_ref[t]
        cot_ref[t, 1 + R2, 1 : 1 + W2] = below
        lines = slice(2 * COL, 2 * COL + R2 + 2)
        left, right = col_halo(col_first_ref, col_second_ref, t, lines)
        cot_ref[t, :, 0] = left
        cot_ref[t, :, 1 + W2] = right
    flow = jnp.concatenate([flow_high[...], flow_high[...], flow_low[...]], axis=1)
    for col_tap in range(3):
        cot = shifted_cot(cot_ref, 2 - col_tap)
        for row_tap in range(3):
            window = [v[2 - row_tap : 2 - row_tap + R2].reshape(R2 * W2, 2 * C) for v in cot]
            window = jnp.concatenate([window[0], window[1], window[0]], axis=0)
            store_terms(keep_ref, send_ref, 3 * row_tap + col_tap, dot(flow, window, NN), 16)


def block_kernel(
    feat_ref, row_second_ref, row_first_ref, col_second_ref, col_first_ref,
    taps_high, taps_low, cot_ref, grad_high_ref, grad_low_ref,
    ext_ref, wide_ref, even_high, even_low, odd_high, odd_low, grad_ref,
):
    ext_ref[...] = jnp.zeros_like(ext_ref)
    for t in range(FR):
        lanes = slice(t * C, (t + 1) * C)
        ext_ref[2 : 2 + R, 3 : 3 + W, lanes] = feat_ref[t]
        for row in range(2):
            above, below = row_halo(row_first_ref, row_second_ref, t, slice(row * W, (row + 1) * W))
            ext_ref[row, 3 : 3 + W, lanes] = above
            ext_ref[R + 2 + row, 3 : 3 + W, lanes] = below
            place = slice(row * COL, row * COL + R + 4)
            left, right = col_halo(col_first_ref, col_second_ref, t, place)
            ext_ref[:, 1 + row, lanes] = left
            ext_ref[:, 3 + W + row, lanes] = right
    for t in range(FR):
        lanes = slice(t * C, (t + 1) * C)
        for row in range(R2 + 2):
            line = cot_ref[t, row] * 0.5
            for target in (2 * row - 1, 2 * row):
                if 0 <= target < R + 2:
                    wide_ref[t, target, pl.ds(0, W2 + 2, stride=2), :] = line
                    wide_ref[t, target, pl.ds(1, W2 + 2, stride=2), :] = line
    rows = R + 4
    for e in range(3):
        shifted = ext_ref[:, e : e + PITCH, :].reshape(rows * PITCH, 2 * C)
        high, low = split(shifted)
        even_high[e] = high
        even_low[e] = low
        odd_high[e] = high[PITCH : PITCH + EXT]
        odd_low[e] = low[PITCH : PITCH + EXT]
    step = EXT // 3
    for part in range(3):
        start = part * step
        total = jnp.zeros((step, 2 * C), f32)
        for row_tap in range(3):
            for e in range(3):
                if row_tap == 1:
                    window = (odd_high[e, start : start + step], odd_low[e, start : start + step])
                else:
                    first = start + row_tap * PITCH
                    window = (even_high[e, first : first + step], even_low[e, first : first + step])
                tap = 3 * row_tap + e
                total = total + product(window, (taps_high[tap], taps_low[tap]), NN)
        sigma = jax.nn.sigmoid(total)
        slope = sigma * (1.0 + total * (1.0 - sigma))
        lines = step // PITCH
        grad_ref[part * lines : (part + 1) * lines] = slope.reshape(lines, PITCH, 2 * C)
    for t in range(FR):
        lanes = slice(t * C, (t + 1) * C)
        grad_ref[:, :, lanes] = grad_ref[:, :, lanes] * wide_ref[t]
    for e in range(3):
        high, low = split(grad_ref[:, 3 - e : 3 - e + W, :])
        grad_high_ref[e] = high
        grad_low_ref[e] = low


def block_terms_kernel(feat_high, feat_low, grad_high_ref, grad_low_ref, keep_ref, send_ref):
    feat = feat_high[...], feat_low[...]
    for row_tap in range(3):
        for e in range(3):
            window = [
                ref[e, 2 - row_tap : 2 - row_tap + R].reshape(R * W, 2 * C)
                for ref in (grad_high_ref, grad_low_ref)
            ]
            store_terms(keep_ref, send_ref, 3 * row_tap + e, tall_product(feat, window, NN), 8)


def feature_adjoint_kernel(grad_high_ref, grad_low_ref, taps_high, taps_low, feat_out):
    total = jnp.zeros((R * W, 2 * C), f32)
    for row_tap in range(3):
        for e in range(3):
            window = [
                ref[e, 2 - row_tap : 2 - row_tap + R].reshape(R * W, 2 * C)
                for ref in (grad_high_ref, grad_low_ref)
            ]
            tap = 3 * row_tap + e
            total = total + tall_product(window, (taps_high[tap], taps_low[tap]), NT)
    for t in range(FR):
        feat_out[t] = total[:, t * C : (t + 1) * C].reshape(R, W, C)


def flow_adjoint_kernel(cot_ref, weight_two_ref, flow_out):
    total = jnp.zeros((R2 * W2, 2 * CF), f32)
    for e in range(3):
        cot = shifted_cot(cot_ref, 2 - e)
        for row_tap in range(3):
            window = [v[2 - row_tap : 2 - row_tap + R2].reshape(R2 * W2, 2 * C) for v in cot]
            total = total + tall_product(window, split(both_frames(weight_two_ref, 3 * row_tap + e)), NT)
    for t in range(FR):
        flow_out[t] = total[:, t * CF : (t + 1) * CF].reshape(R2, W2, CF)


def first_sum_kernel(*refs):
    ones, twos, outs = refs[:4], refs[4:8], refs[8:]
    for slot, out in enumerate(outs):
        for depth, parts in ((slice(0, 8), ones), (slice(8, 24), twos)):
            own, second, first, third = parts
            out[:, :, depth] = (own[0, slot] + second[slot]) + (first[slot] + third[slot])


def second_sum_kernel(own, second, first, third, keep, send):
    keep[...] = (own[0] + second[0]) + (first[0] + third[0])
    send[...] = (own[1] + second[1]) + (first[1] + third[1])


def gather_kernel(own_ref, two_ref, one_ref, three_ref, grad_one_ref, grad_two_ref):
    scale_one = 1.0 / (FR * R * W * 256) ** 0.5
    scale_two = 1.0 / (FR * R2 * W2 * 256) ** 0.5
    for k, ref in enumerate((own_ref, one_ref, two_ref, three_ref)):
        first = 7 * (lax.axis_index("x") ^ k)

        def put(j, ref=ref, first=first):
            grad_one_ref[first + j] = ref[j, :8] * scale_one
            grad_two_ref[first + j] = ref[j, 8:] * scale_two

        for j in range(6):
            put(j)
        pl.when(first < 21)(functools.partial(put, 6))


def params(mebibytes=24):
    return pltpu.CompilerParams(vmem_limit_bytes=mebibytes * 2**20)


def small(kernel, name, out_shape, count, scratch=(), space=VMEM):
    return pl.pallas_call(
        kernel,
        out_shape=out_shape,
        in_specs=[space] * count,
        out_specs=(VMEM,) * len(out_shape),
        scratch_shapes=scratch,
        compiler_params=params(24 if space is VMEM else 64),
        cost_estimate=pl.CostEstimate(flops=10**6, bytes_accessed=10**6, transcendentals=0),
        name=name,
    )


def flow_terms(*args):
    return pl.pallas_call(
        flow_terms_kernel,
        out_shape=(jax.ShapeDtypeStruct((4, 4, 2, 7, 16, C), f32),) * 2
        + (jax.ShapeDtypeStruct((FR, R2 + 2, W2 + 2, C), f32),),
        in_specs=[VMEM] * 7,
        out_specs=(VMEM,) * 3,
        compiler_params=params(),
        cost_estimate=pl.CostEstimate(flops=2 * 10**9, bytes_accessed=5 * 10**6, transcendentals=0),
        name="flow_terms",
    )(*args)


def block_gradient(*args):
    return pl.pallas_call(
        block_kernel,
        out_shape=(jax.ShapeDtypeStruct((3, R + 2, W, 2 * C), bf16),) * 2,
        in_specs=[VMEM] * 8,
        out_specs=(VMEM,) * 2,
        scratch_shapes=[
            pltpu.VMEM((R + 4, PITCH + 8, 2 * C), f32),
            pltpu.VMEM((FR, R + 2, PITCH, C), f32),
            pltpu.VMEM((3, (R + 4) * PITCH, 2 * C), bf16),
            pltpu.VMEM((3, (R + 4) * PITCH, 2 * C), bf16),
            pltpu.VMEM((3, EXT, 2 * C), bf16),
            pltpu.VMEM((3, EXT, 2 * C), bf16),
            pltpu.VMEM((R + 2, PITCH, 2 * C), f32),
        ],
        compiler_params=params(),
        cost_estimate=pl.CostEstimate(flops=5 * 10**9, bytes_accessed=6 * 10**6, transcendentals=200000),
        name="block_gradient",
    )(*args)


def block_terms(*args):
    return pl.pallas_call(
        block_terms_kernel,
        out_shape=(jax.ShapeDtypeStruct((4, 4, 2, 7, 8, C), f32),) * 2,
        in_specs=[VMEM] * 4,
        out_specs=(VMEM,) * 2,
        compiler_params=params(),
        cost_estimate=pl.CostEstimate(flops=10**9, bytes_accessed=10**6, transcendentals=0),
        name="block_terms",
    )(*args)


def adjoint(kernel, name, shape, *args):
    return pl.pallas_call(
        kernel,
        out_shape=jax.ShapeDtypeStruct(shape, f32),
        in_specs=[VMEM] * len(args),
        out_specs=VMEM,
        compiler_params=params(),
        cost_estimate=pl.CostEstimate(flops=2 * 10**9, bytes_accessed=5 * 10**6, transcendentals=0),
        name=name,
    )(*args)


def swaps(mask, count=4):
    return [(i, i ^ mask) for i in range(count)]


def crossed(mask, axes):
    both = []
    for x in range(4):
        for y in range(4):
            for core in range(2):
                x_to, y_to = (x ^ mask, y) if axes[core] == "x" else (x, y ^ mask)
                both.append((8 * x + 2 * y + core, 8 * x_to + 2 * y_to + core))
    return both


def pairs(start, count=16):
    return [p for i in range(start, count - 1, 2) for p in ((i, i + 1), (i + 1, i))]


def spread(parts, axes):
    if axes == "zl":
        return [lax.ppermute(parts[k], "zl", swaps(k)) for k in (3, 2, 1)]
    return [lax.ppermute(parts[k], ("x", "y", "core"), crossed(k, axes)) for k in (2, 1, 3)]


def summed(own, arrived):
    third, second, first = arrived
    return (own + first) + (second + third)


def local(features, weight_one, flow_feats, weight_two, cotangent):
    kernel_one = weight_one.reshape(27, C, C)
    kernel_two = weight_two.reshape(27, CF, C)
    edges = (jax.ShapeDtypeStruct((FR, 2 * W + W2, C), f32),) * 2
    edges = small(
        row_edges_kernel,
        "row_edges",
        edges,
        2,
        [pltpu.VMEM((FR, 2, W, C), f32)] * 2
        + [pltpu.VMEM((FR, 1, W2, C), f32)] * 2
        + [pltpu.SemaphoreType.DMA((4,))],
        HBM,
    )(features, cotangent)
    rows = [lax.ppermute(edges[k], HA, pairs(k)) for k in (1, 0)]
    feats = (jax.ShapeDtypeStruct((2 * C, R * W), bf16),) * 2
    near = (jax.ShapeDtypeStruct((FR, R2, W2, C), f32),)
    *feats, near = small(prepare_features_kernel, "prepare_features", feats + near, 2)(features, cotangent)
    rows, feats, near = lax.optimization_barrier((rows, feats, near))
    shape = (FR, 56, C)
    edges = small(
        col_edges_kernel,
        "col_edges",
        (jax.ShapeDtypeStruct(shape, f32),) * 2,
        4,
        [pltpu.VMEM((2,) + shape, f32)],
    )(features, near, *rows)
    edges, flow_feats = lax.optimization_barrier((edges, flow_feats))
    cols = [lax.ppermute(edges[k], WA, pairs(k)) for k in (1, 0)]
    taps = (jax.ShapeDtypeStruct((9, 2 * C, 2 * C), bf16),) * 2
    flows = (jax.ShapeDtypeStruct((2 * CF, R2 * W2), bf16),) * 2
    prepared = small(prepare_kernel, "prepare", taps + flows, 2)(kernel_one, flow_feats)
    cols, prepared = lax.optimization_barrier((cols, prepared))
    swap = [(0, 1), (1, 0)]
    taps, flows = prepared[:2], prepared[2:]
    keep, send, cot = flow_terms(*flows, near, *rows, *cols)
    terms_two = keep + lax.ppermute(send, "core", swap)
    grad_high, grad_low = block_gradient(features, *rows, *cols, *taps, cot)
    terms_two, grad_high, grad_low = lax.optimization_barrier((terms_two, grad_high, grad_low))
    arrived_two = spread(terms_two, ("x", "y"))
    keep, send = block_terms(*feats, grad_high, grad_low)
    terms_one = keep + lax.ppermute(send, "core", swap)
    arrived_one = spread(terms_one, ("x", "y"))
    terms_one, cot, kernel_two = lax.optimization_barrier((terms_one, cot, kernel_two))
    grad_flow = adjoint(flow_adjoint_kernel, "flow_adjoint", (FR, R2, W2, CF), cot, kernel_two)
    arrived_one, arrived_two, grad_flow = lax.optimization_barrier((arrived_one, arrived_two, grad_flow))
    parts = (jax.ShapeDtypeStruct((2, 7, 24, C), f32),) * 4
    parts = small(first_sum_kernel, "first_sum", parts, 8)(terms_one, *arrived_one, terms_two, *arrived_two)
    chunk = (jax.ShapeDtypeStruct((7, 24, C), f32),) * 2
    keep, send = small(second_sum_kernel, "second_sum", chunk, 4)(parts[0], *spread(parts, ("y", "x")))
    arrived = lax.ppermute(send, ("zl", "zh"), [(i, 7 - i) for i in range(8)])
    keep, grad_high, grad_low = lax.optimization_barrier((keep, grad_high, grad_low))
    grad_features = adjoint(
        feature_adjoint_kernel, "feature_adjoint", (FR, R, W, C), grad_high, grad_low, *taps
    )
    arrived, grad_features = lax.optimization_barrier((arrived, grad_features))
    chunk = keep + arrived
    chunk = summed(chunk, spread([chunk] * 4, "zl"))
    pieces = [chunk] + [lax.ppermute(chunk, "x", swaps(k)) for k in (2, 1, 3)]
    shares = tuple(jax.ShapeDtypeStruct((27, depth, C), f32) for depth in (8, 16))
    grad_one, grad_two = small(gather_kernel, "gather", shares, 4)(*pieces)
    grad_one = grad_one.reshape(3, 3, 3, 8, C)
    grad_two = grad_two.reshape(3, 3, 3, 16, C)
    return (grad_features, grad_one, grad_flow, grad_two)


def solution(mesh):
    fine = Mesh(mesh.devices.reshape(4, 4, 2, 4, 2), ("x", "zl", "zh", "y", "core"))
    grid = P(None, HA, WA, None)
    share = P(None, None, None, WA, None)
    return jax.shard_map(
        local,
        mesh=fine,
        in_specs=(grid, P(), grid, P(), grid),
        out_specs=(grid, share, grid, share),
        check_vma=False,
    )
```

```python
import functools

import jax
import jax.numpy as jnp
from jax import lax
from jax.experimental import pallas as pl
from jax.experimental.pallas import tpu as pltpu
from jax.sharding import Mesh
from jax.sharding import PartitionSpec as P

FR, R, W, C = 2, 16, 32, 128
R2, W2, CF = 8, 16, 256
PITCH = 40
EXT = (R + 2) * PITCH
COL = 20
HA, WA = ("x", "zl"), ("zh", "y", "core")

f32, bf16 = jnp.float32, jnp.bfloat16
VMEM = pl.BlockSpec(memory_space=pltpu.VMEM)
HBM = pl.BlockSpec(memory_space=pltpu.HBM)


def split(values):
    high = values.astype(bf16)
    return high, (values - high.astype(f32)).astype(bf16)


def dot(left, right, dims):
    return lax.dot_general(left, right, (dims, ((), ())), preferred_element_type=f32)


def product(left, right, dims):
    return dot(left[0], right[0], dims) + (dot(left[0], right[1], dims) + dot(left[1], right[0], dims))


def tall_product(left, right, dims):
    rows = left[0].shape[0]
    both = dot(jnp.concatenate(left, axis=0), right[0], dims)
    return both[:rows] + (both[rows:] + dot(left[0], right[1], dims))


NN = ((1,), (0,))
NT = ((1,), (1,))


def both_frames(kernel, tap):
    first = jnp.concatenate([kernel[9 + tap], kernel[tap]], axis=1)
    second = jnp.concatenate([kernel[18 + tap], kernel[9 + tap]], axis=1)
    return jnp.concatenate([first, second], axis=0)


def store_terms(keep_ref, send_ref, tap, value, depth):
    half = value.shape[0] // 2
    taps = (
        (0, value[:half, C:]),
        (1, value[:half, :C] + value[half:, C:]),
        (2, value[half:, :C]),
    )
    core, y, x, zh = [lax.axis_index(a) for a in ("core", "y", "x", "zh")]
    for time_tap, part in taps:
        number = 9 * time_tap + tap
        slot_x = x ^ (number // 7)
        for owner in range(8):
            slot_y = y ^ (owner % 4)
            slot_zh = zh ^ (owner // 4)
            slots = [jnp.where(core == 1, slot_x, slot_y), jnp.where(core == 1, slot_y, slot_x)]
            first = part[2 * owner * depth : (2 * owner + 1) * depth]
            second = part[(2 * owner + 1) * depth : (2 * owner + 2) * depth]
            keep_ref[slots[0], slots[1], slot_zh, number % 7] = jnp.where(core == 0, first, second)
            send_ref[slots[1], slots[0], slot_zh, number % 7] = jnp.where(core == 0, second, first)


def row_edges_kernel(
    feat_ref, cot_ref, first_ref, second_ref, feat_top, feat_bottom, cot_top, cot_bottom, sems
):
    copies = [
        pltpu.make_async_copy(feat_ref.at[:, 0:2], feat_top, sems.at[0]),
        pltpu.make_async_copy(feat_ref.at[:, R - 2 : R], feat_bottom, sems.at[1]),
        pltpu.make_async_copy(cot_ref.at[:, 0:1], cot_top, sems.at[2]),
        pltpu.make_async_copy(cot_ref.at[:, R2 - 1 : R2], cot_bottom, sems.at[3]),
    ]
    for copy in copies:
        copy.start()
    for copy in copies:
        copy.wait()
    odd = lax.rem(lax.axis_index("zl"), 2) == 1
    for t in range(FR):
        for row in range(2):
            top, bottom = feat_top[t, row], feat_bottom[t, row]
            lines = slice(row * W, (row + 1) * W)
            first_ref[t, lines] = jnp.where(odd, top, bottom)
            second_ref[t, lines] = jnp.where(odd, bottom, top)
        top, bottom = cot_top[t, 0], cot_bottom[t, 0]
        first_ref[t, 2 * W :] = jnp.where(odd, top, bottom)
        second_ref[t, 2 * W :] = jnp.where(odd, bottom, top)


def prepare_features_kernel(feat_ref, cot_ref, feat_high, feat_low, near_cot_ref):
    near_cot_ref[...] = cot_ref[...]
    for t in range(FR):
        lines = slice(t * C, (t + 1) * C)
        feat_high[lines], feat_low[lines] = split(feat_ref[t].reshape(R * W, C).T)


def prepare_kernel(weight_ref, flow_ref, taps_high, taps_low, flow_high, flow_low):
    for tap in range(9):
        taps_high[tap], taps_low[tap] = split(both_frames(weight_ref, tap))
    for t in range(FR):
        lines = slice(t * CF, (t + 1) * CF)
        flow_high[lines], flow_low[lines] = split(flow_ref[t].reshape(R2 * W2, CF).T)


def row_halo(first_ref, second_ref, t, lines):
    odd = lax.rem(lax.axis_index("zl"), 2) == 1
    first, second = first_ref[t, lines], second_ref[t, lines]
    return jnp.where(odd, first, second), jnp.where(odd, second, first)


def col_edges_kernel(feat_ref, cot_ref, row_second_ref, row_first_ref, first_ref, second_ref, edge_ref):
    for t in range(FR):
        halos = [row_halo(row_first_ref, row_second_ref, t, slice(r * W, (r + 1) * W)) for r in range(2)]
        for side, start in ((0, 0), (1, W - 2)):
            for col in range(2):
                at, place = start + col, col * COL
                for row in range(2):
                    edge_ref[side, t, place + row : place + row + 1] = halos[row][0][at : at + 1]
                    low = place + R + 2 + row
                    edge_ref[side, t, low : low + 1] = halos[row][1][at : at + 1]
                edge_ref[side, t, place + 2 : place + 2 + R] = feat_ref[t, :, at, :]
        above, below = row_halo(row_first_ref, row_second_ref, t, slice(2 * W, 2 * W + W2))
        for side, at in ((0, 0), (1, W2 - 1)):
            place = 2 * COL
            edge_ref[side, t, place : place + 1] = above[at : at + 1]
            edge_ref[side, t, place + 1 : place + 1 + R2] = cot_ref[t, :, at, :]
            edge_ref[side, t, place + 1 + R2 : place + 2 + R2] = below[at : at + 1]
    odd = lax.axis_index("core") == 1
    first_ref[...] = jnp.where(odd, edge_ref[0], edge_ref[1])
    second_ref[...] = jnp.where(odd, edge_ref[1], edge_ref[0])


def col_halo(first_ref, second_ref, t, lines):
    odd = lax.axis_index("core") == 1
    first, second = first_ref[t, lines], second_ref[t, lines]
    return jnp.where(odd, first, second), jnp.where(odd, second, first)


def shifted_cot(cot_ref, e):
    both = jnp.concatenate([cot_ref[0, :, e : e + W2, :], cot_ref[1, :, e : e + W2, :]], axis=-1)
    return split(both)


def flow_terms_kernel(
    flow_high, flow_low, local_ref, row_second_ref, row_first_ref, col_second_ref, col_first_ref,
    keep_ref, send_ref, cot_ref,
):
    for t in range(FR):
        above, below = row_halo(row_first_ref, row_second_ref, t, slice(2 * W, 2 * W + W2))
        cot_ref[t, 0, 1 : 1 + W2] = above
        cot_ref[t, 1 : 1 + R2, 1 : 1 + W2] = local_ref[t]
        cot_ref[t, 1 + R2, 1 : 1 + W2] = below
        lines = slice(2 * COL, 2 * COL + R2 + 2)
        left, right = col_halo(col_first_ref, col_second_ref, t, lines)
        cot_ref[t, :, 0] = left
        cot_ref[t, :, 1 + W2] = right
    flow = jnp.concatenate([flow_high[...], flow_high[...], flow_low[...]], axis=1)
    for col_tap in range(3):
        cot = shifted_cot(cot_ref, 2 - col_tap)
        for row_tap in range(3):
            window = [v[2 - row_tap : 2 - row_tap + R2].reshape(R2 * W2, 2 * C) for v in cot]
            window = jnp.concatenate([window[0], window[1], window[0]], axis=0)
            store_terms(keep_ref, send_ref, 3 * row_tap + col_tap, dot(flow, window, NN), 16)


def block_kernel(
    feat_ref, row_second_ref, row_first_ref, col_second_ref, col_first_ref,
    taps_high, taps_low, cot_ref, grad_high_ref, grad_low_ref,
    ext_ref, wide_ref, even_high, even_low, odd_high, odd_low, grad_ref,
):
    ext_ref[...] = jnp.zeros_like(ext_ref)
    for t in range(FR):
        lanes = slice(t * C, (t + 1) * C)
        ext_ref[2 : 2 + R, 3 : 3 + W, lanes] = feat_ref[t]
        for row in range(2):
            above, below = row_halo(row_first_ref, row_second_ref, t, slice(row * W, (row + 1) * W))
            ext_ref[row, 3 : 3 + W, lanes] = above
            ext_ref[R + 2 + row, 3 : 3 + W, lanes] = below
            place = slice(row * COL, row * COL + R + 4)
            left, right = col_halo(col_first_ref, col_second_ref, t, place)
            ext_ref[:, 1 + row, lanes] = left
            ext_ref[:, 3 + W + row, lanes] = right
    for t in range(FR):
        lanes = slice(t * C, (t + 1) * C)
        for row in range(R2 + 2):
            line = cot_ref[t, row] * 0.5
            for target in (2 * row - 1, 2 * row):
                if 0 <= target < R + 2:
                    wide_ref[t, target, pl.ds(0, W2 + 2, stride=2), :] = line
                    wide_ref[t, target, pl.ds(1, W2 + 2, stride=2), :] = line
    rows = R + 4
    for e in range(3):
        shifted = ext_ref[:, e : e + PITCH, :].reshape(rows * PITCH, 2 * C)
        high, low = split(shifted)
        even_high[e] = high
        even_low[e] = low
        odd_high[e] = high[PITCH : PITCH + EXT]
        odd_low[e] = low[PITCH : PITCH + EXT]
    step = EXT // 3
    for part in range(3):
        start = part * step
        total = jnp.zeros((step, 2 * C), f32)
        for row_tap in range(3):
            for e in range(3):
                if row_tap == 1:
                    window = (odd_high[e, start : start + step], odd_low[e, start : start + step])
                else:
                    first = start + row_tap * PITCH
                    window = (even_high[e, first : first + step], even_low[e, first : first + step])
                tap = 3 * row_tap + e
                total = total + product(window, (taps_high[tap], taps_low[tap]), NN)
        sigma = jax.nn.sigmoid(total)
        slope = sigma * (1.0 + total * (1.0 - sigma))
        lines = step // PITCH
        grad_ref[part * lines : (part + 1) * lines] = slope.reshape(lines, PITCH, 2 * C)
    for t in range(FR):
        lanes = slice(t * C, (t + 1) * C)
        grad_ref[:, :, lanes] = grad_ref[:, :, lanes] * wide_ref[t]
    for e in range(3):
        high, low = split(grad_ref[:, 3 - e : 3 - e + W, :])
        grad_high_ref[e] = high
        grad_low_ref[e] = low


def block_terms_kernel(feat_high, feat_low, grad_high_ref, grad_low_ref, keep_ref, send_ref):
    feat = feat_high[...], feat_low[...]
    for row_tap in range(3):
        for e in range(3):
            window = [
                ref[e, 2 - row_tap : 2 - row_tap + R].reshape(R * W, 2 * C)
                for ref in (grad_high_ref, grad_low_ref)
            ]
            store_terms(keep_ref, send_ref, 3 * row_tap + e, tall_product(feat, window, NN), 8)


def feature_adjoint_kernel(grad_high_ref, grad_low_ref, taps_high, taps_low, feat_out):
    total = jnp.zeros((R * W, 2 * C), f32)
    for row_tap in range(3):
        for e in range(3):
            window = [
                ref[e, 2 - row_tap : 2 - row_tap + R].reshape(R * W, 2 * C)
                for ref in (grad_high_ref, grad_low_ref)
            ]
            tap = 3 * row_tap + e
            total = total + tall_product(window, (taps_high[tap], taps_low[tap]), NT)
    for t in range(FR):
        feat_out[t] = total[:, t * C : (t + 1) * C].reshape(R, W, C)


def flow_adjoint_kernel(cot_ref, weight_two_ref, flow_out):
    total = jnp.zeros((R2 * W2, 2 * CF), f32)
    for e in range(3):
        cot = shifted_cot(cot_ref, 2 - e)
        for row_tap in range(3):
            window = [v[2 - row_tap : 2 - row_tap + R2].reshape(R2 * W2, 2 * C) for v in cot]
            total = total + tall_product(window, split(both_frames(weight_two_ref, 3 * row_tap + e)), NT)
    for t in range(FR):
        flow_out[t] = total[:, t * CF : (t + 1) * CF].reshape(R2, W2, CF)


def first_sum_kernel(*refs):
    ones, twos, outs = refs[:4], refs[4:8], refs[8:]
    for slot, out in enumerate(outs):
        for depth, parts in ((slice(0, 8), ones), (slice(8, 24), twos)):
            own, second, first, third = parts
            out[:, :, depth] = (own[0, slot] + second[slot]) + (first[slot] + third[slot])


def second_sum_kernel(own, second, first, third, keep, send):
    keep[...] = (own[0] + second[0]) + (first[0] + third[0])
    send[...] = (own[1] + second[1]) + (first[1] + third[1])


def gather_kernel(own_ref, two_ref, one_ref, three_ref, grad_one_ref, grad_two_ref):
    scale_one = 1.0 / (FR * R * W * 256) ** 0.5
    scale_two = 1.0 / (FR * R2 * W2 * 256) ** 0.5
    for k, ref in enumerate((own_ref, one_ref, two_ref, three_ref)):
        first = 7 * (lax.axis_index("x") ^ k)

        def put(j, ref=ref, first=first):
            grad_one_ref[first + j] = ref[j, :8] * scale_one
            grad_two_ref[first + j] = ref[j, 8:] * scale_two

        for j in range(6):
            put(j)
        pl.when(first < 21)(functools.partial(put, 6))


def params(mebibytes=24):
    return pltpu.CompilerParams(vmem_limit_bytes=mebibytes * 2**20)


def small(kernel, name, out_shape, count, scratch=(), space=VMEM):
    return pl.pallas_call(
        kernel,
        out_shape=out_shape,
        in_specs=[space] * count,
        out_specs=(VMEM,) * len(out_shape),
        scratch_shapes=scratch,
        compiler_params=params(24 if space is VMEM else 64),
        cost_estimate=pl.CostEstimate(flops=10**6, bytes_accessed=10**6, transcendentals=0),
        name=name,
    )


def flow_terms(*args):
    return pl.pallas_call(
        flow_terms_kernel,
        out_shape=(jax.ShapeDtypeStruct((4, 4, 2, 7, 16, C), f32),) * 2
        + (jax.ShapeDtypeStruct((FR, R2 + 2, W2 + 2, C), f32),),
        in_specs=[VMEM] * 7,
        out_specs=(VMEM,) * 3,
        compiler_params=params(),
        cost_estimate=pl.CostEstimate(flops=2 * 10**9, bytes_accessed=5 * 10**6, transcendentals=0),
        name="flow_terms",
    )(*args)


def block_gradient(*args):
    return pl.pallas_call(
        block_kernel,
        out_shape=(jax.ShapeDtypeStruct((3, R + 2, W, 2 * C), bf16),) * 2,
        in_specs=[VMEM] * 8,
        out_specs=(VMEM,) * 2,
        scratch_shapes=[
            pltpu.VMEM((R + 4, PITCH + 8, 2 * C), f32),
            pltpu.VMEM((FR, R + 2, PITCH, C), f32),
            pltpu.VMEM((3, (R + 4) * PITCH, 2 * C), bf16),
            pltpu.VMEM((3, (R + 4) * PITCH, 2 * C), bf16),
            pltpu.VMEM((3, EXT, 2 * C), bf16),
            pltpu.VMEM((3, EXT, 2 * C), bf16),
            pltpu.VMEM((R + 2, PITCH, 2 * C), f32),
        ],
        compiler_params=params(),
        cost_estimate=pl.CostEstimate(flops=5 * 10**9, bytes_accessed=6 * 10**6, transcendentals=200000),
        name="block_gradient",
    )(*args)


def block_terms(*args):
    return pl.pallas_call(
        block_terms_kernel,
        out_shape=(jax.ShapeDtypeStruct((4, 4, 2, 7, 8, C), f32),) * 2,
        in_specs=[VMEM] * 4,
        out_specs=(VMEM,) * 2,
        compiler_params=params(),
        cost_estimate=pl.CostEstimate(flops=10**9, bytes_accessed=10**6, transcendentals=0),
        name="block_terms",
    )(*args)


def adjoint(kernel, name, shape, *args):
    return pl.pallas_call(
        kernel,
        out_shape=jax.ShapeDtypeStruct(shape, f32),
        in_specs=[VMEM] * len(args),
        out_specs=VMEM,
        compiler_params=params(),
        cost_estimate=pl.CostEstimate(flops=2 * 10**9, bytes_accessed=5 * 10**6, transcendentals=0),
        name=name,
    )(*args)


def swaps(mask, count=4):
    return [(i, i ^ mask) for i in range(count)]


def crossed(mask, axes):
    both = []
    for x in range(4):
        for y in range(4):
            for core in range(2):
                x_to, y_to = (x ^ mask, y) if axes[core] == "x" else (x, y ^ mask)
                both.append((8 * x + 2 * y + core, 8 * x_to + 2 * y_to + core))
    return both


def pairs(start, count=16):
    return [p for i in range(start, count - 1, 2) for p in ((i, i + 1), (i + 1, i))]


def spread(parts, axes):
    if axes == "zl":
        return [lax.ppermute(parts[k], "zl", swaps(k)) for k in (3, 2, 1)]
    return [lax.ppermute(parts[k], ("x", "y", "core"), crossed(k, axes)) for k in (2, 1, 3)]


def summed(own, arrived):
    third, second, first = arrived
    return (own + first) + (second + third)


def local(features, weight_one, flow_feats, weight_two, cotangent):
    kernel_one = weight_one.reshape(27, C, C)
    kernel_two = weight_two.reshape(27, CF, C)
    edges = (jax.ShapeDtypeStruct((FR, 2 * W + W2, C), f32),) * 2
    edges = small(
        row_edges_kernel,
        "row_edges",
        edges,
        2,
        [pltpu.VMEM((FR, 2, W, C), f32)] * 2
        + [pltpu.VMEM((FR, 1, W2, C), f32)] * 2
        + [pltpu.SemaphoreType.DMA((4,))],
        HBM,
    )(features, cotangent)
    rows = [lax.ppermute(edges[k], HA, pairs(k)) for k in (1, 0)]
    feats = (jax.ShapeDtypeStruct((2 * C, R * W), bf16),) * 2
    near = (jax.ShapeDtypeStruct((FR, R2, W2, C), f32),)
    *feats, near = small(prepare_features_kernel, "prepare_features", feats + near, 2)(features, cotangent)
    rows, feats, near = lax.optimization_barrier((rows, feats, near))
    shape = (FR, 56, C)
    edges = small(
        col_edges_kernel,
        "col_edges",
        (jax.ShapeDtypeStruct(shape, f32),) * 2,
        4,
        [pltpu.VMEM((2,) + shape, f32)],
    )(features, near, *rows)
    edges, flow_feats = lax.optimization_barrier((edges, flow_feats))
    cols = [lax.ppermute(edges[k], WA, pairs(k)) for k in (1, 0)]
    taps = (jax.ShapeDtypeStruct((9, 2 * C, 2 * C), bf16),) * 2
    flows = (jax.ShapeDtypeStruct((2 * CF, R2 * W2), bf16),) * 2
    prepared = small(prepare_kernel, "prepare", taps + flows, 2)(kernel_one, flow_feats)
    cols, prepared = lax.optimization_barrier((cols, prepared))
    swap = [(0, 1), (1, 0)]
    taps, flows = prepared[:2], prepared[2:]
    keep, send, cot = flow_terms(*flows, near, *rows, *cols)
    terms_two = keep + lax.ppermute(send, "core", swap)
    grad_high, grad_low = block_gradient(features, *rows, *cols, *taps, cot)
    terms_two, grad_high, grad_low = lax.optimization_barrier((terms_two, grad_high, grad_low))
    arrived_two = spread(terms_two, ("y", "x"))
    keep, send = block_terms(*feats, grad_high, grad_low)
    terms_one = keep + lax.ppermute(send, "core", swap)
    arrived_one = spread(terms_one, ("y", "x"))
    terms_one, cot, kernel_two = lax.optimization_barrier((terms_one, cot, kernel_two))
    grad_flow = adjoint(flow_adjoint_kernel, "flow_adjoint", (FR, R2, W2, CF), cot, kernel_two)
    arrived_one, arrived_two, grad_flow = lax.optimization_barrier((arrived_one, arrived_two, grad_flow))
    parts = (jax.ShapeDtypeStruct((2, 7, 24, C), f32),) * 4
    parts = small(first_sum_kernel, "first_sum", parts, 8)(terms_one, *arrived_one, terms_two, *arrived_two)
    chunk = (jax.ShapeDtypeStruct((7, 24, C), f32),) * 2
    keep, send = small(second_sum_kernel, "second_sum", chunk, 4)(parts[0], *spread(parts, ("x", "y")))
    arrived = lax.ppermute(send, ("zl", "zh"), [(i, 7 - i) for i in range(8)])
    keep, grad_high, grad_low = lax.optimization_barrier((keep, grad_high, grad_low))
    grad_features = adjoint(
        feature_adjoint_kernel, "feature_adjoint", (FR, R, W, C), grad_high, grad_low, *taps
    )
    arrived, grad_features = lax.optimization_barrier((arrived, grad_features))
    chunk = keep + arrived
    chunk = summed(chunk, spread([chunk] * 4, "zl"))
    pieces = [chunk] + [lax.ppermute(chunk, "x", swaps(k)) for k in (2, 1, 3)]
    shares = tuple(jax.ShapeDtypeStruct((27, depth, C), f32) for depth in (8, 16))
    grad_one, grad_two = small(gather_kernel, "gather", shares, 4)(*pieces)
    grad_one = grad_one.reshape(3, 3, 3, 8, C)
    grad_two = grad_two.reshape(3, 3, 3, 16, C)
    return (grad_features, grad_one, grad_flow, grad_two)


def solution(mesh):
    fine = Mesh(mesh.devices.reshape(4, 4, 2, 4, 2), ("x", "zl", "zh", "y", "core"))
    grid = P(None, HA, WA, None)
    share = P(None, None, None, WA, None)
    return jax.shard_map(
        local,
        mesh=fine,
        in_specs=(grid, P(), grid, P(), grid),
        out_specs=(grid, share, grid, share),
        check_vma=False,
    )
```

```python
import functools

import jax
import jax.numpy as jnp
from jax import lax
from jax.experimental import pallas as pl
from jax.experimental.pallas import tpu as pltpu
from jax.sharding import Mesh
from jax.sharding import PartitionSpec as P

FR, R, W, C = 2, 16, 32, 128
R2, W2, CF = 8, 16, 256
PITCH = 40
EXT = (R + 2) * PITCH
COL = 20
HA, WA = ("x", "zl"), ("zh", "y", "core")

f32, bf16 = jnp.float32, jnp.bfloat16
VMEM = pl.BlockSpec(memory_space=pltpu.VMEM)
HBM = pl.BlockSpec(memory_space=pltpu.HBM)


def split(values):
    high = values.astype(bf16)
    return high, (values - high.astype(f32)).astype(bf16)


def dot(left, right, dims):
    return lax.dot_general(left, right, (dims, ((), ())), preferred_element_type=f32)


def product(left, right, dims):
    return dot(left[0], right[0], dims) + (dot(left[0], right[1], dims) + dot(left[1], right[0], dims))


def tall_product(left, right, dims):
    rows = left[0].shape[0]
    both = dot(jnp.concatenate(left, axis=0), right[0], dims)
    return both[:rows] + (both[rows:] + dot(left[0], right[1], dims))


NN = ((1,), (0,))
NT = ((1,), (1,))


def both_frames(kernel, tap):
    first = jnp.concatenate([kernel[9 + tap], kernel[tap]], axis=1)
    second = jnp.concatenate([kernel[18 + tap], kernel[9 + tap]], axis=1)
    return jnp.concatenate([first, second], axis=0)


def store_terms(keep_ref, send_ref, tap, value, depth):
    half = value.shape[0] // 2
    taps = (
        (0, value[:half, C:]),
        (1, value[:half, :C] + value[half:, C:]),
        (2, value[half:, :C]),
    )
    core, y, x, zh = [lax.axis_index(a) for a in ("core", "y", "x", "zh")]
    for time_tap, part in taps:
        number = 9 * time_tap + tap
        slot_x = x ^ (number // 7)
        for owner in range(8):
            slot_y = y ^ (owner % 4)
            slot_zh = zh ^ (owner // 4)
            slots = [jnp.where(core == 0, slot_x, slot_y), jnp.where(core == 0, slot_y, slot_x)]
            first = part[2 * owner * depth : (2 * owner + 1) * depth]
            second = part[(2 * owner + 1) * depth : (2 * owner + 2) * depth]
            keep_ref[slots[0], slots[1], slot_zh, number % 7] = jnp.where(core == 0, first, second)
            send_ref[slots[1], slots[0], slot_zh, number % 7] = jnp.where(core == 0, second, first)


def row_edges_kernel(feat_ref, cot_ref, first_ref, second_ref, sems):
    odd = lax.rem(lax.axis_index("zl"), 2)
    copies = []
    for ref, top in ((first_ref, odd), (second_ref, 1 - odd)):
        row, cot_row = (1 - top) * (R - 2), (1 - top) * (R2 - 1)
        pieces = [
            (feat_ref.at[:, row + line // 2, (line % 2) * W2 : (line % 2 + 1) * W2], line) for line in range(4)
        ]
        for source, line in pieces + [(cot_ref.at[:, cot_row], 4)]:
            copies.append(pltpu.make_async_copy(source, ref.at[:, line], sems.at[len(copies)]))
    for copy in copies:
        copy.start()
    for copy in copies:
        copy.wait()


def prepare_features_kernel(feat_ref, cot_ref, feat_high, feat_low, near_cot_ref):
    near_cot_ref[...] = cot_ref[...]
    for t in range(FR):
        lines = slice(t * C, (t + 1) * C)
        feat_high[lines], feat_low[lines] = split(feat_ref[t].reshape(R * W, C).T)


def prepare_kernel(weight_ref, flow_ref, taps_high, taps_low, flow_high, flow_low):
    for tap in range(9):
        taps_high[tap], taps_low[tap] = split(both_frames(weight_ref, tap))
    for t in range(FR):
        lines = slice(t * CF, (t + 1) * CF)
        flow_high[lines], flow_low[lines] = split(flow_ref[t].reshape(R2 * W2, CF).T)


def row_halo(first_ref, second_ref, t, lines):
    odd = lax.rem(lax.axis_index("zl"), 2) == 1
    first, second = first_ref[t, lines], second_ref[t, lines]
    return jnp.where(odd, first, second), jnp.where(odd, second, first)


def col_edges_kernel(feat_ref, cot_ref, row_second_ref, row_first_ref, first_ref, second_ref, edge_ref):
    for t in range(FR):
        halos = [row_halo(row_first_ref, row_second_ref, t, slice(r * W, (r + 1) * W)) for r in range(2)]
        for side, start in ((0, 0), (1, W - 2)):
            for col in range(2):
                at, place = start + col, col * COL
                for row in range(2):
                    edge_ref[side, t, place + row : place + row + 1] = halos[row][0][at : at + 1]
                    low = place + R + 2 + row
                    edge_ref[side, t, low : low + 1] = halos[row][1][at : at + 1]
                edge_ref[side, t, place + 2 : place + 2 + R] = feat_ref[t, :, at, :]
        above, below = row_halo(row_first_ref, row_second_ref, t, slice(2 * W, 2 * W + W2))
        for side, at in ((0, 0), (1, W2 - 1)):
            place = 2 * COL
            edge_ref[side, t, place : place + 1] = above[at : at + 1]
            edge_ref[side, t, place + 1 : place + 1 + R2] = cot_ref[t, :, at, :]
            edge_ref[side, t, place + 1 + R2 : place + 2 + R2] = below[at : at + 1]
    odd = lax.axis_index("core") == 1
    first_ref[...] = jnp.where(odd, edge_ref[0], edge_ref[1])
    second_ref[...] = jnp.where(odd, edge_ref[1], edge_ref[0])


def col_halo(first_ref, second_ref, t, lines):
    odd = lax.axis_index("core") == 1
    first, second = first_ref[t, lines], second_ref[t, lines]
    return jnp.where(odd, first, second), jnp.where(odd, second, first)


def shifted_cot(cot_ref, e):
    both = jnp.concatenate([cot_ref[0, :, e : e + W2, :], cot_ref[1, :, e : e + W2, :]], axis=-1)
    return split(both)


def flow_terms_kernel(
    flow_high, flow_low, local_ref, row_second_ref, row_first_ref, col_second_ref, col_first_ref,
    keep_ref, send_ref, cot_ref,
):
    for t in range(FR):
        above, below = row_halo(row_first_ref, row_second_ref, t, slice(2 * W, 2 * W + W2))
        cot_ref[t, 0, 1 : 1 + W2] = above
        cot_ref[t, 1 : 1 + R2, 1 : 1 + W2] = local_ref[t]
        cot_ref[t, 1 + R2, 1 : 1 + W2] = below
        lines = slice(2 * COL, 2 * COL + R2 + 2)
        left, right = col_halo(col_first_ref, col_second_ref, t, lines)
        cot_ref[t, :, 0] = left
        cot_ref[t, :, 1 + W2] = right
    flow = jnp.concatenate([flow_high[...], flow_high[...], flow_low[...]], axis=1)
    for col_tap in range(3):
        cot = shifted_cot(cot_ref, 2 - col_tap)
        for row_tap in range(3):
            window = [v[2 - row_tap : 2 - row_tap + R2].reshape(R2 * W2, 2 * C) for v in cot]
            window = jnp.concatenate([window[0], window[1], window[0]], axis=0)
            store_terms(keep_ref, send_ref, 3 * row_tap + col_tap, dot(flow, window, NN), 16)


def block_kernel(
    feat_ref, row_second_ref, row_first_ref, col_second_ref, col_first_ref,
    taps_high, taps_low, cot_ref, grad_high_ref, grad_low_ref,
    ext_ref, wide_ref, even_high, even_low, odd_high, odd_low, grad_ref,
):
    ext_ref[...] = jnp.zeros_like(ext_ref)
    for t in range(FR):
        lanes = slice(t * C, (t + 1) * C)
        ext_ref[2 : 2 + R, 3 : 3 + W, lanes] = feat_ref[t]
        for row in range(2):
            above, below = row_halo(row_first_ref, row_second_ref, t, slice(row * W, (row + 1) * W))
            ext_ref[row, 3 : 3 + W, lanes] = above
            ext_ref[R + 2 + row, 3 : 3 + W, lanes] = below
            place = slice(row * COL, row * COL + R + 4)
            left, right = col_halo(col_first_ref, col_second_ref, t, place)
            ext_ref[:, 1 + row, lanes] = left
            ext_ref[:, 3 + W + row, lanes] = right
    for t in range(FR):
        lanes = slice(t * C, (t + 1) * C)
        for row in range(R2 + 2):
            line = cot_ref[t, row] * 0.5
            for target in (2 * row - 1, 2 * row):
                if 0 <= target < R + 2:
                    wide_ref[t, target, pl.ds(0, W2 + 2, stride=2), :] = line
                    wide_ref[t, target, pl.ds(1, W2 + 2, stride=2), :] = line
    rows = R + 4
    for e in range(3):
        shifted = ext_ref[:, e : e + PITCH, :].reshape(rows * PITCH, 2 * C)
        high, low = split(shifted)
        even_high[e] = high
        even_low[e] = low
        odd_high[e] = high[PITCH : PITCH + EXT]
        odd_low[e] = low[PITCH : PITCH + EXT]
    step = EXT // 3
    for part in range(3):
        start = part * step
        total = jnp.zeros((step, 2 * C), f32)
        for row_tap in range(3):
            for e in range(3):
                if row_tap == 1:
                    window = (odd_high[e, start : start + step], odd_low[e, start : start + step])
                else:
                    first = start + row_tap * PITCH
                    window = (even_high[e, first : first + step], even_low[e, first : first + step])
                tap = 3 * row_tap + e
                total = total + product(window, (taps_high[tap], taps_low[tap]), NN)
        sigma = jax.nn.sigmoid(total)
        slope = sigma * (1.0 + total * (1.0 - sigma))
        lines = step // PITCH
        grad_ref[part * lines : (part + 1) * lines] = slope.reshape(lines, PITCH, 2 * C)
    for t in range(FR):
        lanes = slice(t * C, (t + 1) * C)
        grad_ref[:, :, lanes] = grad_ref[:, :, lanes] * wide_ref[t]
    for e in range(3):
        high, low = split(grad_ref[:, 3 - e : 3 - e + W, :])
        grad_high_ref[e] = high
        grad_low_ref[e] = low


def block_terms_kernel(feat_high, feat_low, grad_high_ref, grad_low_ref, keep_ref, send_ref):
    feat = feat_high[...], feat_low[...]
    for row_tap in range(3):
        for e in range(3):
            window = [
                ref[e, 2 - row_tap : 2 - row_tap + R].reshape(R * W, 2 * C)
                for ref in (grad_high_ref, grad_low_ref)
            ]
            store_terms(keep_ref, send_ref, 3 * row_tap + e, tall_product(feat, window, NN), 8)


def feature_adjoint_kernel(grad_high_ref, grad_low_ref, taps_high, taps_low, feat_out):
    total = jnp.zeros((R * W, 2 * C), f32)
    for row_tap in range(3):
        for e in range(3):
            window = [
                ref[e, 2 - row_tap : 2 - row_tap + R].reshape(R * W, 2 * C)
                for ref in (grad_high_ref, grad_low_ref)
            ]
            tap = 3 * row_tap + e
            total = total + tall_product(window, (taps_high[tap], taps_low[tap]), NT)
    for t in range(FR):
        feat_out[t] = total[:, t * C : (t + 1) * C].reshape(R, W, C)


def flow_adjoint_kernel(cot_ref, weight_two_ref, flow_out):
    total = jnp.zeros((R2 * W2, 2 * CF), f32)
    for e in range(3):
        cot = shifted_cot(cot_ref, 2 - e)
        for row_tap in range(3):
            window = [v[2 - row_tap : 2 - row_tap + R2].reshape(R2 * W2, 2 * C) for v in cot]
            total = total + tall_product(window, split(both_frames(weight_two_ref, 3 * row_tap + e)), NT)
    for t in range(FR):
        flow_out[t] = total[:, t * CF : (t + 1) * CF].reshape(R2, W2, CF)


def first_sum_kernel(*refs):
    ones, twos, outs = refs[:4], refs[4:8], refs[8:]
    for slot, out in enumerate(outs):
        for depth, parts in ((slice(0, 8), ones), (slice(8, 24), twos)):
            own, second, first, third = parts
            out[:, :, depth] = (own[0, slot] + second[slot]) + (first[slot] + third[slot])


def second_sum_kernel(own, second, first, third, keep, send):
    keep[...] = (own[0] + second[0]) + (first[0] + third[0])
    send[...] = (own[1] + second[1]) + (first[1] + third[1])


def gather_kernel(own_ref, two_ref, one_ref, three_ref, grad_one_ref, grad_two_ref):
    scale_one = 1.0 / (FR * R * W * 256) ** 0.5
    scale_two = 1.0 / (FR * R2 * W2 * 256) ** 0.5
    for k, ref in enumerate((own_ref, one_ref, two_ref, three_ref)):
        first = 7 * (lax.axis_index("x") ^ k)

        def put(j, ref=ref, first=first):
            grad_one_ref[first + j] = ref[j, :8] * scale_one
            grad_two_ref[first + j] = ref[j, 8:] * scale_two

        for j in range(6):
            put(j)
        pl.when(first < 21)(functools.partial(put, 6))


def params(mebibytes=24):
    return pltpu.CompilerParams(vmem_limit_bytes=mebibytes * 2**20)


def small(kernel, name, out_shape, count, scratch=(), space=VMEM):
    return pl.pallas_call(
        kernel,
        out_shape=out_shape,
        in_specs=[space] * count,
        out_specs=(VMEM,) * len(out_shape),
        scratch_shapes=scratch,
        compiler_params=params(24 if space is VMEM else 64),
        cost_estimate=pl.CostEstimate(flops=10**6, bytes_accessed=10**6, transcendentals=0),
        name=name,
    )


def flow_terms(*args):
    return pl.pallas_call(
        flow_terms_kernel,
        out_shape=(jax.ShapeDtypeStruct((4, 4, 2, 7, 16, C), f32),) * 2
        + (jax.ShapeDtypeStruct((FR, R2 + 2, W2 + 2, C), f32),),
        in_specs=[VMEM] * 7,
        out_specs=(VMEM,) * 3,
        compiler_params=params(),
        cost_estimate=pl.CostEstimate(flops=2 * 10**9, bytes_accessed=5 * 10**6, transcendentals=0),
        name="flow_terms",
    )(*args)


def block_gradient(*args):
    return pl.pallas_call(
        block_kernel,
        out_shape=(jax.ShapeDtypeStruct((3, R + 2, W, 2 * C), bf16),) * 2,
        in_specs=[VMEM] * 8,
        out_specs=(VMEM,) * 2,
        scratch_shapes=[
            pltpu.VMEM((R + 4, PITCH + 8, 2 * C), f32),
            pltpu.VMEM((FR, R + 2, PITCH, C), f32),
            pltpu.VMEM((3, (R + 4) * PITCH, 2 * C), bf16),
            pltpu.VMEM((3, (R + 4) * PITCH, 2 * C), bf16),
            pltpu.VMEM((3, EXT, 2 * C), bf16),
            pltpu.VMEM((3, EXT, 2 * C), bf16),
            pltpu.VMEM((R + 2, PITCH, 2 * C), f32),
        ],
        compiler_params=params(),
        cost_estimate=pl.CostEstimate(flops=5 * 10**9, bytes_accessed=6 * 10**6, transcendentals=200000),
        name="block_gradient",
    )(*args)


def block_terms(*args):
    return pl.pallas_call(
        block_terms_kernel,
        out_shape=(jax.ShapeDtypeStruct((4, 4, 2, 7, 8, C), f32),) * 2,
        in_specs=[VMEM] * 4,
        out_specs=(VMEM,) * 2,
        compiler_params=params(),
        cost_estimate=pl.CostEstimate(flops=10**9, bytes_accessed=10**6, transcendentals=0),
        name="block_terms",
    )(*args)


def adjoint(kernel, name, shape, *args):
    return pl.pallas_call(
        kernel,
        out_shape=jax.ShapeDtypeStruct(shape, f32),
        in_specs=[VMEM] * len(args),
        out_specs=VMEM,
        compiler_params=params(),
        cost_estimate=pl.CostEstimate(flops=2 * 10**9, bytes_accessed=5 * 10**6, transcendentals=0),
        name=name,
    )(*args)


def swaps(mask, count=4):
    return [(i, i ^ mask) for i in range(count)]


def crossed(mask, axes):
    both = []
    for x in range(4):
        for y in range(4):
            for core in range(2):
                x_to, y_to = (x ^ mask, y) if axes[core] == "x" else (x, y ^ mask)
                both.append((8 * x + 2 * y + core, 8 * x_to + 2 * y_to + core))
    return both


def pairs(start, count=16):
    return [p for i in range(start, count - 1, 2) for p in ((i, i + 1), (i + 1, i))]


def spread(parts, axes):
    if axes == "zl":
        return [lax.ppermute(parts[k], "zl", swaps(k)) for k in (3, 2, 1)]
    return [lax.ppermute(parts[k], ("x", "y", "core"), crossed(k, axes)) for k in (2, 1, 3)]


def summed(own, arrived):
    third, second, first = arrived
    return (own + first) + (second + third)


def local(features, weight_one, flow_feats, weight_two, cotangent):
    kernel_one = weight_one.reshape(27, C, C)
    kernel_two = weight_two.reshape(27, CF, C)
    edges = pl.pallas_call(
        row_edges_kernel,
        out_shape=(jax.ShapeDtypeStruct((FR, 5, W2, C), f32),) * 2,
        in_specs=[HBM] * 2,
        out_specs=(HBM,) * 2,
        scratch_shapes=[pltpu.SemaphoreType.DMA((10,))],
        compiler_params=params(64),
        cost_estimate=pl.CostEstimate(flops=10**6, bytes_accessed=10**6, transcendentals=0),
        name="row_edges",
    )(features, cotangent)
    edges = [edge.reshape(FR, 2 * W + W2, C) for edge in edges]
    rows = [lax.ppermute(edges[k], HA, pairs(k)) for k in (1, 0)]
    feats = (jax.ShapeDtypeStruct((2 * C, R * W), bf16),) * 2
    near = (jax.ShapeDtypeStruct((FR, R2, W2, C), f32),)
    *feats, near = small(prepare_features_kernel, "prepare_features", feats + near, 2)(features, cotangent)
    rows, feats, near = lax.optimization_barrier((rows, feats, near))
    shape = (FR, 56, C)
    edges = small(
        col_edges_kernel,
        "col_edges",
        (jax.ShapeDtypeStruct(shape, f32),) * 2,
        4,
        [pltpu.VMEM((2,) + shape, f32)],
    )(features, near, *rows)
    edges, flow_feats = lax.optimization_barrier((edges, flow_feats))
    cols = [lax.ppermute(edges[k], WA, pairs(k)) for k in (1, 0)]
    taps = (jax.ShapeDtypeStruct((9, 2 * C, 2 * C), bf16),) * 2
    flows = (jax.ShapeDtypeStruct((2 * CF, R2 * W2), bf16),) * 2
    prepared = small(prepare_kernel, "prepare", taps + flows, 2)(kernel_one, flow_feats)
    cols, prepared = lax.optimization_barrier((cols, prepared))
    swap = [(0, 1), (1, 0)]
    taps, flows = prepared[:2], prepared[2:]
    keep, send, cot = flow_terms(*flows, near, *rows, *cols)
    terms_two = keep + lax.ppermute(send, "core", swap)
    grad_high, grad_low = block_gradient(features, *rows, *cols, *taps, cot)
    terms_two, grad_high, grad_low = lax.optimization_barrier((terms_two, grad_high, grad_low))
    arrived_two = spread(terms_two, ("x", "y"))
    keep, send = block_terms(*feats, grad_high, grad_low)
    terms_one = keep + lax.ppermute(send, "core", swap)
    arrived_one = spread(terms_one, ("x", "y"))
    terms_one, cot, kernel_two = lax.optimization_barrier((terms_one, cot, kernel_two))
    grad_flow = adjoint(flow_adjoint_kernel, "flow_adjoint", (FR, R2, W2, CF), cot, kernel_two)
    arrived_one, arrived_two, grad_flow = lax.optimization_barrier((arrived_one, arrived_two, grad_flow))
    parts = (jax.ShapeDtypeStruct((2, 7, 24, C), f32),) * 4
    parts = small(first_sum_kernel, "first_sum", parts, 8)(terms_one, *arrived_one, terms_two, *arrived_two)
    chunk = (jax.ShapeDtypeStruct((7, 24, C), f32),) * 2
    keep, send = small(second_sum_kernel, "second_sum", chunk, 4)(parts[0], *spread(parts, ("y", "x")))
    arrived = lax.ppermute(send, ("zl", "zh"), [(i, 7 - i) for i in range(8)])
    keep, grad_high, grad_low = lax.optimization_barrier((keep, grad_high, grad_low))
    grad_features = adjoint(
        feature_adjoint_kernel, "feature_adjoint", (FR, R, W, C), grad_high, grad_low, *taps
    )
    arrived, grad_features = lax.optimization_barrier((arrived, grad_features))
    chunk = keep + arrived
    chunk = summed(chunk, spread([chunk] * 4, "zl"))
    pieces = [chunk] + [lax.ppermute(chunk, "x", swaps(k)) for k in (2, 1, 3)]
    shares = tuple(jax.ShapeDtypeStruct((27, depth, C), f32) for depth in (8, 16))
    grad_one, grad_two = small(gather_kernel, "gather", shares, 4)(*pieces)
    grad_one = grad_one.reshape(3, 3, 3, 8, C)
    grad_two = grad_two.reshape(3, 3, 3, 16, C)
    return (grad_features, grad_one, grad_flow, grad_two)


def solution(mesh):
    fine = Mesh(mesh.devices.reshape(4, 4, 2, 4, 2), ("x", "zl", "zh", "y", "core"))
    grid = P(None, HA, WA, None)
    share = P(None, None, None, WA, None)
    return jax.shard_map(
        local,
        mesh=fine,
        in_specs=(grid, P(), grid, P(), grid),
        out_specs=(grid, share, grid, share),
        check_vma=False,
    )
```
